512 devices in a mesh: gx: 64 (over y, z), gy: 4 (over x), ga: 2 (over core).
Axes of the slice: x: 4, y: 4, z: 16, core: 2. Of those that a mesh axis runs over, the one named last changes fastest.
Arguments:
- right_side: float32 [3, 512, 32, 256], P(None, 'gx', 'gy', 'ga'), may hold values from -24 to 24
- fine_stiff: float32 [3, 512, 32, 256], P(None, 'gx', 'gy', 'ga'), may hold values from 4 to 16
- fine_couple: bfloat16 [7, 3, 3, 512, 32, 256], P(None, None, None, 'gx', 'gy', 'ga'), may hold values from -1 to 1
- fine_prolong: float32 [3, 3, 512, 32, 256], P(None, None, 'gx', 'gy', 'ga'), may hold values from -3.5 to 3.5
- middle_stiff: float32 [3, 256, 16, 128], P(None, 'gx', 'gy', 'ga'), may hold values from 12 to 48
- middle_couple: bfloat16 [7, 3, 3, 256, 16, 128], P(None, None, None, 'gx', 'gy', 'ga'), may hold values from -3 to 3
- middle_prolong: float32 [3, 3, 256, 16, 128], P(None, None, 'gx', 'gy', 'ga'), may hold values from -3.5 to 3.5
- coarse_stiff: float32 [3, 128, 16, 64], P(None, 'gx', 'gy', 'ga'), may hold values from 36 to 144
- coarse_couple: bfloat16 [7, 3, 3, 128, 16, 64], P(None, None, None, 'gx', 'gy', 'ga'), may hold values from -9 to 9
- coarse_prolong: float32 [3, 3, 128, 16, 64], P(None, None, 'gx', 'gy', 'ga'), may hold values from -3.5 to 3.5
- bottom_stiff: float32 [3, 16384], replicated, may hold values from 48 to 192
- bottom_couple: bfloat16 [7, 3, 3, 16384], replicated, may hold values from -27 to 27
Outputs:
- solution: float32 [3, 512, 32, 256], P(None, 'gx', 'gy', 'ga')
- residual: float32 [3, 512, 32, 256], P(None, 'gx', 'gy', 'ga')
The draws below stay inside these ranges and needn't reach their ends.
All inputs are finite; a program needn't handle non-finite values.
Results may differ from the reference program's by a relative error of at most 0.0003.
Values sent between devices are 32-bit elements; how exact they have to be, the bound alone decides.
No kernel may reach another device: no remote copies, remote signals or barrier semaphores. Data moves between devices by JAX's collectives and lax.ppermute only.
A program may use at most 128 MiB of HBM per device.

```python
import math
import jax
import jax.numpy as jnp

SWEEPS = 8
NX0 = 512
NY0 = 32
NZ0 = 256
NX1 = 256
NY1 = 16
NZ1 = 128
NX2 = 128
NY2 = 16
NZ2 = 64
NB3 = 16384


def steps_of(stream_key, extent, cuts, least, top_value):
    gain = 1.0
    for axis_at, blocks in cuts:
        heights = jax.random.uniform(jax.random.fold_in(jax.random.fold_in(stream_key, 6), axis_at), (blocks,), jnp.float32, least / len(cuts), top_value / len(cuts))
        gain = gain * jnp.repeat(jnp.exp(heights), extent[axis_at] // blocks).reshape((-1,) + (1,) * (len(extent) - 1 - axis_at))
    return gain


def noise(own_key, extent, scale, bound, split=(), kind=jnp.bfloat16):
    result = jax.random.normal(own_key, extent, jnp.float32) * scale
    if len(split) > 0:
        result = steps_of(own_key, extent, split, -0.22, 0.18) * result
    return jnp.clip(result, min=-bound, max=bound).astype(kind)


def setup_inputs(seed: int = 0) -> dict:
    keys = jax.random.split(jax.random.key(seed), 13)
    right_side = noise(keys[0], (3, NX0, NY0, NZ0), 4.0, 24.0, ((1, 64), (2, 4), (3, 2)), jnp.float32)
    fine_stiff = jnp.clip(jnp.exp(math.log(16.0) - 1.3862944 * jax.random.uniform(keys[1], (3, NX0, NY0, NZ0), jnp.float32) ** steps_of(keys[1], (3, NX0, NY0, NZ0), ((1, 64), (2, 4), (3, 2)), -0.2, 0.2)), 4.0, 16.0)
    fine_couple = noise(keys[2], (7, 3, 3, NX0, NY0, NZ0), 0.25, 1.0, ((3, 64), (4, 4), (5, 2)))
    fine_prolong = noise(keys[3], (3, 3, NX0, NY0, NZ0), 3 ** -0.5, 3.5, ((2, 64), (3, 4), (4, 2)), jnp.float32)
    middle_stiff = jnp.clip(jnp.exp(math.log(48.0) - 1.3862944 * jax.random.uniform(keys[4], (3, NX1, NY1, NZ1), jnp.float32) ** steps_of(keys[4], (3, NX1, NY1, NZ1), ((1, 64), (2, 4), (3, 2)), -0.2, 0.2)), 12.0, 48.0)
    middle_couple = noise(keys[5], (7, 3, 3, NX1, NY1, NZ1), 0.75, 3.0, ((3, 64), (4, 4), (5, 2)))
    middle_prolong = noise(keys[6], (3, 3, NX1, NY1, NZ1), 3 ** -0.5, 3.5, ((2, 64), (3, 4), (4, 2)), jnp.float32)
    coarse_stiff = jnp.clip(jnp.exp(math.log(144.0) - 1.3862944 * jax.random.uniform(keys[7], (3, NX2, NY2, NZ2), jnp.float32) ** steps_of(keys[7], (3, NX2, NY2, NZ2), ((1, 64), (2, 4), (3, 2)), -0.2, 0.2)), 36.0, 144.0)
    coarse_couple = noise(keys[8], (7, 3, 3, NX2, NY2, NZ2), 2.25, 9.0, ((3, 64), (4, 4), (5, 2)))
    coarse_prolong = noise(keys[9], (3, 3, NX2, NY2, NZ2), 3 ** -0.5, 3.5, ((2, 64), (3, 4), (4, 2)), jnp.float32)
    bottom_stiff = jnp.clip(jnp.exp(jax.random.uniform(keys[10], (3, NB3), jnp.float32, math.log(48.0), math.log(192.0))), 48.0, 192.0)
    bottom_couple = noise(keys[11], (7, 3, 3, NB3), 6.75, 27.0)
    return {"right_side": right_side, "fine_stiff": fine_stiff, "fine_couple": fine_couple, "fine_prolong": fine_prolong, "middle_stiff": middle_stiff, "middle_couple": middle_couple, "middle_prolong": middle_prolong, "coarse_stiff": coarse_stiff, "coarse_couple": coarse_couple, "coarse_prolong": coarse_prolong, "bottom_stiff": bottom_stiff, "bottom_couple": bottom_couple}


center_value = 1.0
half_width = 0.7
damping = 0.7
ratio_first = half_width / center_value
ratio_second = 1.0 / (2.0 * center_value / half_width - ratio_first)
carry_coef = ratio_second * ratio_first
fresh_coef = 2.0 * ratio_second / half_width
inverse_center = 1.0 / center_value
level_factors = ((2, 2, 2), (2, 1, 2), (2, 1, 4))


def pad_field(field):
    return jnp.pad(field, ((0, 0), (1, 1), (1, 1), (1, 1)))


def apply_operator(padded, stiff, couple):
    inner = padded[:, 1:-1, 1:-1, 1:-1]
    views = (inner, padded[:, :-2, 1:-1, 1:-1], padded[:, 2:, 1:-1, 1:-1],
             padded[:, 1:-1, :-2, 1:-1], padded[:, 1:-1, 2:, 1:-1],
             padded[:, 1:-1, 1:-1, :-2], padded[:, 1:-1, 1:-1, 2:])
    rows_out = []
    for comp in range(3):
        total = stiff[comp] * inner[comp]
        for direction in range(7):
            for source in range(3):
                total = total + couple[direction, comp, source].astype(jnp.float32) * views[direction][source]
        rows_out.append(total)
    return jnp.stack(rows_out)


def smooth(solution, residual, stiff, couple, spread):
    first = residual / stiff * inverse_center
    solution = solution + first
    residual = residual - apply_operator(spread(first), stiff, couple)
    second = carry_coef * first + fresh_coef * (residual / stiff)
    solution = solution + second
    residual = residual - apply_operator(spread(second), stiff, couple)
    return solution, residual


def restrict(prolong, residual, factors):
    term = jnp.sum(prolong * residual[:, None], axis=0)
    shape = term.shape
    term = term.reshape(3, shape[1] // factors[0], factors[0], shape[2] // factors[1], factors[1], shape[3] // factors[2], factors[2])
    return jnp.sum(term, axis=(2, 4, 6))


def prolongate(prolong, coarse, factors):
    shape = coarse.shape
    upward = jnp.broadcast_to(coarse[:, :, None, :, None, :, None], (3, shape[1], factors[0], shape[2], factors[1], shape[3], factors[2]))
    upward = upward.reshape(3, shape[1] * factors[0], shape[2] * factors[1], shape[3] * factors[2])
    return jnp.sum(prolong * upward[None], axis=1)


def jacobi(load, stiff, couple, spread):
    solution = damping * load / stiff
    for sweep in range(SWEEPS - 1):
        solution = solution + damping * (load - apply_operator(spread(solution), stiff, couple)) / stiff
    return solution


def reference(right_side, fine_stiff, fine_couple, fine_prolong, middle_stiff, middle_couple, middle_prolong,
              coarse_stiff, coarse_couple, coarse_prolong, bottom_stiff, bottom_couple):
    levels = ((fine_stiff, fine_couple, fine_prolong), (middle_stiff, middle_couple, middle_prolong),
              (coarse_stiff, coarse_couple, coarse_prolong))
    loads = [right_side]
    before = []
    for level in range(3):
        stiff, couple, prolong = levels[level]
        load = loads[level]
        smoothed, remain = smooth(jnp.zeros_like(load), load, stiff, couple, pad_field)
        before.append(smoothed)
        loads.append(restrict(prolong, remain, level_factors[level]))
    grid_shape = loads[3].shape[1:]
    grid_stiff = bottom_stiff.reshape((3,) + grid_shape)
    grid_couple = bottom_couple.reshape((7, 3, 3) + grid_shape)
    correction = jacobi(loads[3], grid_stiff, grid_couple, pad_field)
    remain = loads[0]
    for level in (2, 1, 0):
        stiff, couple, prolong = levels[level]
        guess = before[level] + prolongate(prolong, correction, level_factors[level])
        remain = loads[level] - apply_operator(pad_field(guess), stiff, couple)
        correction, remain = smooth(guess, remain, stiff, couple, pad_field)
    return correction, remain
```

```python
import jax
import jax.numpy as jnp
from jax import lax
from jax.experimental import pallas as pl
from jax.experimental.pallas import tpu as pltpu
from jax.sharding import PartitionSpec as P

SWEEPS = 8
center_value = 1.0
half_width = 0.7
damping = 0.7
ratio_first = half_width / center_value
ratio_second = 1.0 / (2.0 * center_value / half_width - ratio_first)
carry_coef = ratio_second * ratio_first
fresh_coef = 2.0 * ratio_second / half_width

F32 = jnp.float32
REACH = 8
WINDOW = 2 * REACH + 1
ROWS = 40


def iota(shape, dim):
    return lax.broadcasted_iota(jnp.int32, shape, dim)


def dot(a, b):
    return jnp.dot(a, b, precision=lax.Precision.HIGHEST, preferred_element_type=F32)


def combine(stiff, coef, views):
    outs = []
    for a in range(3):
        total = stiff[a] * views[0][a]
        for k in range(7):
            for b in range(3):
                total = total + coef(k * 9 + a * 3 + b) * views[k][b]
        outs.append(total)
    return outs


class Fine:
    def __init__(self, ids):
        self.core = ids[0]
        self.spot = (ids[0], 1 - ids[0])
        right = ids[0].astype(F32)
        self.right = (right, 1.0 - right)
        self.row = iota((8, 128), 0)
        self.lane = iota((8, 128), 1)

    def apply(self, get, halo, stiff, coefs, use, halves=(0, 1)):
        for x in range(8):
            mids = [[get(h, b, x) for b in range(3)] for h in range(2)]
            for h in halves:
                views = [mids[h]]
                spot = self.spot[h]
                lows, highs = [], []
                for b in range(3):
                    lows.append(halo[0, 0, spot, 8 * b : 8 * b + 8, :] if x == 0 else get(h, b, x - 1))
                    highs.append(halo[1, 0, spot, 8 * b : 8 * b + 8, :] if x == 7 else get(h, b, x + 1))
                views += [lows, highs]
                lows, highs = [], []
                for b in range(3):
                    at = 8 * b + x
                    v = mids[h][b]
                    edge = jnp.broadcast_to(halo[0, 1, spot, at : at + 1, :], (8, 128))
                    lows.append(jnp.where(self.row == 0, edge, pltpu.roll(v, 1, 0)))
                    edge = jnp.broadcast_to(halo[1, 1, spot, at : at + 1, :], (8, 128))
                    highs.append(jnp.where(self.row == 7, edge, pltpu.roll(v, 7, 0)))
                views += [lows, highs]
                lows, highs = [], []
                for b in range(3):
                    v, o = mids[h][b], mids[1 - h][b]
                    lows.append(
                        jnp.where(self.lane == 0, pltpu.roll(o, 1, 1) * self.right[h], pltpu.roll(v, 1, 1))
                    )
                    highs.append(
                        jnp.where(
                            self.lane == 127,
                            pltpu.roll(o, 127, 1) * self.right[1 - h],
                            pltpu.roll(v, 127, 1),
                        )
                    )
                views += [lows, highs]
                coef = coefs[h]
                out = combine([stiff(h, a, x) for a in range(3)], lambda i: coef[i * 8 + x], views)
                use(h, x, out)

    def send(self, get, xs, ys):
        up = self.core == 0
        for h in range(2):
            spot = self.spot[h]
            for b in range(3):
                xs[spot, 8 * b : 8 * b + 8, :] = jnp.where(up, get(h, b, 7), get(h, b, 0))
                for x in range(8):
                    v = get(h, b, x)
                    ys[spot, 8 * b + x : 8 * b + x + 1, :] = jnp.where(up, v[7:8], v[0:1])


def at(ref):
    return lambda h, b, x: ref[h, 8 * b + x]


def given(fine, ref, which):
    return lambda h, b, x: ref[fine.spot[h], which, 8 * b + x]


def fine_first(ids, ls, first, xs, ys):
    fine = Fine(ids)
    load, stiff = given(fine, ls, 0), given(fine, ls, 1)
    for h in range(2):
        for i in range(24):
            first[h, i] = load(h, i // 8, i % 8) / stiff(h, i // 8, i % 8)
    fine.send(at(first), xs, ys)


def fine_second(ids, ls, first, halo, own, other, rest, second, xs, ys):
    fine = Fine(ids)
    load, stiff = given(fine, ls, 0), given(fine, ls, 1)

    def use(h, x, out):
        for a in range(3):
            r = load(h, a, x) - out[a]
            rest[h, 8 * a + x] = r
            second[h, 8 * a + x] = carry_coef * first[h, 8 * a + x] + fresh_coef * (r / stiff(h, a, x))

    fine.apply(at(first), halo, stiff, (own, other), use)
    fine.send(at(second), xs, ys)


def fine_down(ids, ls, first, second, rest, halo, own, other, pre, keep, send):
    fine = Fine(ids)
    stiff = given(fine, ls, 1)
    terms = [[[[] for _ in range(4)] for _ in range(3)] for _ in range(2)]
    coefs = (own, other)

    def use(h, x, out):
        r = [rest[h, 8 * a + x] - out[a] for a in range(3)]
        for b in range(3):
            t = sum(coefs[h][(63 + 3 * a + b) * 8 + x] * r[a] for a in range(3))
            terms[h][b][x // 2].append(t)
            pre[h, 8 * b + x] = first[h, 8 * b + x] + second[h, 8 * b + x]

    fine.apply(at(second), halo, stiff, coefs, use)
    pairs = (iota((24, 48), 1) // 2 == iota((24, 48), 0)).astype(F32)
    source, to = iota((128, 128), 0), iota((128, 128), 1)
    tiles = []
    for h in range(2):
        total = None
        for p in range(2):
            stacked = jnp.concatenate([sum(terms[h][b][2 * i + p]) for b in range(3) for i in range(2)], axis=0)
            part = dot(stacked, (to == 64 * p + source // 2).astype(F32))
            total = part if total is None else total + part
        tiles.append(dot(pairs, total))
    keep[...] = tiles[0]
    up = fine.core == 0
    for b in range(3):
        mine = pltpu.roll(tiles[0][8 * b : 8 * b + 8], 4, 0)
        its = tiles[1][8 * b : 8 * b + 8]
        first_rows = fine.row < 4
        send[8 * b : 8 * b + 8, :] = jnp.where(
            up, jnp.where(first_rows, mine, its), jnp.where(first_rows, its, mine)
        )


def fine_up_first(ids, ls, guess, halo, own, other, rest, first, xs, ys):
    fine = Fine(ids)
    load, stiff = given(fine, ls, 0), given(fine, ls, 1)

    def use(h, x, out):
        for a in range(3):
            r = load(h, a, x) - out[a]
            rest[h, 8 * a + x] = r
            first[h, 8 * a + x] = r / stiff(h, a, x)

    fine.apply(at(guess), halo, stiff, (own, other), use)
    fine.send(at(first), xs, ys)


def fine_up_second(ids, ls, guess, first, rest, halo, own, other, result, remain, second, xs, ys):
    fine = Fine(ids)
    stiff = given(fine, ls, 1)

    def use(h, x, out):
        for a in range(3):
            r = rest[h, 8 * a + x] - out[a]
            f = first[h, 8 * a + x]
            s = carry_coef * f + fresh_coef * (r / stiff(h, a, x))
            second[h, 8 * a + x] = s
            if h == 0:
                remain[8 * a + x] = r
                result[8 * a + x] = guess[h, 8 * a + x] + f + s

    fine.apply(at(first), halo, stiff, (own, other), use)
    fine.send(at(second), xs, ys)


def fine_last(ids, ls, second, remain, halo, own, residual):
    fine = Fine(ids)
    stiff = given(fine, ls, 1)

    def use(h, x, out):
        for a in range(3):
            residual[8 * a + x] = remain[8 * a + x] - out[a]

    fine.apply(at(second), halo, stiff, (own, None), use, halves=(0,))


def rows8():
    return iota((8, 128), 0)


def lanes8():
    return iota((8, 128), 1)


def side_views(tiles, g, width):
    row, lane = rows8(), lanes8()
    y, z = g // 2, g % 2
    views = [[], [], [], []]
    for b in range(3):
        v = tiles[g][b]
        edge = pltpu.roll(tiles[g - 2][b], 5, 0) if y > 0 else jnp.zeros_like(v)
        views[0].append(jnp.where(row % 4 == 0, edge, pltpu.roll(v, 1, 0)))
        edge = pltpu.roll(tiles[g + 2][b], 3, 0) if y < 3 else jnp.zeros_like(v)
        views[1].append(jnp.where(row % 4 == 3, edge, pltpu.roll(v, 7, 0)))
        edge = pltpu.roll(tiles[g - 1][b], 129 - width, 1) if z == 1 else jnp.zeros_like(v)
        views[2].append(jnp.where(lane % width == 0, edge, pltpu.roll(v, 1, 1)))
        edge = pltpu.roll(tiles[g + 1][b], width - 1, 1) if z == 0 else jnp.zeros_like(v)
        views[3].append(jnp.where(lane % width == width - 1, edge, pltpu.roll(v, 127, 1)))
    return views


def loaded(ref):
    return [[ref[3 * g + b] for b in range(3)] for g in range(8)]


def filled(stiff):
    return jnp.where(stiff == 0.0, 1.0, stiff)


class Middle:
    def __init__(self, packed):
        self.packed = packed

    def stiff(self, g, a):
        return self.packed[g, 63 + a]

    def stiff_edge(self, g, a):
        return filled(self.packed[g, 107 + a])

    def prolong(self, g, i):
        return self.packed[g, 66 + i]

    def coef(self, g):
        return lambda i: self.packed[g, i]

    def coef_edge(self, g):
        def get(i):
            tile = self.packed[g, 75 + i // 2]
            return pltpu.roll(tile, 64, 1) if i % 2 else tile

        return get

    def apply(self, own_ref, edge_ref, use, use_edge=None):
        row, lane = rows8(), lanes8()
        own, edge = loaded(own_ref), loaded(edge_ref)
        for g in range(8):
            swap = [pltpu.roll(v, 64, 1) for v in own[g]]
            swap_edge = [pltpu.roll(v, 64, 1) for v in edge[g]]
            turned = [pltpu.roll(v, 4, 0) for v in swap]
            low, high, low_edge, high_edge = [], [], [], []
            for b in range(3):
                low.append(jnp.where(lane >= 64, swap[b], jnp.where(row < 4, swap_edge[b], turned[b])))
                high.append(jnp.where(lane < 64, swap[b], jnp.where(row < 4, turned[b], swap_edge[b])))
                low_edge.append(jnp.where(lane >= 64, swap_edge[b], swap[b]))
                high_edge.append(jnp.where(lane >= 64, swap[b], swap_edge[b]))
            views = [own[g], low, high] + side_views(own, g, 64)
            use(g, combine([self.stiff(g, a) for a in range(3)], self.coef(g), views))
            if use_edge is not None:
                views = [edge[g], low_edge, high_edge] + side_views(edge, g, 64)
                use_edge(g, combine([self.stiff_edge(g, a) for a in range(3)], self.coef_edge(g), views))


class Coarse:
    def __init__(self, packed):
        self.packed = packed

    def stiff(self, g, a):
        return filled(self.packed[g, 63 + a])

    def prolong(self, g, i):
        return self.packed[g, 66 + i]

    def apply(self, ref, use):
        lane = lanes8()
        tiles = loaded(ref)
        for g in range(8):
            low, high = [], []
            for v in tiles[g]:
                t = pltpu.roll(v, 32, 1)
                low.append(jnp.where(lane < 32, pltpu.roll(t, 4, 0), t))
                t = pltpu.roll(v, 96, 1)
                high.append(jnp.where(lane >= 96, pltpu.roll(t, 4, 0), t))
            views = [tiles[g], low, high] + side_views(tiles, g, 32)
            use(g, combine([self.stiff(g, a) for a in range(3)], lambda i: self.packed[g, i], views))


def middle_down(ids, got, packed, load, load_edge, pre, down, first, first_edge, rest, second, second_edge):
    level = Middle(packed)
    row, lane = rows8(), lanes8()
    for g in range(8):
        y, z = g // 2, g % 2
        for b in range(3):
            n = 3 * g + b
            load[n] = got[g, 8 * b : 8 * b + 8, :]
            low = got[2 * y, 24 + 8 * b : 32 + 8 * b, :]
            high = got[2 * y + 1, 24 + 8 * b : 32 + 8 * b, :]
            if z == 0:
                high = pltpu.roll(high, 4, 0)
            else:
                low = pltpu.roll(low, 4, 0)
            load_edge[n] = jnp.where(row < 4, low, high)
            first[n] = load[n] / level.stiff(g, b)
            first_edge[n] = load_edge[n] / level.stiff_edge(g, b)

    def use(g, out):
        for a in range(3):
            n = 3 * g + a
            r = load[n] - out[a]
            rest[n] = r
            second[n] = carry_coef * first[n] + fresh_coef * (r / level.stiff(g, a))

    def use_edge(g, out):
        for a in range(3):
            n = 3 * g + a
            r = load_edge[n] - out[a]
            second_edge[n] = carry_coef * first_edge[n] + fresh_coef * (r / level.stiff_edge(g, a))

    level.apply(first, first_edge, use, use_edge)
    terms = [[], [], []]

    def use_last(g, out):
        r = [rest[3 * g + a] - out[a] for a in range(3)]
        for b in range(3):
            n = 3 * g + b
            pre[n] = first[n] + second[n]
            terms[b].append(sum(level.prolong(g, 3 * a + b) * r[a] for a in range(3)))

    level.apply(second, second_edge, use_last)
    source, to = iota((128, 128), 0), iota((128, 128), 1)
    total = None
    for b in range(3):
        pick = to == 32 * b + (source % 64) // 2
        part = dot(jnp.concatenate(terms[b], axis=0), pick.astype(F32))
        total = part if total is None else total + part
    for g in range(8):
        down[g] = total[8 * g : 8 * g + 8]


def own_lanes(y, z):
    return lanes8() // 8 == (4 * (y % 2) + rows8() % 4) * 2 + z


def coarse_down(ids, low, mid, high, packed, load, pre, send, down, first, rest, second):
    level = Coarse(packed)
    row, lane = rows8(), lanes8()
    place = lane // 32
    for g in range(8):
        under, here, over = low[g], mid[g], high[g]
        turned = [pltpu.roll(v, 4, 0) for v in (under, here, over)]

        def moved(v, b, to):
            shift = (32 * (to - b)) % 128
            return pltpu.roll(v, shift, 1) if shift else v

        for b in range(3):
            n = 3 * g + b
            top = jnp.where(place == 0, moved(under, b, 0), moved(turned[0], b, 1))
            own = jnp.where(place == 2, moved(here, b, 2), moved(turned[1], b, 3))
            bottom = jnp.where(place == 0, moved(turned[2], b, 0), moved(over, b, 1))
            tile = jnp.where(row < 4, jnp.where(place < 2, top, own), jnp.where(place < 2, bottom, 0.0))
            load[n] = tile
            first[n] = tile / level.stiff(g, b)

    def use(g, out):
        for a in range(3):
            n = 3 * g + a
            r = load[n] - out[a]
            rest[n] = r
            second[n] = carry_coef * first[n] + fresh_coef * (r / level.stiff(g, a))

    level.apply(first, use)
    terms = []

    def use_last(g, out):
        r = [rest[3 * g + a] - out[a] for a in range(3)]
        for b in range(3):
            n = 3 * g + b
            pre[n] = first[n] + second[n]
            terms.append(sum(level.prolong(g, 3 * a + b) * r[a] for a in range(3)))

    level.apply(second, use_last)
    for m in range(6):
        t = [pre[4 * m + i] for i in range(4)]
        right = jnp.where(row < 4, t[0], pltpu.roll(t[1], 4, 0))
        left = pltpu.roll(jnp.where(row < 4, t[2], pltpu.roll(t[3], 4, 0)), 64, 1)
        send[m] = jnp.where(lane >= 64, right, left)
    source, to = iota((128, 128), 0), iota((128, 128), 1)
    pick = (source >= 64) & (to % 8 == (source % 32) // 4)
    out = dot(jnp.concatenate(terms, axis=0), pick.astype(F32))
    down[...] = jnp.zeros((8, 128), F32)
    for b in range(3):
        for half in range(2):
            total = jnp.zeros((8, 128), F32)
            for g in range(4 * half, 4 * half + 4):
                n = 8 * (3 * g + b)
                total = total + jnp.where((row < 4) & own_lanes(g // 2, g % 2), out[n : n + 8], 0.0)
            down[2 * b + half : 2 * b + half + 1, :] = jnp.sum(total, axis=0, keepdims=True)


SHIFTS = ((-4, -3, -2, -1, 1, 2, 3, 4), (-8, -7, -6, -5, 5, 6, 7, 8))


def bottom_window(ids, stiff, couple, stiff_out, coefs_out):
    tiles = stiff.shape[1] // 128
    for j in range(2 * WINDOW):
        t = jnp.clip(2 * (ids[2] - REACH) + j, 0, tiles - 1)
        span = pl.ds(pl.multiple_of(t * 128, 128), 128)
        v = stiff[:, span]
        for a in range(3):
            stiff_out[a, j : j + 1, :] = v[a : a + 1]
        for k in range(7):
            for a in range(3):
                v = couple[k, a, :, span].astype(F32)
                for b in range(3):
                    coefs_out[k * 9 + a * 3 + b, j : j + 1, :] = v[b : b + 1]
    pad = ROWS - 2 * WINDOW
    for a in range(3):
        stiff_out[a, 2 * WINDOW :, :] = jnp.ones((pad, 128), F32)
    for i in range(63):
        coefs_out[i, 2 * WINDOW :, :] = jnp.zeros((pad, 128), F32)


def bottom_and_up(
    ids, got, mine, bottom_stiff, bottom_coefs, load2, low, mid, high, packed2, pre1, packed1,
    guess1, lower, upper, load, now, guess, first, rest,
):
    load[...] = jnp.zeros((3, ROWS, 128), F32)
    for b in range(3):
        load[b, 2 * REACH : 2 * REACH + 2, :] = mine[2 * b : 2 * b + 2, :]
        for s in range(2):
            for g in range(8):
                p = REACH - SHIFTS[s][g]
                load[b, 2 * p : 2 * p + 2, :] = got[g, 8 * s + 2 * b : 8 * s + 2 * b + 2, :]
    lane = iota((ROWS, 128), 1)
    row = iota((ROWS, 128), 0)
    plane = ids[2] - REACH + row // 2
    inside = (plane >= 0) & (plane < ids[3]) & (row < 2 * WINDOW)
    j, k = (row % 2) * 8 + lane // 16, lane % 16
    weights = [jnp.where(inside, damping / bottom_stiff[a], 0.0) for a in range(3)]
    for a in range(3):
        now[a] = weights[a] * load[a]

    def sweep(_, carry):
        v = [now[b] for b in range(3)]
        views = [v]
        views.append([pltpu.roll(e, 2, 0) for e in v])
        views.append([pltpu.roll(e, ROWS - 2, 0) for e in v])
        low_y, high_y = [], []
        for e in v:
            t = pltpu.roll(e, 16, 1)
            t = jnp.where(lane < 16, pltpu.roll(t, 1, 0), t)
            low_y.append(jnp.where(j == 0, 0.0, t))
            t = pltpu.roll(e, 112, 1)
            t = jnp.where(lane >= 112, pltpu.roll(t, ROWS - 1, 0), t)
            high_y.append(jnp.where(j == 15, 0.0, t))
        views += [low_y, high_y]
        views.append([jnp.where(k == 0, 0.0, pltpu.roll(e, 1, 1)) for e in v])
        views.append([jnp.where(k == 15, 0.0, pltpu.roll(e, 127, 1)) for e in v])
        out = combine([bottom_stiff[a] for a in range(3)], lambda i: bottom_coefs[i], views)
        for a in range(3):
            now[a] = v[a] + weights[a] * (load[a] - out[a])
        return carry

    lax.fori_loop(0, SWEEPS - 1, sweep, 0)

    level = Coarse(packed2)
    row, lane = rows8(), lanes8()

    def spread(b, q, half):
        r = 2 * (REACH + q) + half
        return jnp.broadcast_to(now[b, r : r + 1, :], (8, 128))

    outer, inner = [], []
    for g in range(8):
        here = own_lanes(g // 2, g % 2)
        for b in range(3):
            e = jnp.where(row < 4, spread(b, -1, g // 4), spread(b, 1, g // 4))
            outer.append(jnp.where(here, e, 0.0))
            inner.append(jnp.where(here, spread(b, 0, g // 4), 0.0))
    source, to = iota((128, 128), 0), iota((128, 128), 1)
    pick = (source % 8 == (to % 32) // 4).astype(F32)
    ups = dot(jnp.concatenate(outer + inner, axis=0), pick)
    for g in range(8):
        up = []
        for b in range(3):
            n = 8 * (3 * g + b)
            up.append(jnp.where((row < 4) & (lane >= 64), ups[192 + n : 200 + n], ups[n : n + 8]))
        for a in range(3):
            n = 3 * g + a
            m, u = n // 4, n % 4
            under, over = low[m], high[m]
            if u % 2 == 1:
                under = pltpu.roll(under, 4, 0)
            else:
                over = pltpu.roll(over, 4, 0)
            sides = jnp.where(row < 4, under, over)
            if u < 2:
                sides = pltpu.roll(sides, 64, 1)
            total = jnp.where(lane < 64, sides, jnp.where(row < 4, mid[n], 0.0))
            for b in range(3):
                total = total + level.prolong(g, 3 * a + b) * up[b]
            guess[n] = total

    def use(g, out):
        for a in range(3):
            n = 3 * g + a
            r = load2[n] - out[a]
            rest[n] = r
            first[n] = r / level.stiff(g, a)

    level.apply(guess, use)
    final = []

    def use_last(g, out):
        for a in range(3):
            n = 3 * g + a
            f = first[n]
            e = guess[n] + f + (carry_coef * f + fresh_coef * ((rest[n] - out[a]) / level.stiff(g, a)))
            under = jnp.where((lane >= 64) & (lane < 96), e, 0.0)
            over = jnp.where(lane >= 96, pltpu.roll(e, 4, 0), 0.0)
            final.append(jnp.where(row < 4, under, over))

    level.apply(first, use_last)

    pick = (source >= 64) & (source % 32 == (to % 64) // 2)
    ups = dot(jnp.concatenate(final, axis=0), pick.astype(F32))
    middle = Middle(packed1)
    for g in range(8):
        for a in range(3):
            total = pre1[3 * g + a]
            for b in range(3):
                n = 8 * (3 * g + b)
                total = total + middle.prolong(g, 3 * a + b) * ups[n : n + 8]
            guess1[3 * g + a] = total
    for m in range(12):
        s, t = guess1[2 * m], guess1[2 * m + 1]
        upper[m] = jnp.where(row < 4, pltpu.roll(s, 4, 0), t)
        lower[m] = jnp.where(row < 4, s, pltpu.roll(t, 4, 0))


def middle_up(
    ids, low, mid, high, load, load_edge, packed, pre, own, other, result, xs, ys, guess_edge, first, first_edge, rest, final
):
    fine = Fine(ids)
    level = Middle(packed)
    row = rows8()
    for n in range(24):
        under, over = low[n // 2], high[n // 2]
        if n % 2 == 1:
            under = pltpu.roll(under, 4, 0)
        else:
            over = pltpu.roll(over, 4, 0)
        guess_edge[n] = jnp.where(row < 4, under, over)

    def use(g, out):
        for a in range(3):
            n = 3 * g + a
            r = load[n] - out[a]
            rest[n] = r
            first[n] = r / level.stiff(g, a)

    def use_edge(g, out):
        for a in range(3):
            n = 3 * g + a
            first_edge[n] = (load_edge[n] - out[a]) / level.stiff_edge(g, a)

    level.apply(mid, guess_edge, use, use_edge)

    def use_last(g, out):
        for a in range(3):
            n = 3 * g + a
            f = first[n]
            e = mid[n] + f + (carry_coef * f + fresh_coef * ((rest[n] - out[a]) / level.stiff(g, a)))
            final[g, 8 * a : 8 * a + 8, :] = e

    level.apply(first, first_edge, use_last)
    rows = (iota((48, 24), 0) // 2 == iota((48, 24), 1)).astype(F32)
    source, to = iota((128, 128), 0), iota((128, 128), 1)
    for h in range(2):
        tall = dot(rows, final[2 * ids[1] + fine.spot[h]])
        ups = [dot(tall, (source == 64 * p + to // 2).astype(F32)) for p in range(2)]
        coefs0 = (own, other)[h]
        for a in range(3):
            for x in range(8):
                total = pre[h, 8 * a + x]
                for b in range(3):
                    n = 16 * b + 8 * (x // 4)
                    total = total + coefs0[(63 + 3 * a + b) * 8 + x] * ups[(x // 2) % 2][n : n + 8]
                result[h, 8 * a + x] = total
    fine.send(at(result), xs, ys)


def side_by_side(left, right):
    return jnp.concatenate([left, right], axis=1)


def pack_edges(ids, mc, ms, mp, cc, cs, cp, up, down, coarse):
    def mid(i, x):
        if i < 63:
            return mc[i // 9, i // 3 % 3, i % 3, x].astype(F32)
        return jnp.zeros((4, 64), F32)

    for t in range(32):
        up[t] = side_by_side(mid(2 * t + 1, 3), mid(2 * t, 3))
        down[t] = side_by_side(mid(2 * t, 0), mid(2 * t + 1, 0))
    for a in range(3):
        up[32 + a] = side_by_side(ms[a, 2], ms[a, 3])
        down[32 + a] = side_by_side(ms[a, 0], ms[a, 1])

    def low(i):
        if i < 63:
            got = cc[i // 9, i // 3 % 3, i % 3]
        elif i < 66:
            got = cs[i - 63]
        elif i < 75:
            got = cp[(i - 66) // 3, (i - 66) % 3]
        else:
            return [jnp.zeros((4, 32), F32)] * 2
        return [got[0].astype(F32), got[1].astype(F32)]

    for t in range(38):
        both = jnp.concatenate(low(2 * t) + low(2 * t + 1), axis=1)
        up[35 + t] = both
        down[35 + t] = both
        coarse[t] = both


def pack_levels(ids, mc, ms, mp, low, high, coarse, one, two):
    for i in range(75):
        if i < 63:
            v = [mc[i // 9, i // 3 % 3, i % 3, x].astype(F32) for x in range(4)]
        elif i < 66:
            v = [ms[i - 63, x] for x in range(4)]
        else:
            v = [mp[(i - 66) // 3, (i - 66) % 3, x] for x in range(4)]
        one[i, 0:4, :] = side_by_side(v[0], v[1])
        one[i, 4:8, :] = side_by_side(v[2], v[3])
    for t in range(35):
        one[75 + t, 0:4, :] = low[t]
        one[75 + t, 4:8, :] = high[t]
    lane = iota((4, 128), 1)
    for t in range(38):
        under, here, over = low[35 + t], coarse[t], high[35 + t]
        two[2 * t, 0:4, :] = jnp.where(lane < 64, under, pltpu.roll(here, 64, 1))
        two[2 * t, 4:8, :] = jnp.where(lane < 64, over, 0.0)
        two[2 * t + 1, 0:4, :] = jnp.where(lane < 64, pltpu.roll(under, 64, 1), here)
        two[2 * t + 1, 4:8, :] = jnp.where(lane < 64, pltpu.roll(over, 64, 1), 0.0)


VMEM = pl.BlockSpec(memory_space=pltpu.VMEM)
SMEM = pl.BlockSpec(memory_space=pltpu.SMEM)


def run(kernel, ids, ins, outs, scratch=()):
    return pl.pallas_call(
        kernel,
        out_shape=[jax.ShapeDtypeStruct(s, F32) for s in outs],
        in_specs=[SMEM] + [VMEM] * len(ins),
        out_specs=[VMEM] * len(outs),
        scratch_shapes=[pltpu.VMEM(s, F32) for s in scratch],
        compiler_params=pltpu.CompilerParams(vmem_limit_bytes=24 * 1024 * 1024),
    )(ids, *ins)


def shifted(value, axis, count, shift):
    return lax.ppermute(value, axis, [(i, i + shift) for i in range(count) if 0 <= i + shift < count])


def split_shift(value, axis, count):
    pairs = [(2 * i, 2 * i + 2) for i in range(count - 1)] + [(2 * i + 3, 2 * i + 1) for i in range(count - 1)]
    return lax.ppermute(value, (axis, "ga"), pairs)


def skewed(value, count, shifts):
    pairs = [
        (8 * i + g, 8 * (i + s) + g) for g, s in enumerate(shifts) for i in range(count) if 0 <= i + s < count
    ]
    return lax.ppermute(value, ("gx", "gy", "ga"), pairs)


def group_gather(value):
    return lax.all_to_all(jnp.broadcast_to(value[None], (8,) + value.shape), ("gy", "ga"), 0, 0)


def local(
    right_side,
    fine_stiff,
    fine_couple,
    fine_prolong,
    middle_stiff,
    middle_couple,
    middle_prolong,
    coarse_stiff,
    coarse_couple,
    coarse_prolong,
    bottom_stiff,
    bottom_couple,
):
    count = lax.axis_size("gx")
    gx, gy, ga = lax.axis_index("gx"), lax.axis_index("gy"), lax.axis_index("ga")
    ids = jnp.stack([ga, gy, gx, jnp.int32(count)]).astype(jnp.int32)

    def exchange(xs, ys):
        both = jnp.stack([split_shift(xs, "gx", count), split_shift(ys, "gy", 4)])
        return lax.all_gather(both, "ga")

    half = (2, 24, 8, 128)
    edge = (2, 24, 128)
    block = (24, 8, 128)

    raw = [middle_couple, middle_stiff, middle_prolong]
    up, down, packed = run(
        pack_edges,
        ids,
        raw + [coarse_couple, coarse_stiff, coarse_prolong],
        [(73, 4, 128), (73, 4, 128), (38, 4, 128)],
    )
    below, above = shifted(up, "gx", count, 1), shifted(down, "gx", count, -1)
    one, two = run(pack_levels, ids, raw + [below, above, packed], [(110, 8, 128), (76, 8, 128)])
    packed1 = lax.all_gather(one, ("gy", "ga"))
    packed2 = lax.all_gather(two, ("gy", "ga"))

    ls = lax.all_gather(jnp.stack([right_side.reshape(block), fine_stiff.reshape(block)]), "ga")
    own = jnp.concatenate([fine_couple.astype(F32).reshape(504, 8, 128), fine_prolong.reshape(72, 8, 128)])
    other = lax.ppermute(own, "ga", [(0, 1), (1, 0)])
    first, xs, ys = run(fine_first, ids, [ls], [half, edge, edge])
    halo = exchange(xs, ys)
    rest, second, xs, ys = run(fine_second, ids, [ls, first, halo, own, other], [half, half, edge, edge])

    bottom_s, bottom_c = run(bottom_window, ids, [bottom_stiff, bottom_couple], [(3, ROWS, 128), (63, ROWS, 128)])

    halo = exchange(xs, ys)
    pre0, keep, send = run(
        fine_down, ids, [ls, first, second, rest, halo, own, other], [half, (24, 128), (24, 128)]
    )
    got = group_gather(jnp.concatenate([keep, split_shift(send, "gx", count)]))

    tiles = (24, 8, 128)
    load1, edge1, pre1, load2 = run(
        middle_down, ids, [got, packed1], [tiles, tiles, tiles, (8, 8, 128)], [tiles] * 5
    )
    low, high = shifted(load2, "gx", count, 1), shifted(load2, "gx", count, -1)

    load2, pre2, send, mine = run(
        coarse_down, ids, [low, load2, high, packed2], [tiles, tiles, (6, 8, 128), (8, 128)], [tiles] * 3
    )
    got = group_gather(jnp.concatenate([skewed(mine, count, s) for s in SHIFTS]))
    low, high = shifted(send, "gx", count, 1), shifted(send, "gx", count, -1)

    guess1, lower, upper = run(
        bottom_and_up,
        ids,
        [got, mine, bottom_s, bottom_c, load2, low, pre2, high, packed2, pre1, packed1],
        [tiles, (12, 8, 128), (12, 8, 128)],
        [(3, ROWS, 128), (3, ROWS, 128), tiles, tiles, tiles],
    )
    low, high = shifted(upper, "gx", count, 1), shifted(lower, "gx", count, -1)

    guess, xs, ys = run(
        middle_up,
        ids,
        [low, guess1, high, load1, edge1, packed1, pre0, own, other],
        [half, edge, edge],
        [tiles] * 4 + [(8, 24, 128)],
    )

    halo = exchange(xs, ys)
    rest, first, xs, ys = run(fine_up_first, ids, [ls, guess, halo, own, other], [half, half, edge, edge])
    halo = exchange(xs, ys)
    result, remain, second, xs, ys = run(
        fine_up_second,
        ids,
        [ls, guess, first, rest, halo, own, other],
        [block, block, half, edge, edge],
    )
    halo = exchange(xs, ys)
    (residual,) = run(fine_last, ids, [ls, second, remain, halo, own], [block])
    whole = (3, 8, 8, 128)
    return result.reshape(whole), residual.reshape(whole)


def solution(mesh):
    placed = (
        P(None, "gx", "gy", "ga"),
        P(None, "gx", "gy", "ga"),
        P(None, None, None, "gx", "gy", "ga"),
        P(None, None, "gx", "gy", "ga"),
        P(None, "gx", "gy", "ga"),
        P(None, None, None, "gx", "gy", "ga"),
        P(None, None, "gx", "gy", "ga"),
        P(None, "gx", "gy", "ga"),
        P(None, None, None, "gx", "gy", "ga"),
        P(None, None, "gx", "gy", "ga"),
        P(),
        P(),
    )
    return jax.shard_map(
        local,
        mesh=mesh,
        in_specs=placed,
        out_specs=(P(None, "gx", "gy", "ga"), P(None, "gx", "gy", "ga")),
        check_vma=False,
    )
```

```python
import jax
import jax.numpy as jnp
from jax import lax
from jax.experimental import pallas as pl
from jax.experimental.pallas import tpu as pltpu
from jax.sharding import PartitionSpec as P

SWEEPS = 8
center_value = 1.0
half_width = 0.7
damping = 0.7
ratio_first = half_width / center_value
ratio_second = 1.0 / (2.0 * center_value / half_width - ratio_first)
carry_coef = ratio_second * ratio_first
fresh_coef = 2.0 * ratio_second / half_width

F32 = jnp.float32
REACH = 8
WINDOW = 2 * REACH + 1
ROWS = 40


def iota(shape, dim):
    return lax.broadcasted_iota(jnp.int32, shape, dim)


def dot(a, b):
    return jnp.dot(a, b, precision=lax.Precision.HIGHEST, preferred_element_type=F32)


def combine(stiff, coef, views):
    outs = []
    for a in range(3):
        total = stiff[a] * views[0][a]
        for k in range(7):
            for b in range(3):
                total = total + coef(k * 9 + a * 3 + b) * views[k][b]
        outs.append(total)
    return outs


class Fine:
    def __init__(self, ids):
        self.core = ids[0]
        self.spot = (ids[0], 1 - ids[0])
        right = ids[0].astype(F32)
        self.right = (right, 1.0 - right)
        self.row = iota((8, 128), 0)
        self.lane = iota((8, 128), 1)

    def apply(self, get, halo, stiff, coefs, use, halves=(0, 1)):
        for x in range(8):
            mids = [[get(h, b, x) for b in range(3)] for h in range(2)]
            for h in halves:
                views = [mids[h]]
                spot = self.spot[h]
                lows, highs = [], []
                for b in range(3):
                    lows.append(halo[0, 0, spot, 8 * b : 8 * b + 8, :] if x == 0 else get(h, b, x - 1))
                    highs.append(halo[1, 0, spot, 8 * b : 8 * b + 8, :] if x == 7 else get(h, b, x + 1))
                views += [lows, highs]
                lows, highs = [], []
                for b in range(3):
                    at = 8 * b + x
                    v = mids[h][b]
                    edge = jnp.broadcast_to(halo[0, 1, spot, at : at + 1, :], (8, 128))
                    lows.append(jnp.where(self.row == 0, edge, pltpu.roll(v, 1, 0)))
                    edge = jnp.broadcast_to(halo[1, 1, spot, at : at + 1, :], (8, 128))
                    highs.append(jnp.where(self.row == 7, edge, pltpu.roll(v, 7, 0)))
                views += [lows, highs]
                lows, highs = [], []
                for b in range(3):
                    v, o = mids[h][b], mids[1 - h][b]
                    lows.append(
                        jnp.where(self.lane == 0, pltpu.roll(o, 1, 1) * self.right[h], pltpu.roll(v, 1, 1))
                    )
                    highs.append(
                        jnp.where(
                            self.lane == 127,
                            pltpu.roll(o, 127, 1) * self.right[1 - h],
                            pltpu.roll(v, 127, 1),
                        )
                    )
                views += [lows, highs]
                coef = coefs[h]
                out = combine([stiff(h, a, x) for a in range(3)], lambda i: coef[i * 8 + x], views)
                use(h, x, out)

    def send(self, get, xs, ys):
        up = self.core == 0
        for h in range(2):
            spot = self.spot[h]
            for b in range(3):
                xs[spot, 8 * b : 8 * b + 8, :] = jnp.where(up, get(h, b, 7), get(h, b, 0))
                for x in range(8):
                    v = get(h, b, x)
                    ys[spot, 8 * b + x : 8 * b + x + 1, :] = jnp.where(up, v[7:8], v[0:1])


def at(ref):
    return lambda h, b, x: ref[h, 8 * b + x]


def given(fine, ref, which):
    return lambda h, b, x: ref[fine.spot[h], which, 8 * b + x]


def fine_first(ids, ls, first, xs, ys):
    fine = Fine(ids)
    load, stiff = given(fine, ls, 0), given(fine, ls, 1)
    for h in range(2):
        for i in range(24):
            first[h, i] = load(h, i // 8, i % 8) / stiff(h, i // 8, i % 8)
    fine.send(at(first), xs, ys)


def fine_second(ids, ls, first, halo, own, other, rest, second, xs, ys):
    fine = Fine(ids)
    load, stiff = given(fine, ls, 0), given(fine, ls, 1)

    def use(h, x, out):
        for a in range(3):
            r = load(h, a, x) - out[a]
            rest[h, 8 * a + x] = r
            second[h, 8 * a + x] = carry_coef * first[h, 8 * a + x] + fresh_coef * (r / stiff(h, a, x))

    fine.apply(at(first), halo, stiff, (own, other), use)
    fine.send(at(second), xs, ys)


def fine_down(ids, ls, first, second, rest, halo, own, other, pre, keep, send):
    fine = Fine(ids)
    stiff = given(fine, ls, 1)
    terms = [[[[] for _ in range(4)] for _ in range(3)] for _ in range(2)]
    coefs = (own, other)

    def use(h, x, out):
        r = [rest[h, 8 * a + x] - out[a] for a in range(3)]
        for b in range(3):
            t = sum(coefs[h][(63 + 3 * a + b) * 8 + x] * r[a] for a in range(3))
            terms[h][b][x // 2].append(t)
            pre[h, 8 * b + x] = first[h, 8 * b + x] + second[h, 8 * b + x]

    fine.apply(at(second), halo, stiff, coefs, use)
    pairs = (iota((24, 48), 1) // 2 == iota((24, 48), 0)).astype(F32)
    source, to = iota((128, 128), 0), iota((128, 128), 1)
    tiles = []
    for h in range(2):
        total = None
        for p in range(2):
            stacked = jnp.concatenate([sum(terms[h][b][2 * i + p]) for b in range(3) for i in range(2)], axis=0)
            part = dot(stacked, (to == 64 * p + source // 2).astype(F32))
            total = part if total is None else total + part
        tiles.append(dot(pairs, total))
    keep[...] = tiles[0]
    up = fine.core == 0
    for b in range(3):
        mine = pltpu.roll(tiles[0][8 * b : 8 * b + 8], 4, 0)
        its = tiles[1][8 * b : 8 * b + 8]
        first_rows = fine.row < 4
        send[8 * b : 8 * b + 8, :] = jnp.where(
            up, jnp.where(first_rows, mine, its), jnp.where(first_rows, its, mine)
        )


def fine_up_first(ids, ls, guess, halo, own, other, rest, first, xs, ys):
    fine = Fine(ids)
    load, stiff = given(fine, ls, 0), given(fine, ls, 1)

    def use(h, x, out):
        for a in range(3):
            r = load(h, a, x) - out[a]
            rest[h, 8 * a + x] = r
            first[h, 8 * a + x] = r / stiff(h, a, x)

    fine.apply(at(guess), halo, stiff, (own, other), use)
    fine.send(at(first), xs, ys)


def fine_up_second(ids, ls, guess, first, rest, halo, own, other, result, remain, second, xs, ys):
    fine = Fine(ids)
    stiff = given(fine, ls, 1)

    def use(h, x, out):
        for a in range(3):
            r = rest[h, 8 * a + x] - out[a]
            f = first[h, 8 * a + x]
            s = carry_coef * f + fresh_coef * (r / stiff(h, a, x))
            second[h, 8 * a + x] = s
            if h == 0:
                remain[8 * a + x] = r
                result[8 * a + x] = guess[h, 8 * a + x] + f + s

    fine.apply(at(first), halo, stiff, (own, other), use)
    fine.send(at(second), xs, ys)


def fine_last(ids, ls, second, remain, halo, own, residual):
    fine = Fine(ids)
    stiff = given(fine, ls, 1)

    def use(h, x, out):
        for a in range(3):
            residual[8 * a + x] = remain[8 * a + x] - out[a]

    fine.apply(at(second), halo, stiff, (own, None), use, halves=(0,))


def rows8():
    return iota((8, 128), 0)


def lanes8():
    return iota((8, 128), 1)


class Group:
    def __init__(self, ids, own, other):
        self.packed = (own, other)
        self.spot = (ids[0], 1 - ids[0])
        right = ids[0].astype(F32)
        self.right = (right, 1.0 - right)

    def field(self, g, i):
        return self.packed[g % 2][g // 2, i]

    def sides(self, tiles, g, width):
        row, lane = rows8(), lanes8()
        y, h = g // 2, g % 2
        views = [[], [], [], []]
        for b in range(3):
            v, o = tiles[g][b], tiles[g ^ 1][b]
            edge = pltpu.roll(tiles[g - 2][b], 5, 0) if y > 0 else jnp.zeros_like(v)
            views[0].append(jnp.where(row % 4 == 0, edge, pltpu.roll(v, 1, 0)))
            edge = pltpu.roll(tiles[g + 2][b], 3, 0) if y < 3 else jnp.zeros_like(v)
            views[1].append(jnp.where(row % 4 == 3, edge, pltpu.roll(v, 7, 0)))
            edge = pltpu.roll(o, 129 - width, 1) * self.right[h]
            views[2].append(jnp.where(lane % width == 0, edge, pltpu.roll(v, 1, 1)))
            edge = pltpu.roll(o, width - 1, 1) * self.right[1 - h]
            views[3].append(jnp.where(lane % width == width - 1, edge, pltpu.roll(v, 127, 1)))
        return views


def loaded(ref):
    return [[ref[3 * g + b] for b in range(3)] for g in range(8)]


def filled(stiff):
    return jnp.where(stiff == 0.0, 1.0, stiff)


class Middle(Group):
    def stiff(self, g, a):
        return self.field(g, 63 + a)

    def stiff_edge(self, g, a):
        return filled(self.field(g, 107 + a))

    def prolong(self, g, i):
        return self.field(g, 66 + i)

    def coef(self, g):
        return lambda i: self.field(g, i)

    def coef_edge(self, g):
        def get(i):
            tile = self.field(g, 75 + i // 2)
            return pltpu.roll(tile, 64, 1) if i % 2 else tile

        return get

    def apply(self, own_ref, edge_ref, use, use_edge=None):
        row, lane = rows8(), lanes8()
        own, edge = loaded(own_ref), loaded(edge_ref)
        for g in range(8):
            swap = [pltpu.roll(v, 64, 1) for v in own[g]]
            swap_edge = [pltpu.roll(v, 64, 1) for v in edge[g]]
            turned = [pltpu.roll(v, 4, 0) for v in swap]
            low, high, low_edge, high_edge = [], [], [], []
            for b in range(3):
                low.append(jnp.where(lane >= 64, swap[b], jnp.where(row < 4, swap_edge[b], turned[b])))
                high.append(jnp.where(lane < 64, swap[b], jnp.where(row < 4, turned[b], swap_edge[b])))
                low_edge.append(jnp.where(lane >= 64, swap_edge[b], swap[b]))
                high_edge.append(jnp.where(lane >= 64, swap[b], swap_edge[b]))
            views = [own[g], low, high] + self.sides(own, g, 64)
            use(g, combine([self.stiff(g, a) for a in range(3)], self.coef(g), views))
            if use_edge is not None:
                views = [edge[g], low_edge, high_edge] + self.sides(edge, g, 64)
                use_edge(g, combine([self.stiff_edge(g, a) for a in range(3)], self.coef_edge(g), views))


class Coarse(Group):
    def stiff(self, g, a):
        return filled(self.field(g, 63 + a))

    def prolong(self, g, i):
        return self.field(g, 66 + i)

    def apply(self, ref, use):
        lane = lanes8()
        tiles = loaded(ref)
        for g in range(8):
            low, high = [], []
            for v in tiles[g]:
                t = pltpu.roll(v, 32, 1)
                low.append(jnp.where(lane < 32, pltpu.roll(t, 4, 0), t))
                t = pltpu.roll(v, 96, 1)
                high.append(jnp.where(lane >= 96, pltpu.roll(t, 4, 0), t))
            views = [tiles[g], low, high] + self.sides(tiles, g, 32)
            use(g, combine([self.stiff(g, a) for a in range(3)], lambda i: self.field(g, i), views))


def middle_down(ids, got, packed, other, load, load_edge, pre, down, first, first_edge, rest, second, second_edge):
    level = Middle(ids, packed, other)
    row, lane = rows8(), lanes8()
    for g in range(8):
        y, z = g // 2, level.spot[g % 2]
        for b in range(3):
            n = 3 * g + b
            load[n] = got[z, y, 8 * b : 8 * b + 8, :]
            low = got[0, y, 24 + 8 * b : 32 + 8 * b, :]
            high = got[1, y, 24 + 8 * b : 32 + 8 * b, :]
            low = jnp.where(z == 1, pltpu.roll(low, 4, 0), low)
            high = jnp.where(z == 0, pltpu.roll(high, 4, 0), high)
            load_edge[n] = jnp.where(row < 4, low, high)
            first[n] = load[n] / level.stiff(g, b)
            first_edge[n] = load_edge[n] / level.stiff_edge(g, b)

    def use(g, out):
        for a in range(3):
            n = 3 * g + a
            r = load[n] - out[a]
            rest[n] = r
            second[n] = carry_coef * first[n] + fresh_coef * (r / level.stiff(g, a))

    def use_edge(g, out):
        for a in range(3):
            n = 3 * g + a
            r = load_edge[n] - out[a]
            second_edge[n] = carry_coef * first_edge[n] + fresh_coef * (r / level.stiff_edge(g, a))

    level.apply(first, first_edge, use, use_edge)
    terms = [[], [], []]

    def use_last(g, out):
        r = [rest[3 * g + a] - out[a] for a in range(3)]
        for b in range(3):
            n = 3 * g + b
            pre[n] = first[n] + second[n]
            terms[b].append(sum(level.prolong(g, 3 * a + b) * r[a] for a in range(3)))

    level.apply(second, second_edge, use_last)
    source, to = iota((128, 128), 0), iota((128, 128), 1)
    total = None
    for b in range(3):
        pick = to == 32 * b + (source % 64) // 2
        part = dot(jnp.concatenate(terms[b], axis=0), pick.astype(F32))
        total = part if total is None else total + part
    for g in range(8):
        down[g] = total[8 * g : 8 * g + 8]


def own_lanes(y, z):
    return lanes8() // 8 == (4 * (y % 2) + rows8() % 4) * 2 + z


def coarse_down(ids, low, mid, high, packed, other, load, pre, send, down, first, rest, second):
    level = Coarse(ids, packed, other)
    row, lane = rows8(), lanes8()
    place = lane // 32
    for g in range(8):
        under, here, over = low[g], mid[g], high[g]
        turned = [pltpu.roll(v, 4, 0) for v in (under, here, over)]

        def moved(v, b, to):
            shift = (32 * (to - b)) % 128
            return pltpu.roll(v, shift, 1) if shift else v

        for b in range(3):
            n = 3 * g + b
            top = jnp.where(place == 0, moved(under, b, 0), moved(turned[0], b, 1))
            own = jnp.where(place == 2, moved(here, b, 2), moved(turned[1], b, 3))
            bottom = jnp.where(place == 0, moved(turned[2], b, 0), moved(over, b, 1))
            tile = jnp.where(row < 4, jnp.where(place < 2, top, own), jnp.where(place < 2, bottom, 0.0))
            load[n] = tile
            first[n] = tile / level.stiff(g, b)

    def use(g, out):
        for a in range(3):
            n = 3 * g + a
            r = load[n] - out[a]
            rest[n] = r
            second[n] = carry_coef * first[n] + fresh_coef * (r / level.stiff(g, a))

    level.apply(first, use)
    terms = []

    def use_last(g, out):
        r = [rest[3 * g + a] - out[a] for a in range(3)]
        for b in range(3):
            n = 3 * g + b
            pre[n] = first[n] + second[n]
            terms.append(sum(level.prolong(g, 3 * a + b) * r[a] for a in range(3)))

    level.apply(second, use_last)
    for m in range(6):
        t = [pre[4 * m + i] for i in range(4)]
        right = jnp.where(row < 4, t[0], pltpu.roll(t[1], 4, 0))
        left = pltpu.roll(jnp.where(row < 4, t[2], pltpu.roll(t[3], 4, 0)), 64, 1)
        send[m] = jnp.where(lane >= 64, right, left)
    source, to = iota((128, 128), 0), iota((128, 128), 1)
    pick = (source >= 64) & (to % 8 == (source % 32) // 4)
    out = dot(jnp.concatenate(terms, axis=0), pick.astype(F32))
    down[...] = jnp.zeros((8, 128), F32)
    for b in range(3):
        for half in range(2):
            total = jnp.zeros((8, 128), F32)
            for g in range(4 * half, 4 * half + 4):
                n = 8 * (3 * g + b)
                total = total + jnp.where((row < 4) & own_lanes(g // 2, level.spot[g % 2]), out[n : n + 8], 0.0)
            down[2 * b + half : 2 * b + half + 1, :] = jnp.sum(total, axis=0, keepdims=True)


SHIFTS = ((-4, -3, -2, -1, 1, 2, 3, 4), (-8, -7, -6, -5, 5, 6, 7, 8))


def bottom_window(ids, stiff, couple, stiff_out, coefs_out):
    tiles = ids[3] * 2
    for j in range(2 * WINDOW):
        t = jnp.clip(2 * (ids[2] - REACH) + j, 0, tiles - 1) - ids[4]
        span = pl.ds(pl.multiple_of(t * 128, 128), 128)
        v = stiff[:, span]
        for a in range(3):
            stiff_out[a, j : j + 1, :] = v[a : a + 1]
        for k in range(7):
            for a in range(3):
                v = couple[k, a, :, span].astype(F32)
                for b in range(3):
                    coefs_out[k * 9 + a * 3 + b, j : j + 1, :] = v[b : b + 1]
    pad = ROWS - 2 * WINDOW
    for a in range(3):
        stiff_out[a, 2 * WINDOW :, :] = jnp.ones((pad, 128), F32)
    for i in range(63):
        coefs_out[i, 2 * WINDOW :, :] = jnp.zeros((pad, 128), F32)


def bottom_and_up(
    ids, got, mine, bottom_stiff, bottom_coefs, load2, low, mid, high, packed2, other2, pre1, packed1, other1,
    guess1, lower, upper, load, now, guess, first, rest,
):
    load[...] = jnp.zeros((3, ROWS, 128), F32)
    for b in range(3):
        load[b, 2 * REACH : 2 * REACH + 2, :] = mine[2 * b : 2 * b + 2, :]
        for s in range(2):
            for g in range(8):
                p = REACH - SHIFTS[s][g]
                load[b, 2 * p : 2 * p + 2, :] = got[g % 2, g // 2, 8 * s + 2 * b : 8 * s + 2 * b + 2, :]
    lane = iota((ROWS, 128), 1)
    row = iota((ROWS, 128), 0)
    plane = ids[2] - REACH + row // 2
    inside = (plane >= 0) & (plane < ids[3]) & (row < 2 * WINDOW)
    j, k = (row % 2) * 8 + lane // 16, lane % 16
    weights = [jnp.where(inside, damping / bottom_stiff[a], 0.0) for a in range(3)]
    for a in range(3):
        now[a] = weights[a] * load[a]

    def sweep(_, carry):
        v = [now[b] for b in range(3)]
        views = [v]
        views.append([pltpu.roll(e, 2, 0) for e in v])
        views.append([pltpu.roll(e, ROWS - 2, 0) for e in v])
        low_y, high_y = [], []
        for e in v:
            t = pltpu.roll(e, 16, 1)
            t = jnp.where(lane < 16, pltpu.roll(t, 1, 0), t)
            low_y.append(jnp.where(j == 0, 0.0, t))
            t = pltpu.roll(e, 112, 1)
            t = jnp.where(lane >= 112, pltpu.roll(t, ROWS - 1, 0), t)
            high_y.append(jnp.where(j == 15, 0.0, t))
        views += [low_y, high_y]
        views.append([jnp.where(k == 0, 0.0, pltpu.roll(e, 1, 1)) for e in v])
        views.append([jnp.where(k == 15, 0.0, pltpu.roll(e, 127, 1)) for e in v])
        out = combine([bottom_stiff[a] for a in range(3)], lambda i: bottom_coefs[i], views)
        for a in range(3):
            now[a] = v[a] + weights[a] * (load[a] - out[a])
        return carry

    lax.fori_loop(0, SWEEPS - 1, sweep, 0)

    level = Coarse(ids, packed2, other2)
    row, lane = rows8(), lanes8()

    def spread(b, q, half):
        r = 2 * (REACH + q) + half
        return jnp.broadcast_to(now[b, r : r + 1, :], (8, 128))

    outer, inner = [], []
    for g in range(8):
        here = own_lanes(g // 2, level.spot[g % 2])
        for b in range(3):
            e = jnp.where(row < 4, spread(b, -1, g // 4), spread(b, 1, g // 4))
            outer.append(jnp.where(here, e, 0.0))
            inner.append(jnp.where(here, spread(b, 0, g // 4), 0.0))
    source, to = iota((128, 128), 0), iota((128, 128), 1)
    pick = (source % 8 == (to % 32) // 4).astype(F32)
    ups = dot(jnp.concatenate(outer + inner, axis=0), pick)
    for g in range(8):
        up = []
        for b in range(3):
            n = 8 * (3 * g + b)
            up.append(jnp.where((row < 4) & (lane >= 64), ups[192 + n : 200 + n], ups[n : n + 8]))
        for a in range(3):
            n = 3 * g + a
            m, u = n // 4, n % 4
            under, over = low[m], high[m]
            if u % 2 == 1:
                under = pltpu.roll(under, 4, 0)
            else:
                over = pltpu.roll(over, 4, 0)
            sides = jnp.where(row < 4, under, over)
            if u < 2:
                sides = pltpu.roll(sides, 64, 1)
            total = jnp.where(lane < 64, sides, jnp.where(row < 4, mid[n], 0.0))
            for b in range(3):
                total = total + level.prolong(g, 3 * a + b) * up[b]
            guess[n] = total

    def use(g, out):
        for a in range(3):
            n = 3 * g + a
            r = load2[n] - out[a]
            rest[n] = r
            first[n] = r / level.stiff(g, a)

    level.apply(guess, use)
    final = []

    def use_last(g, out):
        for a in range(3):
            n = 3 * g + a
            f = first[n]
            e = guess[n] + f + (carry_coef * f + fresh_coef * ((rest[n] - out[a]) / level.stiff(g, a)))
            under = jnp.where((lane >= 64) & (lane < 96), e, 0.0)
            over = jnp.where(lane >= 96, pltpu.roll(e, 4, 0), 0.0)
            final.append(jnp.where(row < 4, under, over))

    level.apply(first, use_last)

    pick = (source >= 64) & (source % 32 == (to % 64) // 2)
    ups = dot(jnp.concatenate(final, axis=0), pick.astype(F32))
    middle = Middle(ids, packed1, other1)
    for g in range(8):
        for a in range(3):
            total = pre1[3 * g + a]
            for b in range(3):
                n = 8 * (3 * g + b)
                total = total + middle.prolong(g, 3 * a + b) * ups[n : n + 8]
            guess1[3 * g + a] = total
    for m in range(12):
        s, t = guess1[2 * m], guess1[2 * m + 1]
        upper[m] = jnp.where(row < 4, pltpu.roll(s, 4, 0), t)
        lower[m] = jnp.where(row < 4, s, pltpu.roll(t, 4, 0))


def middle_up(
    ids, low, mid, high, load, load_edge, packed, packed_other, pre, own, other, result, xs, ys, guess_edge, first, first_edge, rest, final
):
    fine = Fine(ids)
    level = Middle(ids, packed, packed_other)
    row = rows8()
    for n in range(24):
        under, over = low[n // 2], high[n // 2]
        if n % 2 == 1:
            under = pltpu.roll(under, 4, 0)
        else:
            over = pltpu.roll(over, 4, 0)
        guess_edge[n] = jnp.where(row < 4, under, over)

    def use(g, out):
        for a in range(3):
            n = 3 * g + a
            r = load[n] - out[a]
            rest[n] = r
            first[n] = r / level.stiff(g, a)

    def use_edge(g, out):
        for a in range(3):
            n = 3 * g + a
            first_edge[n] = (load_edge[n] - out[a]) / level.stiff_edge(g, a)

    level.apply(mid, guess_edge, use, use_edge)

    def use_last(g, out):
        for a in range(3):
            n = 3 * g + a
            f = first[n]
            e = mid[n] + f + (carry_coef * f + fresh_coef * ((rest[n] - out[a]) / level.stiff(g, a)))
            final[g, 8 * a : 8 * a + 8, :] = e

    level.apply(first, first_edge, use_last)
    rows = (iota((48, 24), 0) // 2 == iota((48, 24), 1)).astype(F32)
    source, to = iota((128, 128), 0), iota((128, 128), 1)
    for h in range(2):
        tall = dot(rows, final[2 * ids[1] + h])
        ups = [dot(tall, (source == 64 * p + to // 2).astype(F32)) for p in range(2)]
        coefs0 = (own, other)[h]
        for a in range(3):
            for x in range(8):
                total = pre[h, 8 * a + x]
                for b in range(3):
                    n = 16 * b + 8 * (x // 4)
                    total = total + coefs0[(63 + 3 * a + b) * 8 + x] * ups[(x // 2) % 2][n : n + 8]
                result[h, 8 * a + x] = total
    fine.send(at(result), xs, ys)


def side_by_side(left, right):
    return jnp.concatenate([left, right], axis=1)


def pack_edges(ids, mc, ms, mp, cc, cs, cp, up, down, coarse):
    def mid(i, x):
        if i < 63:
            return mc[i // 9, i // 3 % 3, i % 3, x].astype(F32)
        return jnp.zeros((4, 64), F32)

    for t in range(32):
        up[t] = side_by_side(mid(2 * t + 1, 3), mid(2 * t, 3))
        down[t] = side_by_side(mid(2 * t, 0), mid(2 * t + 1, 0))
    for a in range(3):
        up[32 + a] = side_by_side(ms[a, 2], ms[a, 3])
        down[32 + a] = side_by_side(ms[a, 0], ms[a, 1])

    def low(i):
        if i < 63:
            got = cc[i // 9, i // 3 % 3, i % 3]
        elif i < 66:
            got = cs[i - 63]
        elif i < 75:
            got = cp[(i - 66) // 3, (i - 66) % 3]
        else:
            return [jnp.zeros((4, 32), F32)] * 2
        return [got[0].astype(F32), got[1].astype(F32)]

    for t in range(38):
        both = jnp.concatenate(low(2 * t) + low(2 * t + 1), axis=1)
        up[35 + t] = both
        down[35 + t] = both
        coarse[t] = both


def pack_levels(ids, mc, ms, mp, low, high, coarse, one, two):
    for i in range(75):
        if i < 63:
            v = [mc[i // 9, i // 3 % 3, i % 3, x].astype(F32) for x in range(4)]
        elif i < 66:
            v = [ms[i - 63, x] for x in range(4)]
        else:
            v = [mp[(i - 66) // 3, (i - 66) % 3, x] for x in range(4)]
        one[i, 0:4, :] = side_by_side(v[0], v[1])
        one[i, 4:8, :] = side_by_side(v[2], v[3])
    for t in range(35):
        one[75 + t, 0:4, :] = low[t]
        one[75 + t, 4:8, :] = high[t]
    lane = iota((4, 128), 1)
    for t in range(38):
        under, here, over = low[35 + t], coarse[t], high[35 + t]
        two[2 * t, 0:4, :] = jnp.where(lane < 64, under, pltpu.roll(here, 64, 1))
        two[2 * t, 4:8, :] = jnp.where(lane < 64, over, 0.0)
        two[2 * t + 1, 0:4, :] = jnp.where(lane < 64, pltpu.roll(under, 64, 1), here)
        two[2 * t + 1, 4:8, :] = jnp.where(lane < 64, pltpu.roll(over, 64, 1), 0.0)


VMEM = pl.BlockSpec(memory_space=pltpu.VMEM)
SMEM = pl.BlockSpec(memory_space=pltpu.SMEM)


def run(kernel, ids, ins, outs, scratch=()):
    return pl.pallas_call(
        kernel,
        out_shape=[jax.ShapeDtypeStruct(s, F32) for s in outs],
        in_specs=[SMEM] + [VMEM] * len(ins),
        out_specs=[VMEM] * len(outs),
        scratch_shapes=[pltpu.VMEM(s, F32) for s in scratch],
        compiler_params=pltpu.CompilerParams(vmem_limit_bytes=8 * 1024 * 1024),
    )(ids, *ins)


def shifted(value, axis, count, shift):
    return lax.ppermute(value, axis, [(i, i + shift) for i in range(count) if 0 <= i + shift < count])


def split_shift(value, axis, count):
    pairs = [(2 * i, 2 * i + 2) for i in range(count - 1)] + [(2 * i + 3, 2 * i + 1) for i in range(count - 1)]
    return lax.ppermute(value, (axis, "ga"), pairs)


def skewed(value, count, shifts):
    pairs = [
        (8 * i + g, 8 * (i + s) + g) for g, s in enumerate(shifts) for i in range(count) if 0 <= i + s < count
    ]
    return lax.ppermute(value, ("gx", "gy", "ga"), pairs)


def group_gather(value):
    pair = lax.all_gather(value, "gy", axis_index_groups=[[0, 1], [2, 3]])
    four = lax.all_gather(pair, "gy", axis_index_groups=[[0, 2], [1, 3]])
    return lax.all_gather(four.reshape((4,) + value.shape), "ga")


def local(
    right_side,
    fine_stiff,
    fine_couple,
    fine_prolong,
    middle_stiff,
    middle_couple,
    middle_prolong,
    coarse_stiff,
    coarse_couple,
    coarse_prolong,
    bottom_stiff,
    bottom_couple,
):
    count = lax.axis_size("gx")
    gx, gy, ga = lax.axis_index("gx"), lax.axis_index("gy"), lax.axis_index("ga")
    span = min(WINDOW, count)
    start = 2 * jnp.clip(gx - REACH, 0, count - span)
    ids = jnp.stack([ga, gy, gx, jnp.int32(count), start]).astype(jnp.int32)

    def exchange(xs, ys):
        both = jnp.stack([split_shift(xs, "gx", count), split_shift(ys, "gy", 4)])
        return lax.all_gather(both, "ga")

    half = (2, 24, 8, 128)
    edge = (2, 24, 128)
    block = (24, 8, 128)

    raw = [middle_couple, middle_stiff, middle_prolong]
    up, down, packed = run(
        pack_edges,
        ids,
        raw + [coarse_couple, coarse_stiff, coarse_prolong],
        [(73, 4, 128), (73, 4, 128), (38, 4, 128)],
    )
    below, above = shifted(up, "gx", count, 1), shifted(down, "gx", count, -1)

    ls = lax.all_gather(jnp.stack([right_side.reshape(block), fine_stiff.reshape(block)]), "ga")
    own = jnp.concatenate([fine_couple.astype(F32).reshape(504, 8, 128), fine_prolong.reshape(72, 8, 128)])
    other = lax.ppermute(own, "ga", [(0, 1), (1, 0)])
    first, xs, ys = run(fine_first, ids, [ls], [half, edge, edge])
    below, above, _ = lax.optimization_barrier((below, above, xs))
    one, two = run(pack_levels, ids, raw + [below, above, packed], [(110, 8, 128), (76, 8, 128)])
    swap = [(0, 1), (1, 0)]
    packed1 = lax.all_gather(one, "gy")
    packed2 = lax.all_gather(two, "gy")
    other1 = lax.ppermute(packed1, "ga", swap)
    other2 = lax.ppermute(packed2, "ga", swap)
    halo = exchange(xs, ys)
    rest, second, xs, ys = run(fine_second, ids, [ls, first, halo, own, other], [half, half, edge, edge])

    cut = lax.dynamic_slice_in_dim(bottom_stiff, start * 128, span * 256, 1)
    cut_couple = lax.dynamic_slice_in_dim(bottom_couple, start * 128, span * 256, 3)
    bottom_s, bottom_c = run(bottom_window, ids, [cut, cut_couple], [(3, ROWS, 128), (63, ROWS, 128)])

    halo = exchange(xs, ys)
    pre0, keep, send = run(
        fine_down, ids, [ls, first, second, rest, halo, own, other], [half, (24, 128), (24, 128)]
    )
    got = group_gather(jnp.concatenate([keep, split_shift(send, "gx", count)]))

    tiles = (24, 8, 128)
    load1, edge1, pre1, load2 = run(
        middle_down, ids, [got, packed1, other1], [tiles, tiles, tiles, (8, 8, 128)], [tiles] * 5
    )
    low, high = shifted(load2, "gx", count, 1), shifted(load2, "gx", count, -1)

    load2, pre2, send, mine = run(
        coarse_down, ids, [low, load2, high, packed2, other2], [tiles, tiles, (6, 8, 128), (8, 128)], [tiles] * 3
    )
    got = group_gather(jnp.concatenate([skewed(mine, count, s) for s in SHIFTS]))
    low, high = shifted(send, "gx", count, 1), shifted(send, "gx", count, -1)

    guess1, lower, upper = run(
        bottom_and_up,
        ids,
        [got, mine, bottom_s, bottom_c, load2, low, pre2, high, packed2, other2, pre1, packed1, other1],
        [tiles, (12, 8, 128), (12, 8, 128)],
        [(3, ROWS, 128), (3, ROWS, 128), tiles, tiles, tiles],
    )
    low, high = shifted(upper, "gx", count, 1), shifted(lower, "gx", count, -1)

    guess, xs, ys = run(
        middle_up,
        ids,
        [low, guess1, high, load1, edge1, packed1, other1, pre0, own, other],
        [half, edge, edge],
        [tiles] * 4 + [(8, 24, 128)],
    )

    halo = exchange(xs, ys)
    rest, first, xs, ys = run(fine_up_first, ids, [ls, guess, halo, own, other], [half, half, edge, edge])
    halo = exchange(xs, ys)
    result, remain, second, xs, ys = run(
        fine_up_second,
        ids,
        [ls, guess, first, rest, halo, own, other],
        [block, block, half, edge, edge],
    )
    halo = exchange(xs, ys)
    (residual,) = run(fine_last, ids, [ls, second, remain, halo, own], [block])
    whole = (3, 8, 8, 128)
    return result.reshape(whole), residual.reshape(whole)


def solution(mesh):
    placed = (
        P(None, "gx", "gy", "ga"),
        P(None, "gx", "gy", "ga"),
        P(None, None, None, "gx", "gy", "ga"),
        P(None, None, "gx", "gy", "ga"),
        P(None, "gx", "gy", "ga"),
        P(None, None, None, "gx", "gy", "ga"),
        P(None, None, "gx", "gy", "ga"),
        P(None, "gx", "gy", "ga"),
        P(None, None, None, "gx", "gy", "ga"),
        P(None, None, "gx", "gy", "ga"),
        P(),
        P(),
    )
    return jax.shard_map(
        local,
        mesh=mesh,
        in_specs=placed,
        out_specs=(P(None, "gx", "gy", "ga"), P(None, "gx", "gy", "ga")),
        check_vma=False,
    )
```

```python
import jax
import jax.numpy as jnp
from jax import lax
from jax.experimental import pallas as pl
from jax.experimental.pallas import tpu as pltpu
from jax.sharding import PartitionSpec as P

SWEEPS = 8
center_value = 1.0
half_width = 0.7
damping = 0.7
ratio_first = half_width / center_value
ratio_second = 1.0 / (2.0 * center_value / half_width - ratio_first)
carry_coef = ratio_second * ratio_first
fresh_coef = 2.0 * ratio_second / half_width

F32 = jnp.float32
REACH = 8
WINDOW = 2 * REACH + 1
ROWS = 40


def iota(shape, dim):
    return lax.broadcasted_iota(jnp.int32, shape, dim)


def dot(a, b):
    return jnp.dot(a, b, precision=lax.Precision.HIGHEST, preferred_element_type=F32)


def combine(stiff, coef, views):
    outs = []
    for a in range(3):
        total = stiff[a] * views[0][a]
        for k in range(7):
            for b in range(3):
                total = total + coef(k * 9 + a * 3 + b) * views[k][b]
        outs.append(total)
    return outs


class Fine:
    def __init__(self, ids):
        self.core = ids[0]
        self.spot = (ids[0], 1 - ids[0])
        right = ids[0].astype(F32)
        self.right = (right, 1.0 - right)
        self.row = iota((8, 128), 0)
        self.lane = iota((8, 128), 1)

    def apply(self, get, halo, stiff, coefs, use, halves=(0, 1)):
        for x in range(8):
            mids = [[get(h, b, x) for b in range(3)] for h in range(2)]
            for h in halves:
                views = [mids[h]]
                spot = self.spot[h]
                lows, highs = [], []
                for b in range(3):
                    lows.append(halo[0, 0, spot, 8 * b : 8 * b + 8, :] if x == 0 else get(h, b, x - 1))
                    highs.append(halo[1, 0, spot, 8 * b : 8 * b + 8, :] if x == 7 else get(h, b, x + 1))
                views += [lows, highs]
                lows, highs = [], []
                for b in range(3):
                    at = 8 * b + x
                    v = mids[h][b]
                    edge = jnp.broadcast_to(halo[0, 1, spot, at : at + 1, :], (8, 128))
                    lows.append(jnp.where(self.row == 0, edge, pltpu.roll(v, 1, 0)))
                    edge = jnp.broadcast_to(halo[1, 1, spot, at : at + 1, :], (8, 128))
                    highs.append(jnp.where(self.row == 7, edge, pltpu.roll(v, 7, 0)))
                views += [lows, highs]
                lows, highs = [], []
                for b in range(3):
                    v, o = mids[h][b], mids[1 - h][b]
                    lows.append(
                        jnp.where(self.lane == 0, pltpu.roll(o, 1, 1) * self.right[h], pltpu.roll(v, 1, 1))
                    )
                    highs.append(
                        jnp.where(
                            self.lane == 127,
                            pltpu.roll(o, 127, 1) * self.right[1 - h],
                            pltpu.roll(v, 127, 1),
                        )
                    )
                views += [lows, highs]
                coef = coefs[h]
                out = combine([stiff(h, a, x) for a in range(3)], lambda i: coef[i * 8 + x], views)
                use(h, x, out)

    def send(self, get, xs, ys):
        up = self.core == 0
        for h in range(2):
            spot = self.spot[h]
            for b in range(3):
                xs[spot, 8 * b : 8 * b + 8, :] = jnp.where(up, get(h, b, 7), get(h, b, 0))
                for x in range(8):
                    v = get(h, b, x)
                    ys[spot, 8 * b + x : 8 * b + x + 1, :] = jnp.where(up, v[7:8], v[0:1])


def at(ref):
    return lambda h, b, x: ref[h, 8 * b + x]


def given(fine, ref, which):
    return lambda h, b, x: ref[fine.spot[h], which, 8 * b + x]


def fine_first(ids, ls, couple, prolong, first, xs, ys, own):
    fine = Fine(ids)
    load, stiff = given(fine, ls, 0), given(fine, ls, 1)
    for h in range(2):
        for i in range(24):
            first[h, i] = load(h, i // 8, i % 8) / stiff(h, i // 8, i % 8)
    fine.send(at(first), xs, ys)
    for i in range(63):
        for x in range(8):
            own[8 * i + x] = couple[i // 9, i // 3 % 3, i % 3, x].astype(F32)
    for i in range(9):
        for x in range(8):
            own[504 + 8 * i + x] = prolong[i // 3, i % 3, x]


def fine_second(ids, ls, first, halo, own, other, rest, second, xs, ys):
    fine = Fine(ids)
    load, stiff = given(fine, ls, 0), given(fine, ls, 1)

    def use(h, x, out):
        for a in range(3):
            r = load(h, a, x) - out[a]
            rest[h, 8 * a + x] = r
            second[h, 8 * a + x] = carry_coef * first[h, 8 * a + x] + fresh_coef * (r / stiff(h, a, x))

    fine.apply(at(first), halo, stiff, (own, other), use)
    fine.send(at(second), xs, ys)


def fine_down(ids, ls, first, second, rest, halo, own, other, pre, keep, send):
    fine = Fine(ids)
    stiff = given(fine, ls, 1)
    terms = [[[[] for _ in range(4)] for _ in range(3)] for _ in range(2)]
    coefs = (own, other)

    def use(h, x, out):
        r = [rest[h, 8 * a + x] - out[a] for a in range(3)]
        for b in range(3):
            t = sum(coefs[h][(63 + 3 * a + b) * 8 + x] * r[a] for a in range(3))
            terms[h][b][x // 2].append(t)
            pre[h, 8 * b + x] = first[h, 8 * b + x] + second[h, 8 * b + x]

    fine.apply(at(second), halo, stiff, coefs, use)
    pairs = (iota((24, 48), 1) // 2 == iota((24, 48), 0)).astype(F32)
    source, to = iota((128, 128), 0), iota((128, 128), 1)
    tiles = []
    for h in range(2):
        total = None
        for p in range(2):
            stacked = jnp.concatenate([sum(terms[h][b][2 * i + p]) for b in range(3) for i in range(2)], axis=0)
            part = dot(stacked, (to == 64 * p + source // 2).astype(F32))
            total = part if total is None else total + part
        tiles.append(dot(pairs, total))
    keep[...] = tiles[0]
    up = fine.core == 0
    for b in range(3):
        mine = pltpu.roll(tiles[0][8 * b : 8 * b + 8], 4, 0)
        its = tiles[1][8 * b : 8 * b + 8]
        first_rows = fine.row < 4
        send[8 * b : 8 * b + 8, :] = jnp.where(
            up, jnp.where(first_rows, mine, its), jnp.where(first_rows, its, mine)
        )


def fine_up_first(ids, ls, guess, halo, own, other, rest, first, xs, ys):
    fine = Fine(ids)
    load, stiff = given(fine, ls, 0), given(fine, ls, 1)

    def use(h, x, out):
        for a in range(3):
            r = load(h, a, x) - out[a]
            rest[h, 8 * a + x] = r
            first[h, 8 * a + x] = r / stiff(h, a, x)

    fine.apply(at(guess), halo, stiff, (own, other), use)
    fine.send(at(first), xs, ys)


def fine_up_second(ids, ls, guess, first, rest, halo, own, other, result, remain, second, xs, ys):
    fine = Fine(ids)
    stiff = given(fine, ls, 1)

    def use(h, x, out):
        for a in range(3):
            r = rest[h, 8 * a + x] - out[a]
            f = first[h, 8 * a + x]
            s = carry_coef * f + fresh_coef * (r / stiff(h, a, x))
            second[h, 8 * a + x] = s
            if h == 0:
                remain[8 * a + x] = r
                result[8 * a + x] = guess[h, 8 * a + x] + f + s

    fine.apply(at(first), halo, stiff, (own, other), use)
    fine.send(at(second), xs, ys)


def fine_last(ids, ls, second, remain, halo, own, residual):
    fine = Fine(ids)
    stiff = given(fine, ls, 1)

    def use(h, x, out):
        for a in range(3):
            residual[8 * a + x] = remain[8 * a + x] - out[a]

    fine.apply(at(second), halo, stiff, (own, None), use, halves=(0,))


def rows8():
    return iota((8, 128), 0)


def lanes8():
    return iota((8, 128), 1)


class Group:
    offset = 0

    def __init__(self, ids, own, other):
        self.packed = (own, other)
        self.y = [lax.rem(ids[1] + r, 4) for r in range(4)]
        self.below = [(y != 0).astype(F32) for y in self.y]
        self.above = [(y != 3).astype(F32) for y in self.y]
        self.spot = (ids[0], 1 - ids[0])
        right = ids[0].astype(F32)
        self.right = (right, 1.0 - right)

    def field(self, g, i):
        return self.packed[g % 2][g // 2, self.offset + i]

    def sides(self, tiles, g, width):
        row, lane = rows8(), lanes8()
        r, h = g // 2, g % 2
        down, up = 2 * ((r + 3) % 4) + h, 2 * ((r + 1) % 4) + h
        views = [[], [], [], []]
        for b in range(3):
            v, o = tiles[g][b], tiles[g ^ 1][b]
            edge = pltpu.roll(tiles[down][b], 5, 0) * self.below[r]
            views[0].append(jnp.where(row % 4 == 0, edge, pltpu.roll(v, 1, 0)))
            edge = pltpu.roll(tiles[up][b], 3, 0) * self.above[r]
            views[1].append(jnp.where(row % 4 == 3, edge, pltpu.roll(v, 7, 0)))
            edge = pltpu.roll(o, 129 - width, 1) * self.right[h]
            views[2].append(jnp.where(lane % width == 0, edge, pltpu.roll(v, 1, 1)))
            edge = pltpu.roll(o, width - 1, 1) * self.right[1 - h]
            views[3].append(jnp.where(lane % width == width - 1, edge, pltpu.roll(v, 127, 1)))
        return views


def loaded(ref):
    return [[ref[3 * g + b] for b in range(3)] for g in range(8)]


def filled(stiff):
    return jnp.where(stiff == 0.0, 1.0, stiff)


class Middle(Group):
    def stiff(self, g, a):
        return self.field(g, 63 + a)

    def stiff_edge(self, g, a):
        return filled(self.field(g, 107 + a))

    def prolong(self, g, i):
        return self.field(g, 66 + i)

    def coef(self, g):
        return lambda i: self.field(g, i)

    def coef_edge(self, g):
        def get(i):
            tile = self.field(g, 75 + i // 2)
            return pltpu.roll(tile, 64, 1) if i % 2 else tile

        return get

    def apply(self, own_ref, edge_ref, use, use_edge=None):
        row, lane = rows8(), lanes8()
        own, edge = loaded(own_ref), loaded(edge_ref)
        for g in range(8):
            swap = [pltpu.roll(v, 64, 1) for v in own[g]]
            swap_edge = [pltpu.roll(v, 64, 1) for v in edge[g]]
            turned = [pltpu.roll(v, 4, 0) for v in swap]
            low, high, low_edge, high_edge = [], [], [], []
            for b in range(3):
                low.append(jnp.where(lane >= 64, swap[b], jnp.where(row < 4, swap_edge[b], turned[b])))
                high.append(jnp.where(lane < 64, swap[b], jnp.where(row < 4, turned[b], swap_edge[b])))
                low_edge.append(jnp.where(lane >= 64, swap_edge[b], swap[b]))
                high_edge.append(jnp.where(lane >= 64, swap[b], swap_edge[b]))
            views = [own[g], low, high] + self.sides(own, g, 64)
            use(g, combine([self.stiff(g, a) for a in range(3)], self.coef(g), views))
            if use_edge is not None:
                views = [edge[g], low_edge, high_edge] + self.sides(edge, g, 64)
                use_edge(g, combine([self.stiff_edge(g, a) for a in range(3)], self.coef_edge(g), views))


class Coarse(Group):
    offset = 110

    def stiff(self, g, a):
        return filled(self.field(g, 63 + a))

    def prolong(self, g, i):
        return self.field(g, 66 + i)

    def apply(self, ref, use):
        lane = lanes8()
        tiles = loaded(ref)
        for g in range(8):
            low, high = [], []
            for v in tiles[g]:
                t = pltpu.roll(v, 32, 1)
                low.append(jnp.where(lane < 32, pltpu.roll(t, 4, 0), t))
                t = pltpu.roll(v, 96, 1)
                high.append(jnp.where(lane >= 96, pltpu.roll(t, 4, 0), t))
            views = [tiles[g], low, high] + self.sides(tiles, g, 32)
            use(g, combine([self.stiff(g, a) for a in range(3)], lambda i: self.field(g, i), views))


def middle_down(ids, got, packed, other, load, load_edge, pre, down, first, first_edge, rest, second, second_edge):
    level = Middle(ids, packed, other)
    row, lane = rows8(), lanes8()
    for g in range(8):
        y, z = level.y[g // 2], level.spot[g % 2]
        for b in range(3):
            n = 3 * g + b
            load[n] = got[z, y, 8 * b : 8 * b + 8, :]
            low = got[0, y, 24 + 8 * b : 32 + 8 * b, :]
            high = got[1, y, 24 + 8 * b : 32 + 8 * b, :]
            low = jnp.where(z == 1, pltpu.roll(low, 4, 0), low)
            high = jnp.where(z == 0, pltpu.roll(high, 4, 0), high)
            load_edge[n] = jnp.where(row < 4, low, high)
            first[n] = load[n] / level.stiff(g, b)
            first_edge[n] = load_edge[n] / level.stiff_edge(g, b)

    def use(g, out):
        for a in range(3):
            n = 3 * g + a
            r = load[n] - out[a]
            rest[n] = r
            second[n] = carry_coef * first[n] + fresh_coef * (r / level.stiff(g, a))

    def use_edge(g, out):
        for a in range(3):
            n = 3 * g + a
            r = load_edge[n] - out[a]
            second_edge[n] = carry_coef * first_edge[n] + fresh_coef * (r / level.stiff_edge(g, a))

    level.apply(first, first_edge, use, use_edge)
    terms = [[], [], []]

    def use_last(g, out):
        r = [rest[3 * g + a] - out[a] for a in range(3)]
        for b in range(3):
            n = 3 * g + b
            pre[n] = first[n] + second[n]
            terms[b].append(sum(level.prolong(g, 3 * a + b) * r[a] for a in range(3)))

    level.apply(second, second_edge, use_last)
    source, to = iota((128, 128), 0), iota((128, 128), 1)
    total = None
    for b in range(3):
        pick = to == 32 * b + (source % 64) // 2
        part = dot(jnp.concatenate(terms[b], axis=0), pick.astype(F32))
        total = part if total is None else total + part
    for g in range(8):
        down[g] = total[8 * g : 8 * g + 8]


def own_lanes(y, z):
    return lanes8() // 8 == (4 * (y % 2) + rows8() % 4) * 2 + z


def coarse_down(ids, low, mid, high, packed, other, load, pre, down, first, rest, second, ordered):
    level = Coarse(ids, packed, other)
    row, lane = rows8(), lanes8()
    place = lane // 32
    for g in range(8):
        under, here, over = low[g], mid[g], high[g]
        turned = [pltpu.roll(v, 4, 0) for v in (under, here, over)]

        def moved(v, b, to):
            shift = (32 * (to - b)) % 128
            return pltpu.roll(v, shift, 1) if shift else v

        for b in range(3):
            n = 3 * g + b
            top = jnp.where(place == 0, moved(under, b, 0), moved(turned[0], b, 1))
            own = jnp.where(place == 2, moved(here, b, 2), moved(turned[1], b, 3))
            bottom = jnp.where(place == 0, moved(turned[2], b, 0), moved(over, b, 1))
            tile = jnp.where(row < 4, jnp.where(place < 2, top, own), jnp.where(place < 2, bottom, 0.0))
            load[n] = tile
            first[n] = tile / level.stiff(g, b)

    def use(g, out):
        for a in range(3):
            n = 3 * g + a
            r = load[n] - out[a]
            rest[n] = r
            second[n] = carry_coef * first[n] + fresh_coef * (r / level.stiff(g, a))

    level.apply(first, use)
    terms = []

    def use_last(g, out):
        r = [rest[3 * g + a] - out[a] for a in range(3)]
        for b in range(3):
            n = 3 * g + b
            pre[n] = first[n] + second[n]
            ordered[3 * (2 * level.y[g // 2] + level.spot[g % 2]) + b] = pre[n]
            terms.append(sum(level.prolong(g, 3 * a + b) * r[a] for a in range(3)))

    level.apply(second, use_last)
    for m in range(6):
        t = [ordered[4 * m + i] for i in range(4)]
        right = jnp.where(row < 4, t[0], pltpu.roll(t[1], 4, 0))
        left = pltpu.roll(jnp.where(row < 4, t[2], pltpu.roll(t[3], 4, 0)), 64, 1)
        down[8 + 8 * m : 16 + 8 * m, :] = jnp.where(lane >= 64, right, left)
    source, to = iota((128, 128), 0), iota((128, 128), 1)
    pick = (source >= 64) & (to % 8 == (source % 32) // 4)
    out = dot(jnp.concatenate(terms, axis=0), pick.astype(F32))
    down[0:8, :] = jnp.zeros((8, 128), F32)
    for b in range(3):
        totals = [jnp.zeros((8, 128), F32)] * 2
        for g in range(8):
            n = 8 * (3 * g + b)
            y = level.y[g // 2]
            mine = jnp.where((row < 4) & own_lanes(y, level.spot[g % 2]), out[n : n + 8], 0.0)
            upper = (y // 2).astype(F32)
            totals[0] = totals[0] + mine * (1.0 - upper)
            totals[1] = totals[1] + mine * upper
        for half in range(2):
            down[2 * b + half : 2 * b + half + 1, :] = jnp.sum(totals[half], axis=0, keepdims=True)


SHIFTS = ((-4, -3, -2, -1, 1, 2, 3, 4), (-8, -7, -6, -5, 5, 6, 7, 8))


def bottom_window(ids, stiff, couple, stiff_out, coefs_out):
    tiles = ids[3] * 2
    for j in range(2 * WINDOW):
        t = jnp.clip(2 * (ids[2] - REACH) + j, 0, tiles - 1) - ids[4]
        span = pl.ds(pl.multiple_of(t * 128, 128), 128)
        v = stiff[:, span]
        for a in range(3):
            stiff_out[a, j : j + 1, :] = v[a : a + 1]
        for k in range(7):
            for a in range(3):
                v = couple[k, a, :, span].astype(F32)
                for b in range(3):
                    coefs_out[k * 9 + a * 3 + b, j : j + 1, :] = v[b : b + 1]
    pad = ROWS - 2 * WINDOW
    for a in range(3):
        stiff_out[a, 2 * WINDOW :, :] = jnp.ones((pad, 128), F32)
    for i in range(63):
        coefs_out[i, 2 * WINDOW :, :] = jnp.zeros((pad, 128), F32)


def bottom_and_up(
    ids, got, mine, bottom_stiff, bottom_coefs, load2, mid, packed, other, pre1,
    guess1, lower, upper, load, now, guess, first, rest, ordered,
):
    load[...] = jnp.zeros((3, ROWS, 128), F32)
    for b in range(3):
        load[b, 2 * REACH : 2 * REACH + 2, :] = mine[2 * b : 2 * b + 2, :]
        for s in range(2):
            for g in range(8):
                p = REACH - SHIFTS[s][g]
                load[b, 2 * p : 2 * p + 2, :] = got[g % 2, g // 2, 56 * s + 2 * b : 56 * s + 2 * b + 2, :]
    lane = iota((ROWS, 128), 1)
    row = iota((ROWS, 128), 0)
    plane = ids[2] - REACH + row // 2
    inside = (plane >= 0) & (plane < ids[3]) & (row < 2 * WINDOW)
    j, k = (row % 2) * 8 + lane // 16, lane % 16
    weights = [jnp.where(inside, damping / bottom_stiff[a], 0.0) for a in range(3)]
    for a in range(3):
        now[a] = weights[a] * load[a]

    def sweep(_, carry):
        v = [now[b] for b in range(3)]
        views = [v]
        views.append([pltpu.roll(e, 2, 0) for e in v])
        views.append([pltpu.roll(e, ROWS - 2, 0) for e in v])
        low_y, high_y = [], []
        for e in v:
            t = pltpu.roll(e, 16, 1)
            t = jnp.where(lane < 16, pltpu.roll(t, 1, 0), t)
            low_y.append(jnp.where(j == 0, 0.0, t))
            t = pltpu.roll(e, 112, 1)
            t = jnp.where(lane >= 112, pltpu.roll(t, ROWS - 1, 0), t)
            high_y.append(jnp.where(j == 15, 0.0, t))
        views += [low_y, high_y]
        views.append([jnp.where(k == 0, 0.0, pltpu.roll(e, 1, 1)) for e in v])
        views.append([jnp.where(k == 15, 0.0, pltpu.roll(e, 127, 1)) for e in v])
        out = combine([bottom_stiff[a] for a in range(3)], lambda i: bottom_coefs[i], views)
        for a in range(3):
            now[a] = v[a] + weights[a] * (load[a] - out[a])
        return carry

    lax.fori_loop(0, SWEEPS - 1, sweep, 0)

    level = Coarse(ids, packed, other)
    row, lane = rows8(), lanes8()

    def spread(b, q, y):
        r = 2 * (REACH + q)
        return jnp.broadcast_to(jnp.where(y < 2, now[b, r : r + 1, :], now[b, r + 1 : r + 2, :]), (8, 128))

    for n in range(24):
        m, u = n // 4, n % 4
        rows = slice(8 + 8 * m, 16 + 8 * m)
        under = got[SHIFTS[0].index(1) % 2, SHIFTS[0].index(1) // 2, rows, :]
        over = got[SHIFTS[0].index(-1) % 2, SHIFTS[0].index(-1) // 2, rows, :]
        if u % 2 == 1:
            under = pltpu.roll(under, 4, 0)
        else:
            over = pltpu.roll(over, 4, 0)
        sides = jnp.where(row < 4, under, over)
        ordered[n] = pltpu.roll(sides, 64, 1) if u < 2 else sides
    outer, inner = [], []
    for g in range(8):
        y = level.y[g // 2]
        here = own_lanes(y, level.spot[g % 2])
        for b in range(3):
            e = jnp.where(row < 4, spread(b, -1, y), spread(b, 1, y))
            outer.append(jnp.where(here, e, 0.0))
            inner.append(jnp.where(here, spread(b, 0, y), 0.0))
    source, to = iota((128, 128), 0), iota((128, 128), 1)
    pick = (source % 8 == (to % 32) // 4).astype(F32)
    ups = dot(jnp.concatenate(outer + inner, axis=0), pick)
    for g in range(8):
        up = []
        for b in range(3):
            n = 8 * (3 * g + b)
            up.append(jnp.where((row < 4) & (lane >= 64), ups[192 + n : 200 + n], ups[n : n + 8]))
        for a in range(3):
            n = 3 * g + a
            sides = ordered[3 * (2 * level.y[g // 2] + level.spot[g % 2]) + a]
            total = jnp.where(lane < 64, sides, jnp.where(row < 4, mid[n], 0.0))
            for b in range(3):
                total = total + level.prolong(g, 3 * a + b) * up[b]
            guess[n] = total

    def use(g, out):
        for a in range(3):
            n = 3 * g + a
            r = load2[n] - out[a]
            rest[n] = r
            first[n] = r / level.stiff(g, a)

    level.apply(guess, use)
    final = []

    def use_last(g, out):
        for a in range(3):
            n = 3 * g + a
            f = first[n]
            e = guess[n] + f + (carry_coef * f + fresh_coef * ((rest[n] - out[a]) / level.stiff(g, a)))
            under = jnp.where((lane >= 64) & (lane < 96), e, 0.0)
            over = jnp.where(lane >= 96, pltpu.roll(e, 4, 0), 0.0)
            final.append(jnp.where(row < 4, under, over))

    level.apply(first, use_last)

    pick = (source >= 64) & (source % 32 == (to % 64) // 2)
    ups = dot(jnp.concatenate(final, axis=0), pick.astype(F32))
    middle = Middle(ids, packed, other)
    for g in range(8):
        for a in range(3):
            total = pre1[3 * g + a]
            for b in range(3):
                n = 8 * (3 * g + b)
                total = total + middle.prolong(g, 3 * a + b) * ups[n : n + 8]
            guess1[3 * g + a] = total
    for m in range(12):
        s, t = guess1[2 * m], guess1[2 * m + 1]
        upper[m] = jnp.where(row < 4, pltpu.roll(s, 4, 0), t)
        lower[m] = jnp.where(row < 4, s, pltpu.roll(t, 4, 0))


def middle_up(
    ids, low, mid, high, load, load_edge, packed, packed_other, pre, own, other, result, xs, ys, guess_edge, first, first_edge, rest, final
):
    fine = Fine(ids)
    level = Middle(ids, packed, packed_other)
    row = rows8()
    for n in range(24):
        under, over = low[n // 2], high[n // 2]
        if n % 2 == 1:
            under = pltpu.roll(under, 4, 0)
        else:
            over = pltpu.roll(over, 4, 0)
        guess_edge[n] = jnp.where(row < 4, under, over)

    def use(g, out):
        for a in range(3):
            n = 3 * g + a
            r = load[n] - out[a]
            rest[n] = r
            first[n] = r / level.stiff(g, a)

    def use_edge(g, out):
        for a in range(3):
            n = 3 * g + a
            first_edge[n] = (load_edge[n] - out[a]) / level.stiff_edge(g, a)

    level.apply(mid, guess_edge, use, use_edge)

    def use_last(g, out):
        for a in range(3):
            n = 3 * g + a
            f = first[n]
            e = mid[n] + f + (carry_coef * f + fresh_coef * ((rest[n] - out[a]) / level.stiff(g, a)))
            final[g, 8 * a : 8 * a + 8, :] = e

    level.apply(first, first_edge, use_last)
    rows = (iota((48, 24), 0) // 2 == iota((48, 24), 1)).astype(F32)
    source, to = iota((128, 128), 0), iota((128, 128), 1)
    for h in range(2):
        tall = dot(rows, final[h])
        ups = [dot(tall, (source == 64 * p + to // 2).astype(F32)) for p in range(2)]
        coefs0 = (own, other)[h]
        for a in range(3):
            for x in range(8):
                total = pre[h, 8 * a + x]
                for b in range(3):
                    n = 16 * b + 8 * (x // 4)
                    total = total + coefs0[(63 + 3 * a + b) * 8 + x] * ups[(x // 2) % 2][n : n + 8]
                result[h, 8 * a + x] = total
    fine.send(at(result), xs, ys)


def side_by_side(left, right):
    return jnp.concatenate([left, right], axis=1)


def pack_edges(ids, mc, ms, mp, cc, cs, cp, up, down, coarse, body):
    def mid(i, x):
        if i < 63:
            return mc[i // 9, i // 3 % 3, i % 3, x].astype(F32)
        return jnp.zeros((4, 64), F32)

    for t in range(32):
        up[t] = side_by_side(mid(2 * t + 1, 3), mid(2 * t, 3))
        down[t] = side_by_side(mid(2 * t, 0), mid(2 * t + 1, 0))
    for a in range(3):
        up[32 + a] = side_by_side(ms[a, 2], ms[a, 3])
        down[32 + a] = side_by_side(ms[a, 0], ms[a, 1])

    def low(i):
        if i < 63:
            got = cc[i // 9, i // 3 % 3, i % 3]
        elif i < 66:
            got = cs[i - 63]
        elif i < 75:
            got = cp[(i - 66) // 3, (i - 66) % 3]
        else:
            return [jnp.zeros((4, 32), F32)] * 2
        return [got[0].astype(F32), got[1].astype(F32)]

    for t in range(38):
        both = jnp.concatenate(low(2 * t) + low(2 * t + 1), axis=1)
        up[35 + t] = both
        down[35 + t] = both
        coarse[t] = both


    for i in range(75):
        if i < 63:
            v = [mc[i // 9, i // 3 % 3, i % 3, x].astype(F32) for x in range(4)]
        elif i < 66:
            v = [ms[i - 63, x] for x in range(4)]
        else:
            v = [mp[(i - 66) // 3, (i - 66) % 3, x] for x in range(4)]
        body[i, 0:4, :] = side_by_side(v[0], v[1])
        body[i, 4:8, :] = side_by_side(v[2], v[3])


def pack_levels(ids, body, low, high, coarse, one):
    for i in range(75):
        one[i] = body[i]
    for t in range(35):
        one[75 + t, 0:4, :] = low[t]
        one[75 + t, 4:8, :] = high[t]
    lane = iota((4, 128), 1)
    for t in range(38):
        under, here, over = low[35 + t], coarse[t], high[35 + t]
        one[110 + 2 * t, 0:4, :] = jnp.where(lane < 64, under, pltpu.roll(here, 64, 1))
        one[110 + 2 * t, 4:8, :] = jnp.where(lane < 64, over, 0.0)
        one[111 + 2 * t, 0:4, :] = jnp.where(lane < 64, pltpu.roll(under, 64, 1), here)
        one[111 + 2 * t, 4:8, :] = jnp.where(lane < 64, pltpu.roll(over, 64, 1), 0.0)


VMEM = pl.BlockSpec(memory_space=pltpu.VMEM)
SMEM = pl.BlockSpec(memory_space=pltpu.SMEM)


def run(kernel, ids, ins, outs, scratch=()):
    return pl.pallas_call(
        kernel,
        out_shape=[jax.ShapeDtypeStruct(s, F32) for s in outs],
        in_specs=[SMEM] + [VMEM] * len(ins),
        out_specs=[VMEM] * len(outs),
        scratch_shapes=[pltpu.VMEM(s, F32) for s in scratch],
        compiler_params=pltpu.CompilerParams(vmem_limit_bytes=8 * 1024 * 1024),
    )(ids, *ins)


def shifted(value, axis, count, shift):
    return lax.ppermute(value, axis, [(i, i + shift) for i in range(count) if 0 <= i + shift < count])


def split_shift(value, axis, count):
    pairs = [(2 * i, 2 * i + 2) for i in range(count - 1)] + [(2 * i + 3, 2 * i + 1) for i in range(count - 1)]
    return lax.ppermute(value, (axis, "ga"), pairs)


def skewed(value, count, shifts):
    pairs = [
        (8 * i + g, 8 * (i + s) + g) for g, s in enumerate(shifts) for i in range(count) if 0 <= i + s < count
    ]
    return lax.ppermute(value, ("gx", "gy", "ga"), pairs)


def group_gather(value):
    pair = lax.all_gather(value, "gy", axis_index_groups=[[0, 1], [2, 3]])
    four = lax.all_gather(pair, "gy", axis_index_groups=[[0, 2], [1, 3]])
    return lax.all_gather(four.reshape((4,) + value.shape), "ga")


def local(
    right_side,
    fine_stiff,
    fine_couple,
    fine_prolong,
    middle_stiff,
    middle_couple,
    middle_prolong,
    coarse_stiff,
    coarse_couple,
    coarse_prolong,
    bottom_stiff,
    bottom_couple,
):
    count = lax.axis_size("gx")
    gx, gy, ga = lax.axis_index("gx"), lax.axis_index("gy"), lax.axis_index("ga")
    span = min(WINDOW, count)
    start = 2 * jnp.clip(gx - REACH, 0, count - span)
    ids = jnp.stack([ga, gy, gx, jnp.int32(count), start]).astype(jnp.int32)

    def exchange(xs, ys):
        both = jnp.stack([split_shift(xs, "gx", count), split_shift(ys, "gy", 4)])
        return lax.all_gather(both, "ga")

    half = (2, 24, 8, 128)
    edge = (2, 24, 128)
    block = (24, 8, 128)

    cut = lax.dynamic_slice_in_dim(bottom_stiff, start * 128, span * 256, 1)
    cut_couple = lax.dynamic_slice_in_dim(bottom_couple, start * 128, span * 256, 3)
    bottom_s, bottom_c = run(bottom_window, ids, [cut, cut_couple], [(3, ROWS, 128), (63, ROWS, 128)])
    right_side, middle_stiff, bottom_s = lax.optimization_barrier((right_side, middle_stiff, bottom_s))

    up, down, coarse, body = run(
        pack_edges,
        ids,
        [middle_couple, middle_stiff, middle_prolong, coarse_couple, coarse_stiff, coarse_prolong],
        [(73, 4, 128), (73, 4, 128), (38, 4, 128), (75, 8, 128)],
    )
    below, above = shifted(up, "gx", count, 1), shifted(down, "gx", count, -1)

    ls = lax.all_gather(jnp.stack([right_side.reshape(block), fine_stiff.reshape(block)]), "ga")
    first, xs, ys, own = run(
        fine_first, ids, [ls, fine_couple, fine_prolong], [half, edge, edge, (576, 8, 128)]
    )
    swap = [(0, 1), (1, 0)]
    other = lax.ppermute(own, "ga", swap)
    below, above, _ = lax.optimization_barrier((below, above, xs))
    (bulk,) = run(pack_levels, ids, [body, below, above, coarse], [(186, 8, 128)])
    others = [lax.ppermute(bulk, "gy", [((i + r) % 4, i) for i in range(4)]) for r in range(1, 4)]
    halo = exchange(xs, ys)
    rest, second, xs, ys = run(fine_second, ids, [ls, first, halo, own, other], [half, half, edge, edge])
    others = lax.optimization_barrier((*others, xs))[:3]
    packed = jnp.stack([bulk, *others])
    packed_other = lax.ppermute(packed, "ga", swap)

    halo = exchange(xs, ys)
    pre0, keep, send = run(
        fine_down, ids, [ls, first, second, rest, halo, own, other], [half, (24, 128), (24, 128)]
    )
    got = group_gather(jnp.concatenate([keep, split_shift(send, "gx", count)]))

    tiles = (24, 8, 128)
    load1, edge1, pre1, load2 = run(
        middle_down, ids, [got, packed, packed_other], [tiles, tiles, tiles, (8, 8, 128)], [tiles] * 5
    )
    low, high = shifted(load2, "gx", count, 1), shifted(load2, "gx", count, -1)

    load2, pre2, mine = run(
        coarse_down, ids, [low, load2, high, packed, packed_other], [tiles, tiles, (56, 128)], [tiles] * 4
    )
    got = group_gather(jnp.concatenate([skewed(mine, count, SHIFTS[0]), skewed(mine[:8], count, SHIFTS[1])]))

    guess1, lower, upper = run(
        bottom_and_up,
        ids,
        [got, mine, bottom_s, bottom_c, load2, pre2, packed, packed_other, pre1],
        [tiles, (12, 8, 128), (12, 8, 128)],
        [(3, ROWS, 128), (3, ROWS, 128), tiles, tiles, tiles, tiles],
    )
    low, high = shifted(upper, "gx", count, 1), shifted(lower, "gx", count, -1)

    guess, xs, ys = run(
        middle_up,
        ids,
        [low, guess1, high, load1, edge1, packed, packed_other, pre0, own, other],
        [half, edge, edge],
        [tiles] * 4 + [(8, 24, 128)],
    )

    halo = exchange(xs, ys)
    rest, first, xs, ys = run(fine_up_first, ids, [ls, guess, halo, own, other], [half, half, edge, edge])
    halo = exchange(xs, ys)
    result, remain, second, xs, ys = run(
        fine_up_second,
        ids,
        [ls, guess, first, rest, halo, own, other],
        [block, block, half, edge, edge],
    )
    halo = exchange(xs, ys)
    (residual,) = run(fine_last, ids, [ls, second, remain, halo, own], [block])
    whole = (3, 8, 8, 128)
    return result.reshape(whole), residual.reshape(whole)


def solution(mesh):
    placed = (
        P(None, "gx", "gy", "ga"),
        P(None, "gx", "gy", "ga"),
        P(None, None, None, "gx", "gy", "ga"),
        P(None, None, "gx", "gy", "ga"),
        P(None, "gx", "gy", "ga"),
        P(None, None, None, "gx", "gy", "ga"),
        P(None, None, "gx", "gy", "ga"),
        P(None, "gx", "gy", "ga"),
        P(None, None, None, "gx", "gy", "ga"),
        P(None, None, "gx", "gy", "ga"),
        P(),
        P(),
    )
    return jax.shard_map(
        local,
        mesh=mesh,
        in_specs=placed,
        out_specs=(P(None, "gx", "gy", "ga"), P(None, "gx", "gy", "ga")),
        check_vma=False,
    )
```

```python
import jax
import jax.numpy as jnp
from jax import lax
from jax.experimental import pallas as pl
from jax.experimental.pallas import tpu as pltpu
from jax.sharding import PartitionSpec as P

SWEEPS = 8
center_value = 1.0
half_width = 0.7
damping = 0.7
ratio_first = half_width / center_value
ratio_second = 1.0 / (2.0 * center_value / half_width - ratio_first)
carry_coef = ratio_second * ratio_first
fresh_coef = 2.0 * ratio_second / half_width

F32 = jnp.float32
REACH = 8
WINDOW = 2 * REACH + 1
ROWS = 40


def iota(shape, dim):
    return lax.broadcasted_iota(jnp.int32, shape, dim)


def dot(a, b):
    return jnp.dot(a, b, precision=lax.Precision.HIGHEST, preferred_element_type=F32)


def combine(stiff, coef, views):
    outs = []
    for a in range(3):
        total = stiff[a] * views[0][a]
        for k in range(7):
            for b in range(3):
                total = total + coef(k * 9 + a * 3 + b) * views[k][b]
        outs.append(total)
    return outs


class Fine:
    def __init__(self, ids):
        self.core = ids[0]
        self.spot = (ids[0], 1 - ids[0])
        right = ids[0].astype(F32)
        self.right = (right, 1.0 - right)
        self.row = iota((8, 128), 0)
        self.lane = iota((8, 128), 1)

    def apply(self, get, halo, stiff, coefs, use, halves=(0, 1)):
        for x in range(8):
            mids = [[get(h, b, x) for b in range(3)] for h in range(2)]
            for h in halves:
                views = [mids[h]]
                spot = self.spot[h]
                lows, highs = [], []
                for b in range(3):
                    lows.append(halo[0, 0, spot, 8 * b : 8 * b + 8, :] if x == 0 else get(h, b, x - 1))
                    highs.append(halo[1, 0, spot, 8 * b : 8 * b + 8, :] if x == 7 else get(h, b, x + 1))
                views += [lows, highs]
                lows, highs = [], []
                for b in range(3):
                    at = 8 * b + x
                    v = mids[h][b]
                    edge = jnp.broadcast_to(halo[0, 1, spot, at : at + 1, :], (8, 128))
                    lows.append(jnp.where(self.row == 0, edge, pltpu.roll(v, 1, 0)))
                    edge = jnp.broadcast_to(halo[1, 1, spot, at : at + 1, :], (8, 128))
                    highs.append(jnp.where(self.row == 7, edge, pltpu.roll(v, 7, 0)))
                views += [lows, highs]
                lows, highs = [], []
                for b in range(3):
                    v, o = mids[h][b], mids[1 - h][b]
                    lows.append(
                        jnp.where(self.lane == 0, pltpu.roll(o, 1, 1) * self.right[h], pltpu.roll(v, 1, 1))
                    )
                    highs.append(
                        jnp.where(
                            self.lane == 127,
                            pltpu.roll(o, 127, 1) * self.right[1 - h],
                            pltpu.roll(v, 127, 1),
                        )
                    )
                views += [lows, highs]
                coef = coefs[h]
                out = combine([stiff(h, a, x) for a in range(3)], lambda i: coef[i * 8 + x], views)
                use(h, x, out)

    def send(self, get, xs, ys):
        up = self.core == 0
        for h in range(2):
            spot = self.spot[h]
            for b in range(3):
                xs[spot, 8 * b : 8 * b + 8, :] = jnp.where(up, get(h, b, 7), get(h, b, 0))
                for x in range(8):
                    v = get(h, b, x)
                    ys[spot, 8 * b + x : 8 * b + x + 1, :] = jnp.where(up, v[7:8], v[0:1])


def at(ref):
    return lambda h, b, x: ref[h, 8 * b + x]


def given(fine, ref, which):
    return lambda h, b, x: ref[fine.spot[h], which, 8 * b + x]


def fine_first(ids, ls, couple, prolong, first, xs, ys, own):
    fine = Fine(ids)
    load, stiff = given(fine, ls, 0), given(fine, ls, 1)
    for h in range(2):
        for i in range(24):
            first[h, i] = load(h, i // 8, i % 8) / stiff(h, i // 8, i % 8)
    fine.send(at(first), xs, ys)
    for i in range(63):
        for x in range(8):
            own[8 * i + x] = couple[i // 9, i // 3 % 3, i % 3, x].astype(F32)
    for i in range(9):
        for x in range(8):
            own[504 + 8 * i + x] = prolong[i // 3, i % 3, x]


def fine_second(ids, ls, first, halo, own, other, rest, second, xs, ys):
    fine = Fine(ids)
    load, stiff = given(fine, ls, 0), given(fine, ls, 1)

    def use(h, x, out):
        for a in range(3):
            r = load(h, a, x) - out[a]
            rest[h, 8 * a + x] = r
            second[h, 8 * a + x] = carry_coef * first[h, 8 * a + x] + fresh_coef * (r / stiff(h, a, x))

    fine.apply(at(first), halo, stiff, (own, other), use)
    fine.send(at(second), xs, ys)


def fine_down(ids, ls, first, second, rest, halo, own, other, pre, keep, send):
    fine = Fine(ids)
    stiff = given(fine, ls, 1)
    terms = [[[[] for _ in range(4)] for _ in range(3)] for _ in range(2)]
    coefs = (own, other)

    def use(h, x, out):
        r = [rest[h, 8 * a + x] - out[a] for a in range(3)]
        for b in range(3):
            t = sum(coefs[h][(63 + 3 * a + b) * 8 + x] * r[a] for a in range(3))
            terms[h][b][x // 2].append(t)
            pre[h, 8 * b + x] = first[h, 8 * b + x] + second[h, 8 * b + x]

    fine.apply(at(second), halo, stiff, coefs, use)
    pairs = (iota((24, 48), 1) // 2 == iota((24, 48), 0)).astype(F32)
    source, to = iota((128, 128), 0), iota((128, 128), 1)
    tiles = []
    for h in range(2):
        total = None
        for p in range(2):
            stacked = jnp.concatenate([sum(terms[h][b][2 * i + p]) for b in range(3) for i in range(2)], axis=0)
            part = dot(stacked, (to == 64 * p + source // 2).astype(F32))
            total = part if total is None else total + part
        tiles.append(dot(pairs, total))
    keep[...] = tiles[0]
    up = fine.core == 0
    for b in range(3):
        mine = pltpu.roll(tiles[0][8 * b : 8 * b + 8], 4, 0)
        its = tiles[1][8 * b : 8 * b + 8]
        first_rows = fine.row < 4
        send[8 * b : 8 * b + 8, :] = jnp.where(
            up, jnp.where(first_rows, mine, its), jnp.where(first_rows, its, mine)
        )


def fine_up_first(ids, ls, guess, halo, own, other, rest, first, xs, ys):
    fine = Fine(ids)
    load, stiff = given(fine, ls, 0), given(fine, ls, 1)

    def use(h, x, out):
        for a in range(3):
            r = load(h, a, x) - out[a]
            rest[h, 8 * a + x] = r
            first[h, 8 * a + x] = r / stiff(h, a, x)

    fine.apply(at(guess), halo, stiff, (own, other), use)
    fine.send(at(first), xs, ys)


def fine_up_second(ids, ls, guess, first, rest, halo, own, other, result, remain, second, xs, ys):
    fine = Fine(ids)
    stiff = given(fine, ls, 1)

    def use(h, x, out):
        for a in range(3):
            r = rest[h, 8 * a + x] - out[a]
            f = first[h, 8 * a + x]
            s = carry_coef * f + fresh_coef * (r / stiff(h, a, x))
            second[h, 8 * a + x] = s
            if h == 0:
                remain[8 * a + x] = r
                result[8 * a + x] = guess[h, 8 * a + x] + f + s

    fine.apply(at(first), halo, stiff, (own, other), use)
    fine.send(at(second), xs, ys)


def fine_last(ids, ls, second, remain, halo, own, residual):
    fine = Fine(ids)
    stiff = given(fine, ls, 1)

    def use(h, x, out):
        for a in range(3):
            residual[8 * a + x] = remain[8 * a + x] - out[a]

    fine.apply(at(second), halo, stiff, (own, None), use, halves=(0,))


def rows8():
    return iota((8, 128), 0)


def lanes8():
    return iota((8, 128), 1)


class Group:
    def __init__(self, ids, packed):
        self.packed = packed
        self.y = [lax.rem(ids[1] + r, 4) for r in range(4)]
        self.below = [(y != 0).astype(F32) for y in self.y]
        self.above = [(y != 3).astype(F32) for y in self.y]
        self.spot = (ids[0], 1 - ids[0])
        right = ids[0].astype(F32)
        self.right = (right, 1.0 - right)
        self.place = [2 * self.y[g // 2] + self.spot[g % 2] for g in range(8)]

    def field(self, g, i):
        return self.packed[self.place[g], i]

    def sides(self, tiles, g, width):
        row, lane = rows8(), lanes8()
        r, h = g // 2, g % 2
        down, up = 2 * ((r + 3) % 4) + h, 2 * ((r + 1) % 4) + h
        views = [[], [], [], []]
        for b in range(3):
            v, o = tiles[g][b], tiles[g ^ 1][b]
            edge = pltpu.roll(tiles[down][b], 5, 0) * self.below[r]
            views[0].append(jnp.where(row % 4 == 0, edge, pltpu.roll(v, 1, 0)))
            edge = pltpu.roll(tiles[up][b], 3, 0) * self.above[r]
            views[1].append(jnp.where(row % 4 == 3, edge, pltpu.roll(v, 7, 0)))
            edge = pltpu.roll(o, 129 - width, 1) * self.right[h]
            views[2].append(jnp.where(lane % width == 0, edge, pltpu.roll(v, 1, 1)))
            edge = pltpu.roll(o, width - 1, 1) * self.right[1 - h]
            views[3].append(jnp.where(lane % width == width - 1, edge, pltpu.roll(v, 127, 1)))
        return views


def loaded(ref):
    return [[ref[3 * g + b] for b in range(3)] for g in range(8)]


def filled(stiff):
    return jnp.where(stiff == 0.0, 1.0, stiff)


class Middle(Group):
    def stiff(self, g, a):
        return self.field(g, 63 + a)

    def stiff_edge(self, g, a):
        return filled(self.field(g, 107 + a))

    def prolong(self, g, i):
        return self.field(g, 66 + i)

    def coef(self, g):
        return lambda i: self.field(g, i)

    def coef_edge(self, g):
        def get(i):
            tile = self.field(g, 75 + i // 2)
            return pltpu.roll(tile, 64, 1) if i % 2 else tile

        return get

    def apply(self, own_ref, edge_ref, use, use_edge=None):
        row, lane = rows8(), lanes8()
        own, edge = loaded(own_ref), loaded(edge_ref)
        for g in range(8):
            swap = [pltpu.roll(v, 64, 1) for v in own[g]]
            swap_edge = [pltpu.roll(v, 64, 1) for v in edge[g]]
            turned = [pltpu.roll(v, 4, 0) for v in swap]
            low, high, low_edge, high_edge = [], [], [], []
            for b in range(3):
                low.append(jnp.where(lane >= 64, swap[b], jnp.where(row < 4, swap_edge[b], turned[b])))
                high.append(jnp.where(lane < 64, swap[b], jnp.where(row < 4, turned[b], swap_edge[b])))
                low_edge.append(jnp.where(lane >= 64, swap_edge[b], swap[b]))
                high_edge.append(jnp.where(lane >= 64, swap[b], swap_edge[b]))
            views = [own[g], low, high] + self.sides(own, g, 64)
            use(g, combine([self.stiff(g, a) for a in range(3)], self.coef(g), views))
            if use_edge is not None:
                views = [edge[g], low_edge, high_edge] + self.sides(edge, g, 64)
                use_edge(g, combine([self.stiff_edge(g, a) for a in range(3)], self.coef_edge(g), views))


class Coarse(Group):
    def stiff(self, g, a):
        return filled(self.field(g, 63 + a))

    def prolong(self, g, i):
        return self.field(g, 66 + i)

    def apply(self, ref, use):
        lane = lanes8()
        tiles = loaded(ref)
        for g in range(8):
            low, high = [], []
            for v in tiles[g]:
                t = pltpu.roll(v, 32, 1)
                low.append(jnp.where(lane < 32, pltpu.roll(t, 4, 0), t))
                t = pltpu.roll(v, 96, 1)
                high.append(jnp.where(lane >= 96, pltpu.roll(t, 4, 0), t))
            views = [tiles[g], low, high] + self.sides(tiles, g, 32)
            use(g, combine([self.stiff(g, a) for a in range(3)], lambda i: self.field(g, i), views))


def middle_down(ids, got, packed, load, load_edge, pre, down, first, first_edge, rest, second, second_edge):
    level = Middle(ids, packed)
    row, lane = rows8(), lanes8()
    for g in range(8):
        y, z = level.y[g // 2], level.spot[g % 2]
        for b in range(3):
            n = 3 * g + b
            load[n] = got[z, y, 8 * b : 8 * b + 8, :]
            low = got[0, y, 24 + 8 * b : 32 + 8 * b, :]
            high = got[1, y, 24 + 8 * b : 32 + 8 * b, :]
            low = jnp.where(z == 1, pltpu.roll(low, 4, 0), low)
            high = jnp.where(z == 0, pltpu.roll(high, 4, 0), high)
            load_edge[n] = jnp.where(row < 4, low, high)
            first[n] = load[n] / level.stiff(g, b)
            first_edge[n] = load_edge[n] / level.stiff_edge(g, b)

    def use(g, out):
        for a in range(3):
            n = 3 * g + a
            r = load[n] - out[a]
            rest[n] = r
            second[n] = carry_coef * first[n] + fresh_coef * (r / level.stiff(g, a))

    def use_edge(g, out):
        for a in range(3):
            n = 3 * g + a
            r = load_edge[n] - out[a]
            second_edge[n] = carry_coef * first_edge[n] + fresh_coef * (r / level.stiff_edge(g, a))

    level.apply(first, first_edge, use, use_edge)
    terms = [[], [], []]

    def use_last(g, out):
        r = [rest[3 * g + a] - out[a] for a in range(3)]
        for b in range(3):
            n = 3 * g + b
            pre[n] = first[n] + second[n]
            terms[b].append(sum(level.prolong(g, 3 * a + b) * r[a] for a in range(3)))

    level.apply(second, second_edge, use_last)
    source, to = iota((128, 128), 0), iota((128, 128), 1)
    total = None
    for b in range(3):
        pick = to == 32 * b + (source % 64) // 2
        part = dot(jnp.concatenate(terms[b], axis=0), pick.astype(F32))
        total = part if total is None else total + part
    for g in range(8):
        down[g] = total[8 * g : 8 * g + 8]


def own_lanes(y, z):
    return lanes8() // 8 == (4 * (y % 2) + rows8() % 4) * 2 + z


def coarse_down(ids, low, mid, high, packed, load, pre, down, first, rest, second, ordered):
    level = Coarse(ids, packed)
    row, lane = rows8(), lanes8()
    place = lane // 32
    for g in range(8):
        under, here, over = low[g], mid[g], high[g]
        turned = [pltpu.roll(v, 4, 0) for v in (under, here, over)]

        def moved(v, b, to):
            shift = (32 * (to - b)) % 128
            return pltpu.roll(v, shift, 1) if shift else v

        for b in range(3):
            n = 3 * g + b
            top = jnp.where(place == 0, moved(under, b, 0), moved(turned[0], b, 1))
            own = jnp.where(place == 2, moved(here, b, 2), moved(turned[1], b, 3))
            bottom = jnp.where(place == 0, moved(turned[2], b, 0), moved(over, b, 1))
            tile = jnp.where(row < 4, jnp.where(place < 2, top, own), jnp.where(place < 2, bottom, 0.0))
            load[n] = tile
            first[n] = tile / level.stiff(g, b)

    def use(g, out):
        for a in range(3):
            n = 3 * g + a
            r = load[n] - out[a]
            rest[n] = r
            second[n] = carry_coef * first[n] + fresh_coef * (r / level.stiff(g, a))

    level.apply(first, use)
    terms = []

    def use_last(g, out):
        r = [rest[3 * g + a] - out[a] for a in range(3)]
        for b in range(3):
            n = 3 * g + b
            pre[n] = first[n] + second[n]
            ordered[3 * level.place[g] + b] = pre[n]
            terms.append(sum(level.prolong(g, 3 * a + b) * r[a] for a in range(3)))

    level.apply(second, use_last)
    for m in range(6):
        t = [ordered[4 * m + i] for i in range(4)]
        right = jnp.where(row < 4, t[0], pltpu.roll(t[1], 4, 0))
        left = pltpu.roll(jnp.where(row < 4, t[2], pltpu.roll(t[3], 4, 0)), 64, 1)
        down[8 + 8 * m : 16 + 8 * m, :] = jnp.where(lane >= 64, right, left)
    source, to = iota((128, 128), 0), iota((128, 128), 1)
    pick = (source >= 64) & (to % 8 == (source % 32) // 4)
    out = dot(jnp.concatenate(terms, axis=0), pick.astype(F32))
    down[0:8, :] = jnp.zeros((8, 128), F32)
    for b in range(3):
        totals = [jnp.zeros((8, 128), F32)] * 2
        for g in range(8):
            n = 8 * (3 * g + b)
            y = level.y[g // 2]
            mine = jnp.where((row < 4) & own_lanes(y, level.spot[g % 2]), out[n : n + 8], 0.0)
            upper = (y // 2).astype(F32)
            totals[0] = totals[0] + mine * (1.0 - upper)
            totals[1] = totals[1] + mine * upper
        for half in range(2):
            down[2 * b + half : 2 * b + half + 1, :] = jnp.sum(totals[half], axis=0, keepdims=True)


SHIFTS = ((-4, -3, -2, -1, 1, 2, 3, 4), (-8, -7, -6, -5, 5, 6, 7, 8))


def bottom_window(ids, stiff, couple, stiff_out, coefs_out):
    tiles = ids[3] * 2
    for j in range(2 * WINDOW):
        t = jnp.clip(2 * (ids[2] - REACH) + j, 0, tiles - 1) - ids[4]
        span = pl.ds(pl.multiple_of(t * 128, 128), 128)
        v = stiff[:, span]
        for a in range(3):
            stiff_out[a, j : j + 1, :] = v[a : a + 1]
        for k in range(7):
            for a in range(3):
                v = couple[k, a, :, span].astype(F32)
                for b in range(3):
                    coefs_out[k * 9 + a * 3 + b, j : j + 1, :] = v[b : b + 1]
    pad = ROWS - 2 * WINDOW
    for a in range(3):
        stiff_out[a, 2 * WINDOW :, :] = jnp.ones((pad, 128), F32)
    for i in range(63):
        coefs_out[i, 2 * WINDOW :, :] = jnp.zeros((pad, 128), F32)


def bottom_and_up(
    ids, got, mine, bottom_stiff, bottom_coefs, load2, mid, packed, pre1, packed1,
    guess1, lower, upper, load, now, guess, first, rest, ordered,
):
    load[...] = jnp.zeros((3, ROWS, 128), F32)
    for b in range(3):
        load[b, 2 * REACH : 2 * REACH + 2, :] = mine[2 * b : 2 * b + 2, :]
        for s in range(2):
            for g in range(8):
                p = REACH - SHIFTS[s][g]
                load[b, 2 * p : 2 * p + 2, :] = got[g % 2, g // 2, 56 * s + 2 * b : 56 * s + 2 * b + 2, :]
    lane = iota((ROWS, 128), 1)
    row = iota((ROWS, 128), 0)
    plane = ids[2] - REACH + row // 2
    inside = (plane >= 0) & (plane < ids[3]) & (row < 2 * WINDOW)
    j, k = (row % 2) * 8 + lane // 16, lane % 16
    weights = [jnp.where(inside, damping / bottom_stiff[a], 0.0) for a in range(3)]
    for a in range(3):
        now[a] = weights[a] * load[a]

    def sweep(_, carry):
        v = [now[b] for b in range(3)]
        views = [v]
        views.append([pltpu.roll(e, 2, 0) for e in v])
        views.append([pltpu.roll(e, ROWS - 2, 0) for e in v])
        low_y, high_y = [], []
        for e in v:
            t = pltpu.roll(e, 16, 1)
            t = jnp.where(lane < 16, pltpu.roll(t, 1, 0), t)
            low_y.append(jnp.where(j == 0, 0.0, t))
            t = pltpu.roll(e, 112, 1)
            t = jnp.where(lane >= 112, pltpu.roll(t, ROWS - 1, 0), t)
            high_y.append(jnp.where(j == 15, 0.0, t))
        views += [low_y, high_y]
        views.append([jnp.where(k == 0, 0.0, pltpu.roll(e, 1, 1)) for e in v])
        views.append([jnp.where(k == 15, 0.0, pltpu.roll(e, 127, 1)) for e in v])
        out = combine([bottom_stiff[a] for a in range(3)], lambda i: bottom_coefs[i], views)
        for a in range(3):
            now[a] = v[a] + weights[a] * (load[a] - out[a])
        return carry

    lax.fori_loop(0, SWEEPS - 1, sweep, 0)

    level = Coarse(ids, packed)
    row, lane = rows8(), lanes8()

    def spread(b, q, y):
        r = 2 * (REACH + q)
        return jnp.broadcast_to(jnp.where(y < 2, now[b, r : r + 1, :], now[b, r + 1 : r + 2, :]), (8, 128))

    for n in range(24):
        m, u = n // 4, n % 4
        rows = slice(8 + 8 * m, 16 + 8 * m)
        under = got[SHIFTS[0].index(1) % 2, SHIFTS[0].index(1) // 2, rows, :]
        over = got[SHIFTS[0].index(-1) % 2, SHIFTS[0].index(-1) // 2, rows, :]
        if u % 2 == 1:
            under = pltpu.roll(under, 4, 0)
        else:
            over = pltpu.roll(over, 4, 0)
        sides = jnp.where(row < 4, under, over)
        ordered[n] = pltpu.roll(sides, 64, 1) if u < 2 else sides
    outer, inner = [], []
    for g in range(8):
        y = level.y[g // 2]
        here = own_lanes(y, level.spot[g % 2])
        for b in range(3):
            e = jnp.where(row < 4, spread(b, -1, y), spread(b, 1, y))
            outer.append(jnp.where(here, e, 0.0))
            inner.append(jnp.where(here, spread(b, 0, y), 0.0))
    source, to = iota((128, 128), 0), iota((128, 128), 1)
    pick = (source % 8 == (to % 32) // 4).astype(F32)
    ups = dot(jnp.concatenate(outer + inner, axis=0), pick)
    for g in range(8):
        up = []
        for b in range(3):
            n = 8 * (3 * g + b)
            up.append(jnp.where((row < 4) & (lane >= 64), ups[192 + n : 200 + n], ups[n : n + 8]))
        for a in range(3):
            n = 3 * g + a
            sides = ordered[3 * level.place[g] + a]
            total = jnp.where(lane < 64, sides, jnp.where(row < 4, mid[n], 0.0))
            for b in range(3):
                total = total + level.prolong(g, 3 * a + b) * up[b]
            guess[n] = total

    def use(g, out):
        for a in range(3):
            n = 3 * g + a
            r = load2[n] - out[a]
            rest[n] = r
            first[n] = r / level.stiff(g, a)

    level.apply(guess, use)
    final = []

    def use_last(g, out):
        for a in range(3):
            n = 3 * g + a
            f = first[n]
            e = guess[n] + f + (carry_coef * f + fresh_coef * ((rest[n] - out[a]) / level.stiff(g, a)))
            under = jnp.where((lane >= 64) & (lane < 96), e, 0.0)
            over = jnp.where(lane >= 96, pltpu.roll(e, 4, 0), 0.0)
            final.append(jnp.where(row < 4, under, over))

    level.apply(first, use_last)

    pick = (source >= 64) & (source % 32 == (to % 64) // 2)
    ups = dot(jnp.concatenate(final, axis=0), pick.astype(F32))
    middle = Middle(ids, packed1)
    for g in range(8):
        for a in range(3):
            total = pre1[3 * g + a]
            for b in range(3):
                n = 8 * (3 * g + b)
                total = total + middle.prolong(g, 3 * a + b) * ups[n : n + 8]
            guess1[3 * g + a] = total
    for m in range(12):
        s, t = guess1[2 * m], guess1[2 * m + 1]
        upper[m] = jnp.where(row < 4, pltpu.roll(s, 4, 0), t)
        lower[m] = jnp.where(row < 4, s, pltpu.roll(t, 4, 0))


def middle_up(
    ids, low, mid, high, load, load_edge, packed, pre, own, other, result, xs, ys, guess_edge, first, first_edge, rest, final
):
    fine = Fine(ids)
    level = Middle(ids, packed)
    row = rows8()
    for n in range(24):
        under, over = low[n // 2], high[n // 2]
        if n % 2 == 1:
            under = pltpu.roll(under, 4, 0)
        else:
            over = pltpu.roll(over, 4, 0)
        guess_edge[n] = jnp.where(row < 4, under, over)

    def use(g, out):
        for a in range(3):
            n = 3 * g + a
            r = load[n] - out[a]
            rest[n] = r
            first[n] = r / level.stiff(g, a)

    def use_edge(g, out):
        for a in range(3):
            n = 3 * g + a
            first_edge[n] = (load_edge[n] - out[a]) / level.stiff_edge(g, a)

    level.apply(mid, guess_edge, use, use_edge)

    def use_last(g, out):
        for a in range(3):
            n = 3 * g + a
            f = first[n]
            e = mid[n] + f + (carry_coef * f + fresh_coef * ((rest[n] - out[a]) / level.stiff(g, a)))
            final[g, 8 * a : 8 * a + 8, :] = e

    level.apply(first, first_edge, use_last)
    rows = (iota((48, 24), 0) // 2 == iota((48, 24), 1)).astype(F32)
    source, to = iota((128, 128), 0), iota((128, 128), 1)
    for h in range(2):
        tall = dot(rows, final[h])
        ups = [dot(tall, (source == 64 * p + to // 2).astype(F32)) for p in range(2)]
        coefs0 = (own, other)[h]
        for a in range(3):
            for x in range(8):
                total = pre[h, 8 * a + x]
                for b in range(3):
                    n = 16 * b + 8 * (x // 4)
                    total = total + coefs0[(63 + 3 * a + b) * 8 + x] * ups[(x // 2) % 2][n : n + 8]
                result[h, 8 * a + x] = total
    fine.send(at(result), xs, ys)


def side_by_side(left, right):
    return jnp.concatenate([left, right], axis=1)


def pack_edges(ids, mc, ms, mp, cc, cs, cp, up, down, coarse, body):
    def mid(i, x):
        if i < 63:
            return mc[i // 9, i // 3 % 3, i % 3, x].astype(F32)
        return jnp.zeros((4, 64), F32)

    for t in range(32):
        up[t] = side_by_side(mid(2 * t + 1, 3), mid(2 * t, 3))
        down[t] = side_by_side(mid(2 * t, 0), mid(2 * t + 1, 0))
    for a in range(3):
        up[32 + a] = side_by_side(ms[a, 2], ms[a, 3])
        down[32 + a] = side_by_side(ms[a, 0], ms[a, 1])

    def low(i):
        if i < 63:
            got = cc[i // 9, i // 3 % 3, i % 3]
        elif i < 66:
            got = cs[i - 63]
        elif i < 75:
            got = cp[(i - 66) // 3, (i - 66) % 3]
        else:
            return [jnp.zeros((4, 32), F32)] * 2
        return [got[0].astype(F32), got[1].astype(F32)]

    for t in range(38):
        both = jnp.concatenate(low(2 * t) + low(2 * t + 1), axis=1)
        up[35 + t] = both
        down[35 + t] = both
        coarse[t] = both


    for i in range(75):
        if i < 63:
            v = [mc[i // 9, i // 3 % 3, i % 3, x].astype(F32) for x in range(4)]
        elif i < 66:
            v = [ms[i - 63, x] for x in range(4)]
        else:
            v = [mp[(i - 66) // 3, (i - 66) % 3, x] for x in range(4)]
        body[i, 0:4, :] = side_by_side(v[0], v[1])
        body[i, 4:8, :] = side_by_side(v[2], v[3])


def pack_levels(ids, body, low, high, coarse, one, two):
    for i in range(75):
        one[i] = body[i]
    for t in range(35):
        one[75 + t, 0:4, :] = low[t]
        one[75 + t, 4:8, :] = high[t]
    lane = iota((4, 128), 1)
    for t in range(38):
        under, here, over = low[35 + t], coarse[t], high[35 + t]
        two[2 * t, 0:4, :] = jnp.where(lane < 64, under, pltpu.roll(here, 64, 1))
        two[2 * t, 4:8, :] = jnp.where(lane < 64, over, 0.0)
        two[2 * t + 1, 0:4, :] = jnp.where(lane < 64, pltpu.roll(under, 64, 1), here)
        two[2 * t + 1, 4:8, :] = jnp.where(lane < 64, pltpu.roll(over, 64, 1), 0.0)


VMEM = pl.BlockSpec(memory_space=pltpu.VMEM)
SMEM = pl.BlockSpec(memory_space=pltpu.SMEM)


def run(kernel, ids, ins, outs, scratch=()):
    return pl.pallas_call(
        kernel,
        out_shape=[jax.ShapeDtypeStruct(s, F32) for s in outs],
        in_specs=[SMEM] + [VMEM] * len(ins),
        out_specs=[VMEM] * len(outs),
        scratch_shapes=[pltpu.VMEM(s, F32) for s in scratch],
        compiler_params=pltpu.CompilerParams(vmem_limit_bytes=8 * 1024 * 1024),
    )(ids, *ins)


def shifted(value, axis, count, shift):
    return lax.ppermute(value, axis, [(i, i + shift) for i in range(count) if 0 <= i + shift < count])


def split_shift(value, axis, count):
    pairs = [(2 * i, 2 * i + 2) for i in range(count - 1)] + [(2 * i + 3, 2 * i + 1) for i in range(count - 1)]
    return lax.ppermute(value, (axis, "ga"), pairs)


def skewed(value, count, shifts):
    pairs = [
        (8 * i + g, 8 * (i + s) + g) for g, s in enumerate(shifts) for i in range(count) if 0 <= i + s < count
    ]
    return lax.ppermute(value, ("gx", "gy", "ga"), pairs)


def group_gather(value):
    pair = lax.all_gather(value, "gy", axis_index_groups=[[0, 1], [2, 3]])
    four = lax.all_gather(pair, "gy", axis_index_groups=[[0, 2], [1, 3]])
    return lax.all_gather(four.reshape((4,) + value.shape), "ga")


def local(
    right_side,
    fine_stiff,
    fine_couple,
    fine_prolong,
    middle_stiff,
    middle_couple,
    middle_prolong,
    coarse_stiff,
    coarse_couple,
    coarse_prolong,
    bottom_stiff,
    bottom_couple,
):
    count = lax.axis_size("gx")
    gx, gy, ga = lax.axis_index("gx"), lax.axis_index("gy"), lax.axis_index("ga")
    span = min(WINDOW, count)
    start = 2 * jnp.clip(gx - REACH, 0, count - span)
    ids = jnp.stack([ga, gy, gx, jnp.int32(count), start]).astype(jnp.int32)

    def exchange(xs, ys):
        both = jnp.stack([split_shift(xs, "gx", count), split_shift(ys, "gy", 4)])
        return lax.all_gather(both, "ga")

    half = (2, 24, 8, 128)
    edge = (2, 24, 128)
    block = (24, 8, 128)

    cut = lax.dynamic_slice_in_dim(bottom_stiff, start * 128, span * 256, 1)
    cut_couple = lax.dynamic_slice_in_dim(bottom_couple, start * 128, span * 256, 3)
    bottom_s, bottom_c = run(bottom_window, ids, [cut, cut_couple], [(3, ROWS, 128), (63, ROWS, 128)])
    right_side, middle_stiff, bottom_s = lax.optimization_barrier((right_side, middle_stiff, bottom_s))

    up, down, coarse, body = run(
        pack_edges,
        ids,
        [middle_couple, middle_stiff, middle_prolong, coarse_couple, coarse_stiff, coarse_prolong],
        [(73, 4, 128), (73, 4, 128), (38, 4, 128), (75, 8, 128)],
    )
    below, above = shifted(up, "gx", count, 1), shifted(down, "gx", count, -1)

    ls = lax.all_gather(jnp.stack([right_side.reshape(block), fine_stiff.reshape(block)]), "ga")
    first, xs, ys, own = run(
        fine_first, ids, [ls, fine_couple, fine_prolong], [half, edge, edge, (576, 8, 128)]
    )
    swap = [(0, 1), (1, 0)]
    other = lax.ppermute(own, "ga", swap)
    below, above, _ = lax.optimization_barrier((below, above, xs))
    one, two = run(pack_levels, ids, [body, below, above, coarse], [(110, 8, 128), (76, 8, 128)])
    packed1 = lax.all_gather(one, ("gy", "ga"))
    packed2 = lax.all_gather(two, ("gy", "ga"))
    halo = exchange(xs, ys)
    rest, second, xs, ys = run(fine_second, ids, [ls, first, halo, own, other], [half, half, edge, edge])
    halo = exchange(xs, ys)
    pre0, keep, send = run(
        fine_down, ids, [ls, first, second, rest, halo, own, other], [half, (24, 128), (24, 128)]
    )
    got = group_gather(jnp.concatenate([keep, split_shift(send, "gx", count)]))

    tiles = (24, 8, 128)
    load1, edge1, pre1, load2 = run(
        middle_down, ids, [got, packed1], [tiles, tiles, tiles, (8, 8, 128)], [tiles] * 5
    )
    low, high = shifted(load2, "gx", count, 1), shifted(load2, "gx", count, -1)

    load2, pre2, mine = run(
        coarse_down, ids, [low, load2, high, packed2], [tiles, tiles, (56, 128)], [tiles] * 4
    )
    got = group_gather(jnp.concatenate([skewed(mine, count, SHIFTS[0]), skewed(mine[:8], count, SHIFTS[1])]))

    guess1, lower, upper = run(
        bottom_and_up,
        ids,
        [got, mine, bottom_s, bottom_c, load2, pre2, packed2, pre1, packed1],
        [tiles, (12, 8, 128), (12, 8, 128)],
        [(3, ROWS, 128), (3, ROWS, 128), tiles, tiles, tiles, tiles],
    )
    low, high = shifted(upper, "gx", count, 1), shifted(lower, "gx", count, -1)

    guess, xs, ys = run(
        middle_up,
        ids,
        [low, guess1, high, load1, edge1, packed1, pre0, own, other],
        [half, edge, edge],
        [tiles] * 4 + [(8, 24, 128)],
    )

    halo = exchange(xs, ys)
    rest, first, xs, ys = run(fine_up_first, ids, [ls, guess, halo, own, other], [half, half, edge, edge])
    halo = exchange(xs, ys)
    result, remain, second, xs, ys = run(
        fine_up_second,
        ids,
        [ls, guess, first, rest, halo, own, other],
        [block, block, half, edge, edge],
    )
    halo = exchange(xs, ys)
    (residual,) = run(fine_last, ids, [ls, second, remain, halo, own], [block])
    whole = (3, 8, 8, 128)
    return result.reshape(whole), residual.reshape(whole)


def solution(mesh):
    placed = (
        P(None, "gx", "gy", "ga"),
        P(None, "gx", "gy", "ga"),
        P(None, None, None, "gx", "gy", "ga"),
        P(None, None, "gx", "gy", "ga"),
        P(None, "gx", "gy", "ga"),
        P(None, None, None, "gx", "gy", "ga"),
        P(None, None, "gx", "gy", "ga"),
        P(None, "gx", "gy", "ga"),
        P(None, None, None, "gx", "gy", "ga"),
        P(None, None, "gx", "gy", "ga"),
        P(),
        P(),
    )
    return jax.shard_map(
        local,
        mesh=mesh,
        in_specs=placed,
        out_specs=(P(None, "gx", "gy", "ga"), P(None, "gx", "gy", "ga")),
        check_vma=False,
    )
```

```python
import jax
import jax.numpy as jnp
from jax import lax
from jax.experimental import pallas as pl
from jax.experimental.pallas import tpu as pltpu
from jax.sharding import PartitionSpec as P

SWEEPS = 8
center_value = 1.0
half_width = 0.7
damping = 0.7
ratio_first = half_width / center_value
ratio_second = 1.0 / (2.0 * center_value / half_width - ratio_first)
carry_coef = ratio_second * ratio_first
fresh_coef = 2.0 * ratio_second / half_width

F32 = jnp.float32
REACH = 8
WINDOW = 2 * REACH + 1
ROWS = 40


def iota(shape, dim):
    return lax.broadcasted_iota(jnp.int32, shape, dim)


def dot(a, b):
    return jnp.dot(a, b, precision=lax.Precision.HIGHEST, preferred_element_type=F32)


def combine(stiff, coef, views):
    outs = []
    for a in range(3):
        total = stiff[a] * views[0][a]
        for k in range(7):
            for b in range(3):
                total = total + coef(k * 9 + a * 3 + b) * views[k][b]
        outs.append(total)
    return outs


class Fine:
    def __init__(self, ids):
        self.core = ids[0]
        self.spot = (ids[0], 1 - ids[0])
        right = ids[0].astype(F32)
        self.right = (right, 1.0 - right)
        self.row = iota((8, 128), 0)
        self.lane = iota((8, 128), 1)

    def apply(self, get, halo, stiff, coefs, use, halves=(0, 1)):
        for x in range(8):
            mids = [[get(h, b, x) for b in range(3)] for h in range(2)]
            for h in halves:
                views = [mids[h]]
                spot = self.spot[h]
                lows, highs = [], []
                for b in range(3):
                    lows.append(halo[0, 0, spot, 8 * b : 8 * b + 8, :] if x == 0 else get(h, b, x - 1))
                    highs.append(halo[1, 0, spot, 8 * b : 8 * b + 8, :] if x == 7 else get(h, b, x + 1))
                views += [lows, highs]
                lows, highs = [], []
                for b in range(3):
                    at = 8 * b + x
                    v = mids[h][b]
                    edge = jnp.broadcast_to(halo[0, 1, spot, at : at + 1, :], (8, 128))
                    lows.append(jnp.where(self.row == 0, edge, pltpu.roll(v, 1, 0)))
                    edge = jnp.broadcast_to(halo[1, 1, spot, at : at + 1, :], (8, 128))
                    highs.append(jnp.where(self.row == 7, edge, pltpu.roll(v, 7, 0)))
                views += [lows, highs]
                lows, highs = [], []
                for b in range(3):
                    v, o = mids[h][b], mids[1 - h][b]
                    lows.append(
                        jnp.where(self.lane == 0, pltpu.roll(o, 1, 1) * self.right[h], pltpu.roll(v, 1, 1))
                    )
                    highs.append(
                        jnp.where(
                            self.lane == 127,
                            pltpu.roll(o, 127, 1) * self.right[1 - h],
                            pltpu.roll(v, 127, 1),
                        )
                    )
                views += [lows, highs]
                coef = coefs[h]
                out = combine([stiff(h, a, x) for a in range(3)], lambda i: coef[i * 8 + x], views)
                use(h, x, out)

    def send(self, get, xs, ys):
        up = self.core == 0
        for h in range(2):
            spot = self.spot[h]
            for b in range(3):
                xs[spot, 8 * b : 8 * b + 8, :] = jnp.where(up, get(h, b, 7), get(h, b, 0))
                for x in range(8):
                    v = get(h, b, x)
                    ys[spot, 8 * b + x : 8 * b + x + 1, :] = jnp.where(up, v[7:8], v[0:1])


def at(ref):
    return lambda h, b, x: ref[h, 8 * b + x]


def given(fine, ref, which):
    return lambda h, b, x: ref[fine.spot[h], which, 8 * b + x]


def fine_first(ids, ls, couple, prolong, first, xs, ys, own):
    fine = Fine(ids)
    load, stiff = given(fine, ls, 0), given(fine, ls, 1)
    for h in range(2):
        for i in range(24):
            first[h, i] = load(h, i // 8, i % 8) / stiff(h, i // 8, i % 8)
    fine.send(at(first), xs, ys)
    for i in range(63):
        for x in range(8):
            own[8 * i + x] = couple[i // 9, i // 3 % 3, i % 3, x].astype(F32)
    for i in range(9):
        for x in range(8):
            own[504 + 8 * i + x] = prolong[i // 3, i % 3, x]


def fine_second(ids, ls, first, halo, own, other, rest, second, xs, ys):
    fine = Fine(ids)
    load, stiff = given(fine, ls, 0), given(fine, ls, 1)

    def use(h, x, out):
        for a in range(3):
            r = load(h, a, x) - out[a]
            rest[h, 8 * a + x] = r
            second[h, 8 * a + x] = carry_coef * first[h, 8 * a + x] + fresh_coef * (r / stiff(h, a, x))

    fine.apply(at(first), halo, stiff, (own, other), use)
    fine.send(at(second), xs, ys)


def fine_down(ids, ls, first, second, rest, halo, own, other, pre, keep, send):
    fine = Fine(ids)
    stiff = given(fine, ls, 1)
    terms = [[[[] for _ in range(4)] for _ in range(3)] for _ in range(2)]
    coefs = (own, other)

    def use(h, x, out):
        r = [rest[h, 8 * a + x] - out[a] for a in range(3)]
        for b in range(3):
            t = sum(coefs[h][(63 + 3 * a + b) * 8 + x] * r[a] for a in range(3))
            terms[h][b][x // 2].append(t)
            pre[h, 8 * b + x] = first[h, 8 * b + x] + second[h, 8 * b + x]

    fine.apply(at(second), halo, stiff, coefs, use)
    pairs = (iota((24, 48), 1) // 2 == iota((24, 48), 0)).astype(F32)
    source, to = iota((128, 128), 0), iota((128, 128), 1)
    tiles = []
    for h in range(2):
        total = None
        for p in range(2):
            stacked = jnp.concatenate([sum(terms[h][b][2 * i + p]) for b in range(3) for i in range(2)], axis=0)
            part = dot(stacked, (to == 64 * p + source // 2).astype(F32))
            total = part if total is None else total + part
        tiles.append(dot(pairs, total))
    keep[...] = tiles[0]
    up = fine.core == 0
    for b in range(3):
        mine = pltpu.roll(tiles[0][8 * b : 8 * b + 8], 4, 0)
        its = tiles[1][8 * b : 8 * b + 8]
        first_rows = fine.row < 4
        send[8 * b : 8 * b + 8, :] = jnp.where(
            up, jnp.where(first_rows, mine, its), jnp.where(first_rows, its, mine)
        )


def fine_up_first(ids, ls, guess, halo, own, other, rest, first, xs, ys):
    fine = Fine(ids)
    load, stiff = given(fine, ls, 0), given(fine, ls, 1)

    def use(h, x, out):
        for a in range(3):
            r = load(h, a, x) - out[a]
            rest[h, 8 * a + x] = r
            first[h, 8 * a + x] = r / stiff(h, a, x)

    fine.apply(at(guess), halo, stiff, (own, other), use)
    fine.send(at(first), xs, ys)


def fine_up_second(ids, ls, guess, first, rest, halo, own, other, result, remain, second, xs, ys):
    fine = Fine(ids)
    stiff = given(fine, ls, 1)

    def use(h, x, out):
        for a in range(3):
            r = rest[h, 8 * a + x] - out[a]
            f = first[h, 8 * a + x]
            s = carry_coef * f + fresh_coef * (r / stiff(h, a, x))
            second[h, 8 * a + x] = s
            if h == 0:
                remain[8 * a + x] = r
                result[8 * a + x] = guess[h, 8 * a + x] + f + s

    fine.apply(at(first), halo, stiff, (own, other), use)
    fine.send(at(second), xs, ys)


def fine_last(ids, ls, second, remain, halo, own, residual):
    fine = Fine(ids)
    stiff = given(fine, ls, 1)

    def use(h, x, out):
        for a in range(3):
            residual[8 * a + x] = remain[8 * a + x] - out[a]

    fine.apply(at(second), halo, stiff, (own, None), use, halves=(0,))


def rows8():
    return iota((8, 128), 0)


def lanes8():
    return iota((8, 128), 1)


class Group:
    def __init__(self, ids, packed):
        self.packed = packed
        self.y = [lax.rem(ids[1] + r, 4) for r in range(4)]
        self.below = [(y != 0).astype(F32) for y in self.y]
        self.above = [(y != 3).astype(F32) for y in self.y]
        self.spot = (ids[0], 1 - ids[0])
        right = ids[0].astype(F32)
        self.right = (right, 1.0 - right)
        self.place = [2 * self.y[g // 2] + self.spot[g % 2] for g in range(8)]

    def field(self, g, i):
        return self.packed[self.place[g], i]

    def sides(self, tiles, g, width):
        row, lane = rows8(), lanes8()
        r, h = g // 2, g % 2
        down, up = 2 * ((r + 3) % 4) + h, 2 * ((r + 1) % 4) + h
        views = [[], [], [], []]
        for b in range(3):
            v, o = tiles[g][b], tiles[g ^ 1][b]
            edge = pltpu.roll(tiles[down][b], 5, 0) * self.below[r]
            views[0].append(jnp.where(row % 4 == 0, edge, pltpu.roll(v, 1, 0)))
            edge = pltpu.roll(tiles[up][b], 3, 0) * self.above[r]
            views[1].append(jnp.where(row % 4 == 3, edge, pltpu.roll(v, 7, 0)))
            edge = pltpu.roll(o, 129 - width, 1) * self.right[h]
            views[2].append(jnp.where(lane % width == 0, edge, pltpu.roll(v, 1, 1)))
            edge = pltpu.roll(o, width - 1, 1) * self.right[1 - h]
            views[3].append(jnp.where(lane % width == width - 1, edge, pltpu.roll(v, 127, 1)))
        return views


def loaded(ref):
    return [[ref[3 * g + b] for b in range(3)] for g in range(8)]


def filled(stiff):
    return jnp.where(stiff == 0.0, 1.0, stiff)


class Middle(Group):
    def stiff(self, g, a):
        return self.field(g, 63 + a)

    def stiff_edge(self, g, a):
        return filled(self.field(g, 107 + a))

    def prolong(self, g, i):
        return self.field(g, 66 + i)

    def coef(self, g):
        return lambda i: self.field(g, i)

    def coef_edge(self, g):
        def get(i):
            tile = self.field(g, 75 + i // 2)
            return pltpu.roll(tile, 64, 1) if i % 2 else tile

        return get

    def apply(self, own_ref, edge_ref, use, use_edge=None):
        row, lane = rows8(), lanes8()
        own, edge = loaded(own_ref), loaded(edge_ref)
        for g in range(8):
            swap = [pltpu.roll(v, 64, 1) for v in own[g]]
            swap_edge = [pltpu.roll(v, 64, 1) for v in edge[g]]
            turned = [pltpu.roll(v, 4, 0) for v in swap]
            low, high, low_edge, high_edge = [], [], [], []
            for b in range(3):
                low.append(jnp.where(lane >= 64, swap[b], jnp.where(row < 4, swap_edge[b], turned[b])))
                high.append(jnp.where(lane < 64, swap[b], jnp.where(row < 4, turned[b], swap_edge[b])))
                low_edge.append(jnp.where(lane >= 64, swap_edge[b], swap[b]))
                high_edge.append(jnp.where(lane >= 64, swap[b], swap_edge[b]))
            views = [own[g], low, high] + self.sides(own, g, 64)
            use(g, combine([self.stiff(g, a) for a in range(3)], self.coef(g), views))
            if use_edge is not None:
                views = [edge[g], low_edge, high_edge] + self.sides(edge, g, 64)
                use_edge(g, combine([self.stiff_edge(g, a) for a in range(3)], self.coef_edge(g), views))


class Coarse(Group):
    def stiff(self, g, a):
        return filled(self.field(g, 63 + a))

    def prolong(self, g, i):
        return self.field(g, 66 + i)

    def apply(self, ref, use):
        lane = lanes8()
        tiles = loaded(ref)
        for g in range(8):
            low, high = [], []
            for v in tiles[g]:
                t = pltpu.roll(v, 32, 1)
                low.append(jnp.where(lane < 32, pltpu.roll(t, 4, 0), t))
                t = pltpu.roll(v, 96, 1)
                high.append(jnp.where(lane >= 96, pltpu.roll(t, 4, 0), t))
            views = [tiles[g], low, high] + self.sides(tiles, g, 32)
            use(g, combine([self.stiff(g, a) for a in range(3)], lambda i: self.field(g, i), views))


def middle_down(ids, got, packed, load, load_edge, pre, down, first, first_edge, rest, second, second_edge):
    level = Middle(ids, packed)
    row, lane = rows8(), lanes8()
    for g in range(8):
        y, z = level.y[g // 2], level.spot[g % 2]
        for b in range(3):
            n = 3 * g + b
            load[n] = got[z, y, 8 * b : 8 * b + 8, :]
            low = got[0, y, 24 + 8 * b : 32 + 8 * b, :]
            high = got[1, y, 24 + 8 * b : 32 + 8 * b, :]
            low = jnp.where(z == 1, pltpu.roll(low, 4, 0), low)
            high = jnp.where(z == 0, pltpu.roll(high, 4, 0), high)
            load_edge[n] = jnp.where(row < 4, low, high)
            first[n] = load[n] / level.stiff(g, b)
            first_edge[n] = load_edge[n] / level.stiff_edge(g, b)

    def use(g, out):
        for a in range(3):
            n = 3 * g + a
            r = load[n] - out[a]
            rest[n] = r
            second[n] = carry_coef * first[n] + fresh_coef * (r / level.stiff(g, a))

    def use_edge(g, out):
        for a in range(3):
            n = 3 * g + a
            r = load_edge[n] - out[a]
            second_edge[n] = carry_coef * first_edge[n] + fresh_coef * (r / level.stiff_edge(g, a))

    level.apply(first, first_edge, use, use_edge)
    terms = [[], [], []]

    def use_last(g, out):
        r = [rest[3 * g + a] - out[a] for a in range(3)]
        for b in range(3):
            n = 3 * g + b
            pre[n] = first[n] + second[n]
            terms[b].append(sum(level.prolong(g, 3 * a + b) * r[a] for a in range(3)))

    level.apply(second, second_edge, use_last)
    source, to = iota((128, 128), 0), iota((128, 128), 1)
    total = None
    for b in range(3):
        pick = to == 32 * b + (source % 64) // 2
        part = dot(jnp.concatenate(terms[b], axis=0), pick.astype(F32))
        total = part if total is None else total + part
    for g in range(8):
        down[g] = total[8 * g : 8 * g + 8]


def own_lanes(y, z):
    return lanes8() // 8 == (4 * (y % 2) + rows8() % 4) * 2 + z


def coarse_down(ids, low, mid, high, packed, load, pre, down, first, rest, second, ordered):
    level = Coarse(ids, packed)
    row, lane = rows8(), lanes8()
    place = lane // 32
    for g in range(8):
        under, here, over = low[g], mid[g], high[g]
        turned = [pltpu.roll(v, 4, 0) for v in (under, here, over)]

        def moved(v, b, to):
            shift = (32 * (to - b)) % 128
            return pltpu.roll(v, shift, 1) if shift else v

        for b in range(3):
            n = 3 * g + b
            top = jnp.where(place == 0, moved(under, b, 0), moved(turned[0], b, 1))
            own = jnp.where(place == 2, moved(here, b, 2), moved(turned[1], b, 3))
            bottom = jnp.where(place == 0, moved(turned[2], b, 0), moved(over, b, 1))
            tile = jnp.where(row < 4, jnp.where(place < 2, top, own), jnp.where(place < 2, bottom, 0.0))
            load[n] = tile
            first[n] = tile / level.stiff(g, b)

    def use(g, out):
        for a in range(3):
            n = 3 * g + a
            r = load[n] - out[a]
            rest[n] = r
            second[n] = carry_coef * first[n] + fresh_coef * (r / level.stiff(g, a))

    level.apply(first, use)
    terms = []

    def use_last(g, out):
        r = [rest[3 * g + a] - out[a] for a in range(3)]
        for b in range(3):
            n = 3 * g + b
            pre[n] = first[n] + second[n]
            ordered[3 * level.place[g] + b] = pre[n]
            terms.append(sum(level.prolong(g, 3 * a + b) * r[a] for a in range(3)))

    level.apply(second, use_last)
    for m in range(6):
        t = [ordered[4 * m + i] for i in range(4)]
        right = jnp.where(row < 4, t[0], pltpu.roll(t[1], 4, 0))
        left = pltpu.roll(jnp.where(row < 4, t[2], pltpu.roll(t[3], 4, 0)), 64, 1)
        down[8 + 8 * m : 16 + 8 * m, :] = jnp.where(lane >= 64, right, left)
    source, to = iota((128, 128), 0), iota((128, 128), 1)
    pick = (source >= 64) & (to % 8 == (source % 32) // 4)
    out = dot(jnp.concatenate(terms, axis=0), pick.astype(F32))
    down[0:8, :] = jnp.zeros((8, 128), F32)
    for b in range(3):
        totals = [jnp.zeros((8, 128), F32)] * 2
        for g in range(8):
            n = 8 * (3 * g + b)
            y = level.y[g // 2]
            mine = jnp.where((row < 4) & own_lanes(y, level.spot[g % 2]), out[n : n + 8], 0.0)
            upper = (y // 2).astype(F32)
            totals[0] = totals[0] + mine * (1.0 - upper)
            totals[1] = totals[1] + mine * upper
        for half in range(2):
            down[2 * b + half : 2 * b + half + 1, :] = jnp.sum(totals[half], axis=0, keepdims=True)


SHIFTS = ((-4, -3, -2, -1, 1, 2, 3, 4), (-8, -7, -6, -5, 5, 6, 7, 8))


def bottom_window(ids, stiff, couple, stiff_out, coefs_out):
    tiles = ids[3] * 2
    for j in range(2 * WINDOW):
        t = jnp.clip(2 * (ids[2] - REACH) + j, 0, tiles - 1) - ids[4]
        span = pl.ds(pl.multiple_of(t * 128, 128), 128)
        v = stiff[:, span]
        for a in range(3):
            stiff_out[a, j : j + 1, :] = v[a : a + 1]
        for k in range(7):
            for a in range(3):
                v = couple[k, a, :, span].astype(F32)
                for b in range(3):
                    coefs_out[k * 9 + a * 3 + b, j : j + 1, :] = v[b : b + 1]
    pad = ROWS - 2 * WINDOW
    for a in range(3):
        stiff_out[a, 2 * WINDOW :, :] = jnp.ones((pad, 128), F32)
    for i in range(63):
        coefs_out[i, 2 * WINDOW :, :] = jnp.zeros((pad, 128), F32)


def bottom_and_up(
    ids, got, mine, bottom_stiff, bottom_coefs, load2, mid, packed, pre1, packed1,
    guess1, lower, upper, load, now, guess, first, rest, ordered,
):
    load[...] = jnp.zeros((3, ROWS, 128), F32)
    for b in range(3):
        load[b, 2 * REACH : 2 * REACH + 2, :] = mine[2 * b : 2 * b + 2, :]
        for s in range(2):
            for g in range(8):
                p = REACH - SHIFTS[s][g]
                load[b, 2 * p : 2 * p + 2, :] = got[g % 2, g // 2, 56 * s + 2 * b : 56 * s + 2 * b + 2, :]
    lane = iota((ROWS, 128), 1)
    row = iota((ROWS, 128), 0)
    plane = ids[2] - REACH + row // 2
    inside = (plane >= 0) & (plane < ids[3]) & (row < 2 * WINDOW)
    j, k = (row % 2) * 8 + lane // 16, lane % 16
    weights = [jnp.where(inside, damping / bottom_stiff[a], 0.0) for a in range(3)]
    for a in range(3):
        now[a] = weights[a] * load[a]

    def sweep(_, carry):
        v = [now[b] for b in range(3)]
        views = [v]
        views.append([pltpu.roll(e, 2, 0) for e in v])
        views.append([pltpu.roll(e, ROWS - 2, 0) for e in v])
        low_y, high_y = [], []
        for e in v:
            t = pltpu.roll(e, 16, 1)
            t = jnp.where(lane < 16, pltpu.roll(t, 1, 0), t)
            low_y.append(jnp.where(j == 0, 0.0, t))
            t = pltpu.roll(e, 112, 1)
            t = jnp.where(lane >= 112, pltpu.roll(t, ROWS - 1, 0), t)
            high_y.append(jnp.where(j == 15, 0.0, t))
        views += [low_y, high_y]
        views.append([jnp.where(k == 0, 0.0, pltpu.roll(e, 1, 1)) for e in v])
        views.append([jnp.where(k == 15, 0.0, pltpu.roll(e, 127, 1)) for e in v])
        out = combine([bottom_stiff[a] for a in range(3)], lambda i: bottom_coefs[i], views)
        for a in range(3):
            now[a] = v[a] + weights[a] * (load[a] - out[a])
        return carry

    lax.fori_loop(0, SWEEPS - 1, sweep, 0)

    level = Coarse(ids, packed)
    row, lane = rows8(), lanes8()

    def spread(b, q, y):
        r = 2 * (REACH + q)
        return jnp.broadcast_to(jnp.where(y < 2, now[b, r : r + 1, :], now[b, r + 1 : r + 2, :]), (8, 128))

    for n in range(24):
        m, u = n // 4, n % 4
        rows = slice(8 + 8 * m, 16 + 8 * m)
        under = got[SHIFTS[0].index(1) % 2, SHIFTS[0].index(1) // 2, rows, :]
        over = got[SHIFTS[0].index(-1) % 2, SHIFTS[0].index(-1) // 2, rows, :]
        if u % 2 == 1:
            under = pltpu.roll(under, 4, 0)
        else:
            over = pltpu.roll(over, 4, 0)
        sides = jnp.where(row < 4, under, over)
        ordered[n] = pltpu.roll(sides, 64, 1) if u < 2 else sides
    outer, inner = [], []
    for g in range(8):
        y = level.y[g // 2]
        here = own_lanes(y, level.spot[g % 2])
        for b in range(3):
            e = jnp.where(row < 4, spread(b, -1, y), spread(b, 1, y))
            outer.append(jnp.where(here, e, 0.0))
            inner.append(jnp.where(here, spread(b, 0, y), 0.0))
    source, to = iota((128, 128), 0), iota((128, 128), 1)
    pick = (source % 8 == (to % 32) // 4).astype(F32)
    ups = dot(jnp.concatenate(outer + inner, axis=0), pick)
    for g in range(8):
        up = []
        for b in range(3):
            n = 8 * (3 * g + b)
            up.append(jnp.where((row < 4) & (lane >= 64), ups[192 + n : 200 + n], ups[n : n + 8]))
        for a in range(3):
            n = 3 * g + a
            sides = ordered[3 * level.place[g] + a]
            total = jnp.where(lane < 64, sides, jnp.where(row < 4, mid[n], 0.0))
            for b in range(3):
                total = total + level.prolong(g, 3 * a + b) * up[b]
            guess[n] = total

    def use(g, out):
        for a in range(3):
            n = 3 * g + a
            r = load2[n] - out[a]
            rest[n] = r
            first[n] = r / level.stiff(g, a)

    level.apply(guess, use)
    final = []

    def use_last(g, out):
        for a in range(3):
            n = 3 * g + a
            f = first[n]
            e = guess[n] + f + (carry_coef * f + fresh_coef * ((rest[n] - out[a]) / level.stiff(g, a)))
            under = jnp.where((lane >= 64) & (lane < 96), e, 0.0)
            over = jnp.where(lane >= 96, pltpu.roll(e, 4, 0), 0.0)
            final.append(jnp.where(row < 4, under, over))

    level.apply(first, use_last)

    pick = (source >= 64) & (source % 32 == (to % 64) // 2)
    ups = dot(jnp.concatenate(final, axis=0), pick.astype(F32))
    middle = Middle(ids, packed1)
    for g in range(8):
        for a in range(3):
            total = pre1[3 * g + a]
            for b in range(3):
                n = 8 * (3 * g + b)
                total = total + middle.prolong(g, 3 * a + b) * ups[n : n + 8]
            guess1[3 * g + a] = total
    for m in range(12):
        s, t = guess1[2 * m], guess1[2 * m + 1]
        upper[m] = jnp.where(row < 4, pltpu.roll(s, 4, 0), t)
        lower[m] = jnp.where(row < 4, s, pltpu.roll(t, 4, 0))


def middle_up(
    ids, low, mid, high, load, load_edge, packed, pre, own, other, result, xs, ys, guess_edge, first, first_edge, rest, final
):
    fine = Fine(ids)
    level = Middle(ids, packed)
    row = rows8()
    for n in range(24):
        under, over = low[n // 2], high[n // 2]
        if n % 2 == 1:
            under = pltpu.roll(under, 4, 0)
        else:
            over = pltpu.roll(over, 4, 0)
        guess_edge[n] = jnp.where(row < 4, under, over)

    def use(g, out):
        for a in range(3):
            n = 3 * g + a
            r = load[n] - out[a]
            rest[n] = r
            first[n] = r / level.stiff(g, a)

    def use_edge(g, out):
        for a in range(3):
            n = 3 * g + a
            first_edge[n] = (load_edge[n] - out[a]) / level.stiff_edge(g, a)

    level.apply(mid, guess_edge, use, use_edge)

    def use_last(g, out):
        for a in range(3):
            n = 3 * g + a
            f = first[n]
            e = mid[n] + f + (carry_coef * f + fresh_coef * ((rest[n] - out[a]) / level.stiff(g, a)))
            final[g, 8 * a : 8 * a + 8, :] = e

    level.apply(first, first_edge, use_last)
    rows = (iota((48, 24), 0) // 2 == iota((48, 24), 1)).astype(F32)
    source, to = iota((128, 128), 0), iota((128, 128), 1)
    for h in range(2):
        tall = dot(rows, final[h])
        ups = [dot(tall, (source == 64 * p + to // 2).astype(F32)) for p in range(2)]
        coefs0 = (own, other)[h]
        for a in range(3):
            for x in range(8):
                total = pre[h, 8 * a + x]
                for b in range(3):
                    n = 16 * b + 8 * (x // 4)
                    total = total + coefs0[(63 + 3 * a + b) * 8 + x] * ups[(x // 2) % 2][n : n + 8]
                result[h, 8 * a + x] = total
    fine.send(at(result), xs, ys)


def side_by_side(left, right):
    return jnp.concatenate([left, right], axis=1)


def pack_edges(ids, mc, ms, mp, cc, cs, cp, up, down, coarse, body):
    def mid(i, x):
        if i < 63:
            return mc[i // 9, i // 3 % 3, i % 3, x].astype(F32)
        return jnp.zeros((4, 64), F32)

    for t in range(32):
        up[t] = side_by_side(mid(2 * t + 1, 3), mid(2 * t, 3))
        down[t] = side_by_side(mid(2 * t, 0), mid(2 * t + 1, 0))
    for a in range(3):
        up[32 + a] = side_by_side(ms[a, 2], ms[a, 3])
        down[32 + a] = side_by_side(ms[a, 0], ms[a, 1])

    def low(i):
        if i < 63:
            got = cc[i // 9, i // 3 % 3, i % 3]
        elif i < 66:
            got = cs[i - 63]
        elif i < 75:
            got = cp[(i - 66) // 3, (i - 66) % 3]
        else:
            return [jnp.zeros((4, 32), F32)] * 2
        return [got[0].astype(F32), got[1].astype(F32)]

    for t in range(38):
        both = jnp.concatenate(low(2 * t) + low(2 * t + 1), axis=1)
        coarse[t] = both
    for t in range(16):
        four = [low(i) if i < 63 else low(75) for i in range(4 * t, 4 * t + 4)]
        up[35 + t] = jnp.concatenate([v[1] for v in four], axis=1)
        down[35 + t] = jnp.concatenate([v[0] for v in four], axis=1)
    for t in range(6):
        both = jnp.concatenate(low(63 + 2 * t) + low(64 + 2 * t), axis=1)
        up[51 + t] = both
        down[51 + t] = both


    for i in range(75):
        if i < 63:
            v = [mc[i // 9, i // 3 % 3, i % 3, x].astype(F32) for x in range(4)]
        elif i < 66:
            v = [ms[i - 63, x] for x in range(4)]
        else:
            v = [mp[(i - 66) // 3, (i - 66) % 3, x] for x in range(4)]
        body[i, 0:4, :] = side_by_side(v[0], v[1])
        body[i, 4:8, :] = side_by_side(v[2], v[3])


def pack_levels(ids, body, low, high, coarse, one, two):
    for i in range(75):
        one[i] = body[i]
    for t in range(35):
        one[75 + t, 0:4, :] = low[t]
        one[75 + t, 4:8, :] = high[t]
    for t in range(19):
        two[t, 0:4, :] = coarse[2 * t]
        two[t, 4:8, :] = coarse[2 * t + 1]
    for t in range(22):
        two[19 + t, 0:4, :] = low[35 + t]
        two[19 + t, 4:8, :] = high[35 + t]


def unpack_coarse(ids, packed, fields):
    row, lane = rows8(), lanes8()
    own = (row < 4) & (lane >= 64)
    free = (row >= 4) & (lane >= 64)

    def turned(v, shift):
        return pltpu.roll(v, shift % 128, 1) if shift % 128 else v

    def block(g, carry):
        for f in range(75):
            i = f % 4
            mine = packed[g, f // 4]
            if i // 2:
                mine = pltpu.roll(mine, 4, 0)
            if i % 2 == 0:
                mine = turned(mine, 64)
            if f < 63:
                v = packed[g, 19 + f // 4]
                edges = jnp.where(row < 4, turned(v, 32 - 32 * i), turned(v, -32 * i))
            else:
                edges = turned(packed[g, 35 + (f - 63) // 2], 64 * ((f - 63) % 2))
            v = jnp.where(own, mine, edges)
            if 63 <= f < 66:
                v = jnp.where(free, 1.0, v)
            fields[g, f] = v
        return carry

    lax.fori_loop(0, 8, block, 0)


VMEM = pl.BlockSpec(memory_space=pltpu.VMEM)
SMEM = pl.BlockSpec(memory_space=pltpu.SMEM)


def run(kernel, ids, ins, outs, scratch=()):
    return pl.pallas_call(
        kernel,
        out_shape=[jax.ShapeDtypeStruct(s, F32) for s in outs],
        in_specs=[SMEM] + [VMEM] * len(ins),
        out_specs=[VMEM] * len(outs),
        scratch_shapes=[pltpu.VMEM(s, F32) for s in scratch],
        compiler_params=pltpu.CompilerParams(vmem_limit_bytes=8 * 1024 * 1024),
    )(ids, *ins)


def shifted(value, axis, count, shift):
    return lax.ppermute(value, axis, [(i, i + shift) for i in range(count) if 0 <= i + shift < count])


def split_shift(value, axis, count):
    pairs = [(2 * i, 2 * i + 2) for i in range(count - 1)] + [(2 * i + 3, 2 * i + 1) for i in range(count - 1)]
    return lax.ppermute(value, (axis, "ga"), pairs)


def skewed(value, count, shifts):
    pairs = [
        (8 * i + g, 8 * (i + s) + g) for g, s in enumerate(shifts) for i in range(count) if 0 <= i + s < count
    ]
    return lax.ppermute(value, ("gx", "gy", "ga"), pairs)


def group_gather(value):
    pair = lax.all_gather(value, "gy", axis_index_groups=[[0, 1], [2, 3]])
    four = lax.all_gather(pair, "gy", axis_index_groups=[[0, 2], [1, 3]])
    return lax.all_gather(four.reshape((4,) + value.shape), "ga")


def local(
    right_side,
    fine_stiff,
    fine_couple,
    fine_prolong,
    middle_stiff,
    middle_couple,
    middle_prolong,
    coarse_stiff,
    coarse_couple,
    coarse_prolong,
    bottom_stiff,
    bottom_couple,
):
    count = lax.axis_size("gx")
    gx, gy, ga = lax.axis_index("gx"), lax.axis_index("gy"), lax.axis_index("ga")
    span = min(WINDOW, count)
    start = 2 * jnp.clip(gx - REACH, 0, count - span)
    ids = jnp.stack([ga, gy, gx, jnp.int32(count), start]).astype(jnp.int32)

    def exchange(xs, ys):
        both = jnp.stack([split_shift(xs, "gx", count), split_shift(ys, "gy", 4)])
        return lax.all_gather(both, "ga")

    half = (2, 24, 8, 128)
    edge = (2, 24, 128)
    block = (24, 8, 128)

    cut = lax.dynamic_slice_in_dim(bottom_stiff, start * 128, span * 256, 1)
    cut_couple = lax.dynamic_slice_in_dim(bottom_couple, start * 128, span * 256, 3)
    right_side, middle_stiff, cut = lax.optimization_barrier((right_side, middle_stiff, cut))

    up, down, coarse, body = run(
        pack_edges,
        ids,
        [middle_couple, middle_stiff, middle_prolong, coarse_couple, coarse_stiff, coarse_prolong],
        [(57, 4, 128), (57, 4, 128), (38, 4, 128), (75, 8, 128)],
    )
    below, above = shifted(up, "gx", count, 1), shifted(down, "gx", count, -1)

    ls = lax.all_gather(jnp.stack([right_side.reshape(block), fine_stiff.reshape(block)]), "ga")
    first, xs, ys, own = run(
        fine_first, ids, [ls, fine_couple, fine_prolong], [half, edge, edge, (576, 8, 128)]
    )
    swap = [(0, 1), (1, 0)]
    other = lax.ppermute(own, "ga", swap)
    below, above, _ = lax.optimization_barrier((below, above, xs))
    one, two = run(pack_levels, ids, [body, below, above, coarse], [(110, 8, 128), (41, 8, 128)])
    packed1 = lax.all_gather(one, ("gy", "ga"))
    halo = exchange(xs, ys)
    two, _ = lax.optimization_barrier((two, halo))
    packed2 = lax.all_gather(two, ("gy", "ga"))
    rest, second, xs, ys = run(fine_second, ids, [ls, first, halo, own, other], [half, half, edge, edge])
    halo = exchange(xs, ys)
    pre0, keep, send = run(
        fine_down, ids, [ls, first, second, rest, halo, own, other], [half, (24, 128), (24, 128)]
    )
    got = group_gather(jnp.concatenate([keep, split_shift(send, "gx", count)]))

    tiles = (24, 8, 128)
    load1, edge1, pre1, load2 = run(
        middle_down, ids, [got, packed1], [tiles, tiles, tiles, (8, 8, 128)], [tiles] * 5
    )
    low, high = shifted(load2, "gx", count, 1), shifted(load2, "gx", count, -1)

    cut, cut_couple, packed2, _ = lax.optimization_barrier((cut, cut_couple, packed2, load2))
    bottom_s, bottom_c = run(bottom_window, ids, [cut, cut_couple], [(3, ROWS, 128), (63, ROWS, 128)])
    (fields2,) = run(unpack_coarse, ids, [packed2], [(8, 75, 8, 128)])

    load2, pre2, mine = run(
        coarse_down, ids, [low, load2, high, fields2], [tiles, tiles, (56, 128)], [tiles] * 4
    )
    got = group_gather(jnp.concatenate([skewed(mine, count, SHIFTS[0]), skewed(mine[:8], count, SHIFTS[1])]))

    guess1, lower, upper = run(
        bottom_and_up,
        ids,
        [got, mine, bottom_s, bottom_c, load2, pre2, fields2, pre1, packed1],
        [tiles, (12, 8, 128), (12, 8, 128)],
        [(3, ROWS, 128), (3, ROWS, 128), tiles, tiles, tiles, tiles],
    )
    low, high = shifted(upper, "gx", count, 1), shifted(lower, "gx", count, -1)

    guess, xs, ys = run(
        middle_up,
        ids,
        [low, guess1, high, load1, edge1, packed1, pre0, own, other],
        [half, edge, edge],
        [tiles] * 4 + [(8, 24, 128)],
    )

    halo = exchange(xs, ys)
    rest, first, xs, ys = run(fine_up_first, ids, [ls, guess, halo, own, other], [half, half, edge, edge])
    halo = exchange(xs, ys)
    result, remain, second, xs, ys = run(
        fine_up_second,
        ids,
        [ls, guess, first, rest, halo, own, other],
        [block, block, half, edge, edge],
    )
    halo = exchange(xs, ys)
    (residual,) = run(fine_last, ids, [ls, second, remain, halo, own], [block])
    whole = (3, 8, 8, 128)
    return result.reshape(whole), residual.reshape(whole)


def solution(mesh):
    placed = (
        P(None, "gx", "gy", "ga"),
        P(None, "gx", "gy", "ga"),
        P(None, None, None, "gx", "gy", "ga"),
        P(None, None, "gx", "gy", "ga"),
        P(None, "gx", "gy", "ga"),
        P(None, None, None, "gx", "gy", "ga"),
        P(None, None, "gx", "gy", "ga"),
        P(None, "gx", "gy", "ga"),
        P(None, None, None, "gx", "gy", "ga"),
        P(None, None, "gx", "gy", "ga"),
        P(),
        P(),
    )
    return jax.shard_map(
        local,
        mesh=mesh,
        in_specs=placed,
        out_specs=(P(None, "gx", "gy", "ga"), P(None, "gx", "gy", "ga")),
        check_vma=False,
    )
```

```python
import jax
import jax.numpy as jnp
from jax import lax
from jax.experimental import pallas as pl
from jax.experimental.pallas import tpu as pltpu
from jax.sharding import PartitionSpec as P

SWEEPS = 8
center_value = 1.0
half_width = 0.7
damping = 0.7
ratio_first = half_width / center_value
ratio_second = 1.0 / (2.0 * center_value / half_width - ratio_first)
carry_coef = ratio_second * ratio_first
fresh_coef = 2.0 * ratio_second / half_width

F32 = jnp.float32
REACH = 8
WINDOW = 2 * REACH + 1
ROWS = 40


def iota(shape, dim):
    return lax.broadcasted_iota(jnp.int32, shape, dim)


def dot(a, b):
    return jnp.dot(a, b, precision=lax.Precision.HIGHEST, preferred_element_type=F32)


def combine(stiff, coef, views):
    outs = []
    for a in range(3):
        total = stiff[a] * views[0][a]
        for k in range(7):
            for b in range(3):
                total = total + coef(k * 9 + a * 3 + b) * views[k][b]
        outs.append(total)
    return outs


class Fine:
    def __init__(self, ids):
        self.core = ids[0]
        self.spot = (ids[0], 1 - ids[0])
        right = ids[0].astype(F32)
        self.right = (right, 1.0 - right)
        self.row = iota((8, 128), 0)
        self.lane = iota((8, 128), 1)

    def apply(self, get, halo, stiff, coefs, use, halves=(0, 1)):
        for x in range(8):
            mids = [[get(h, b, x) for b in range(3)] for h in range(2)]
            for h in halves:
                views = [mids[h]]
                spot = self.spot[h]
                lows, highs = [], []
                for b in range(3):
                    lows.append(halo[0, 0, spot, 8 * b : 8 * b + 8, :] if x == 0 else get(h, b, x - 1))
                    highs.append(halo[1, 0, spot, 8 * b : 8 * b + 8, :] if x == 7 else get(h, b, x + 1))
                views += [lows, highs]
                lows, highs = [], []
                for b in range(3):
                    at = 8 * b + x
                    v = mids[h][b]
                    edge = jnp.broadcast_to(halo[0, 1, spot, at : at + 1, :], (8, 128))
                    lows.append(jnp.where(self.row == 0, edge, pltpu.roll(v, 1, 0)))
                    edge = jnp.broadcast_to(halo[1, 1, spot, at : at + 1, :], (8, 128))
                    highs.append(jnp.where(self.row == 7, edge, pltpu.roll(v, 7, 0)))
                views += [lows, highs]
                lows, highs = [], []
                for b in range(3):
                    v, o = mids[h][b], mids[1 - h][b]
                    lows.append(
                        jnp.where(self.lane == 0, pltpu.roll(o, 1, 1) * self.right[h], pltpu.roll(v, 1, 1))
                    )
                    highs.append(
                        jnp.where(
                            self.lane == 127,
                            pltpu.roll(o, 127, 1) * self.right[1 - h],
                            pltpu.roll(v, 127, 1),
                        )
                    )
                views += [lows, highs]
                coef = coefs[h]
                out = combine([stiff(h, a, x) for a in range(3)], lambda i: coef[i * 8 + x], views)
                use(h, x, out)

    def send(self, get, xs, ys):
        up = self.core == 0
        for h in range(2):
            spot = self.spot[h]
            for b in range(3):
                xs[spot, 8 * b : 8 * b + 8, :] = jnp.where(up, get(h, b, 7), get(h, b, 0))
                for x in range(8):
                    v = get(h, b, x)
                    ys[spot, 8 * b + x : 8 * b + x + 1, :] = jnp.where(up, v[7:8], v[0:1])


def at(ref):
    return lambda h, b, x: ref[h, 8 * b + x]


def given(fine, ref, which):
    return lambda h, b, x: ref[fine.spot[h], which, 8 * b + x]


def fine_first(ids, ls, couple, prolong, first, xs, ys, own):
    fine = Fine(ids)
    load, stiff = given(fine, ls, 0), given(fine, ls, 1)
    for h in range(2):
        for i in range(24):
            first[h, i] = load(h, i // 8, i % 8) / stiff(h, i // 8, i % 8)
    fine.send(at(first), xs, ys)
    for i in range(63):
        for x in range(8):
            own[8 * i + x] = couple[i // 9, i // 3 % 3, i % 3, x].astype(F32)
    for i in range(9):
        for x in range(8):
            own[504 + 8 * i + x] = prolong[i // 3, i % 3, x]


def fine_second(ids, ls, first, halo, own, other, rest, second, xs, ys, kept):
    fine = Fine(ids)
    load, stiff = given(fine, ls, 0), given(fine, ls, 1)

    def use(h, x, out):
        for a in range(3):
            r = load(h, a, x) - out[a]
            rest[h, 8 * a + x] = r
            second[h, 8 * a + x] = carry_coef * first[h, 8 * a + x] + fresh_coef * (r / stiff(h, a, x))

    fine.apply(at(first), halo, stiff, (own, other), use)
    fine.send(at(second), xs, ys)
    for i in range(576):
        kept[i] = other[i]


def fine_down(ids, ls, first, second, rest, halo, own, other, pre, keep, send):
    fine = Fine(ids)
    stiff = given(fine, ls, 1)
    terms = [[[[] for _ in range(4)] for _ in range(3)] for _ in range(2)]
    coefs = (own, other)

    def use(h, x, out):
        r = [rest[h, 8 * a + x] - out[a] for a in range(3)]
        for b in range(3):
            t = sum(coefs[h][(63 + 3 * a + b) * 8 + x] * r[a] for a in range(3))
            terms[h][b][x // 2].append(t)
            pre[h, 8 * b + x] = first[h, 8 * b + x] + second[h, 8 * b + x]

    fine.apply(at(second), halo, stiff, coefs, use)
    pairs = (iota((24, 48), 1) // 2 == iota((24, 48), 0)).astype(F32)
    source, to = iota((128, 128), 0), iota((128, 128), 1)
    tiles = []
    for h in range(2):
        total = None
        for p in range(2):
            stacked = jnp.concatenate([sum(terms[h][b][2 * i + p]) for b in range(3) for i in range(2)], axis=0)
            part = dot(stacked, (to == 64 * p + source // 2).astype(F32))
            total = part if total is None else total + part
        tiles.append(dot(pairs, total))
    keep[...] = tiles[0]
    up = fine.core == 0
    for b in range(3):
        mine = pltpu.roll(tiles[0][8 * b : 8 * b + 8], 4, 0)
        its = tiles[1][8 * b : 8 * b + 8]
        first_rows = fine.row < 4
        send[8 * b : 8 * b + 8, :] = jnp.where(
            up, jnp.where(first_rows, mine, its), jnp.where(first_rows, its, mine)
        )


def fine_up_first(ids, ls, guess, halo, own, other, rest, first, xs, ys):
    fine = Fine(ids)
    load, stiff = given(fine, ls, 0), given(fine, ls, 1)

    def use(h, x, out):
        for a in range(3):
            r = load(h, a, x) - out[a]
            rest[h, 8 * a + x] = r
            first[h, 8 * a + x] = r / stiff(h, a, x)

    fine.apply(at(guess), halo, stiff, (own, other), use)
    fine.send(at(first), xs, ys)


def fine_up_second(ids, ls, guess, first, rest, halo, own, other, result, remain, second, xs, ys):
    fine = Fine(ids)
    stiff = given(fine, ls, 1)

    def use(h, x, out):
        for a in range(3):
            r = rest[h, 8 * a + x] - out[a]
            f = first[h, 8 * a + x]
            s = carry_coef * f + fresh_coef * (r / stiff(h, a, x))
            second[h, 8 * a + x] = s
            if h == 0:
                remain[8 * a + x] = r
                result[8 * a + x] = guess[h, 8 * a + x] + f + s

    fine.apply(at(first), halo, stiff, (own, other), use)
    fine.send(at(second), xs, ys)


def fine_last(ids, ls, second, remain, halo, own, residual):
    fine = Fine(ids)
    stiff = given(fine, ls, 1)

    def use(h, x, out):
        for a in range(3):
            residual[8 * a + x] = remain[8 * a + x] - out[a]

    fine.apply(at(second), halo, stiff, (own, None), use, halves=(0,))


def rows8():
    return iota((8, 128), 0)


def lanes8():
    return iota((8, 128), 1)


class Group:
    def __init__(self, ids, packed):
        self.packed = packed
        self.y = [lax.rem(ids[1] + r, 4) for r in range(4)]
        self.below = [(y != 0).astype(F32) for y in self.y]
        self.above = [(y != 3).astype(F32) for y in self.y]
        self.spot = (ids[0], 1 - ids[0])
        right = ids[0].astype(F32)
        self.right = (right, 1.0 - right)
        self.place = [2 * self.y[g // 2] + self.spot[g % 2] for g in range(8)]

    def field(self, g, i):
        return self.packed[self.place[g], i]

    def sides(self, tiles, g, width):
        row, lane = rows8(), lanes8()
        r, h = g // 2, g % 2
        down, up = 2 * ((r + 3) % 4) + h, 2 * ((r + 1) % 4) + h
        views = [[], [], [], []]
        for b in range(3):
            v, o = tiles[g][b], tiles[g ^ 1][b]
            edge = pltpu.roll(tiles[down][b], 5, 0) * self.below[r]
            views[0].append(jnp.where(row % 4 == 0, edge, pltpu.roll(v, 1, 0)))
            edge = pltpu.roll(tiles[up][b], 3, 0) * self.above[r]
            views[1].append(jnp.where(row % 4 == 3, edge, pltpu.roll(v, 7, 0)))
            edge = pltpu.roll(o, 129 - width, 1) * self.right[h]
            views[2].append(jnp.where(lane % width == 0, edge, pltpu.roll(v, 1, 1)))
            edge = pltpu.roll(o, width - 1, 1) * self.right[1 - h]
            views[3].append(jnp.where(lane % width == width - 1, edge, pltpu.roll(v, 127, 1)))
        return views


def loaded(ref):
    return [[ref[3 * g + b] for b in range(3)] for g in range(8)]


def filled(stiff):
    return jnp.where(stiff == 0.0, 1.0, stiff)


class Middle(Group):
    def stiff(self, g, a):
        return self.field(g, 63 + a)

    def stiff_edge(self, g, a):
        return filled(self.field(g, 107 + a))

    def prolong(self, g, i):
        return self.field(g, 66 + i)

    def coef(self, g):
        return lambda i: self.field(g, i)

    def coef_edge(self, g):
        def get(i):
            tile = self.field(g, 75 + i // 2)
            return pltpu.roll(tile, 64, 1) if i % 2 else tile

        return get

    def apply(self, own_ref, edge_ref, use, use_edge=None):
        row, lane = rows8(), lanes8()
        own, edge = loaded(own_ref), loaded(edge_ref)
        for g in range(8):
            swap = [pltpu.roll(v, 64, 1) for v in own[g]]
            swap_edge = [pltpu.roll(v, 64, 1) for v in edge[g]]
            turned = [pltpu.roll(v, 4, 0) for v in swap]
            low, high, low_edge, high_edge = [], [], [], []
            for b in range(3):
                low.append(jnp.where(lane >= 64, swap[b], jnp.where(row < 4, swap_edge[b], turned[b])))
                high.append(jnp.where(lane < 64, swap[b], jnp.where(row < 4, turned[b], swap_edge[b])))
                low_edge.append(jnp.where(lane >= 64, swap_edge[b], swap[b]))
                high_edge.append(jnp.where(lane >= 64, swap[b], swap_edge[b]))
            views = [own[g], low, high] + self.sides(own, g, 64)
            use(g, combine([self.stiff(g, a) for a in range(3)], self.coef(g), views))
            if use_edge is not None:
                views = [edge[g], low_edge, high_edge] + self.sides(edge, g, 64)
                use_edge(g, combine([self.stiff_edge(g, a) for a in range(3)], self.coef_edge(g), views))


class Coarse(Group):
    def stiff(self, g, a):
        return filled(self.field(g, 63 + a))

    def prolong(self, g, i):
        return self.field(g, 66 + i)

    def apply(self, ref, use):
        lane = lanes8()
        tiles = loaded(ref)
        for g in range(8):
            low, high = [], []
            for v in tiles[g]:
                t = pltpu.roll(v, 32, 1)
                low.append(jnp.where(lane < 32, pltpu.roll(t, 4, 0), t))
                t = pltpu.roll(v, 96, 1)
                high.append(jnp.where(lane >= 96, pltpu.roll(t, 4, 0), t))
            views = [tiles[g], low, high] + self.sides(tiles, g, 32)
            use(g, combine([self.stiff(g, a) for a in range(3)], lambda i: self.field(g, i), views))


def middle_down(ids, got, packed, load, load_edge, pre, down, first, first_edge, rest, second, second_edge):
    level = Middle(ids, packed)
    row, lane = rows8(), lanes8()
    for g in range(8):
        y, z = level.y[g // 2], level.spot[g % 2]
        for b in range(3):
            n = 3 * g + b
            load[n] = got[z, y, 8 * b : 8 * b + 8, :]
            low = got[0, y, 24 + 8 * b : 32 + 8 * b, :]
            high = got[1, y, 24 + 8 * b : 32 + 8 * b, :]
            low = jnp.where(z == 1, pltpu.roll(low, 4, 0), low)
            high = jnp.where(z == 0, pltpu.roll(high, 4, 0), high)
            load_edge[n] = jnp.where(row < 4, low, high)
            first[n] = load[n] / level.stiff(g, b)
            first_edge[n] = load_edge[n] / level.stiff_edge(g, b)

    def use(g, out):
        for a in range(3):
            n = 3 * g + a
            r = load[n] - out[a]
            rest[n] = r
            second[n] = carry_coef * first[n] + fresh_coef * (r / level.stiff(g, a))

    def use_edge(g, out):
        for a in range(3):
            n = 3 * g + a
            r = load_edge[n] - out[a]
            second_edge[n] = carry_coef * first_edge[n] + fresh_coef * (r / level.stiff_edge(g, a))

    level.apply(first, first_edge, use, use_edge)
    terms = [[], [], []]

    def use_last(g, out):
        r = [rest[3 * g + a] - out[a] for a in range(3)]
        for b in range(3):
            n = 3 * g + b
            pre[n] = first[n] + second[n]
            terms[b].append(sum(level.prolong(g, 3 * a + b) * r[a] for a in range(3)))

    level.apply(second, second_edge, use_last)
    source, to = iota((128, 128), 0), iota((128, 128), 1)
    total = None
    for b in range(3):
        pick = to == 32 * b + (source % 64) // 2
        part = dot(jnp.concatenate(terms[b], axis=0), pick.astype(F32))
        total = part if total is None else total + part
    for g in range(8):
        down[g] = total[8 * g : 8 * g + 8]


def own_lanes(y, z):
    return lanes8() // 8 == (4 * (y % 2) + rows8() % 4) * 2 + z


def coarse_down(ids, low, mid, high, packed, load, pre, down, first, rest, second, ordered):
    level = Coarse(ids, packed)
    row, lane = rows8(), lanes8()
    place = lane // 32
    for g in range(8):
        under, here, over = low[g], mid[g], high[g]
        turned = [pltpu.roll(v, 4, 0) for v in (under, here, over)]

        def moved(v, b, to):
            shift = (32 * (to - b)) % 128
            return pltpu.roll(v, shift, 1) if shift else v

        for b in range(3):
            n = 3 * g + b
            top = jnp.where(place == 0, moved(under, b, 0), moved(turned[0], b, 1))
            own = jnp.where(place == 2, moved(here, b, 2), moved(turned[1], b, 3))
            bottom = jnp.where(place == 0, moved(turned[2], b, 0), moved(over, b, 1))
            tile = jnp.where(row < 4, jnp.where(place < 2, top, own), jnp.where(place < 2, bottom, 0.0))
            load[n] = tile
            first[n] = tile / level.stiff(g, b)

    def use(g, out):
        for a in range(3):
            n = 3 * g + a
            r = load[n] - out[a]
            rest[n] = r
            second[n] = carry_coef * first[n] + fresh_coef * (r / level.stiff(g, a))

    level.apply(first, use)
    terms = []

    def use_last(g, out):
        r = [rest[3 * g + a] - out[a] for a in range(3)]
        for b in range(3):
            n = 3 * g + b
            pre[n] = first[n] + second[n]
            ordered[3 * level.place[g] + b] = pre[n]
            terms.append(sum(level.prolong(g, 3 * a + b) * r[a] for a in range(3)))

    level.apply(second, use_last)
    for m in range(6):
        t = [ordered[4 * m + i] for i in range(4)]
        right = jnp.where(row < 4, t[0], pltpu.roll(t[1], 4, 0))
        left = pltpu.roll(jnp.where(row < 4, t[2], pltpu.roll(t[3], 4, 0)), 64, 1)
        down[8 + 8 * m : 16 + 8 * m, :] = jnp.where(lane >= 64, right, left)
    source, to = iota((128, 128), 0), iota((128, 128), 1)
    pick = (source >= 64) & (to % 8 == (source % 32) // 4)
    out = dot(jnp.concatenate(terms, axis=0), pick.astype(F32))
    down[0:8, :] = jnp.zeros((8, 128), F32)
    for b in range(3):
        totals = [jnp.zeros((8, 128), F32)] * 2
        for g in range(8):
            n = 8 * (3 * g + b)
            y = level.y[g // 2]
            mine = jnp.where((row < 4) & own_lanes(y, level.spot[g % 2]), out[n : n + 8], 0.0)
            upper = (y // 2).astype(F32)
            totals[0] = totals[0] + mine * (1.0 - upper)
            totals[1] = totals[1] + mine * upper
        for half in range(2):
            down[2 * b + half : 2 * b + half + 1, :] = jnp.sum(totals[half], axis=0, keepdims=True)


SHIFTS = ((-4, -3, -2, -1, 1, 2, 3, 4), (-8, -7, -6, -5, 5, 6, 7, 8))


def bottom_window(ids, stiff, couple, stiff_out, coefs_out):
    tiles = ids[3] * 2
    for j in range(2 * WINDOW):
        t = jnp.clip(2 * (ids[2] - REACH) + j, 0, tiles - 1) - ids[4]
        span = pl.ds(pl.multiple_of(t * 128, 128), 128)
        v = stiff[:, span]
        for a in range(3):
            stiff_out[a, j : j + 1, :] = v[a : a + 1]
        for k in range(7):
            for a in range(3):
                v = couple[k, a, :, span].astype(F32)
                for b in range(3):
                    coefs_out[k * 9 + a * 3 + b, j : j + 1, :] = v[b : b + 1]
    pad = ROWS - 2 * WINDOW
    for a in range(3):
        stiff_out[a, 2 * WINDOW :, :] = jnp.ones((pad, 128), F32)
    for i in range(63):
        coefs_out[i, 2 * WINDOW :, :] = jnp.zeros((pad, 128), F32)


def bottom_and_up(
    ids, got, mine, bottom_stiff, bottom_coefs, load2, mid, packed, pre1, packed1,
    guess1, lower, upper, load, now, guess, first, rest, ordered,
):
    load[...] = jnp.zeros((3, ROWS, 128), F32)
    for b in range(3):
        load[b, 2 * REACH : 2 * REACH + 2, :] = mine[2 * b : 2 * b + 2, :]
        for s in range(2):
            for g in range(8):
                p = REACH - SHIFTS[s][g]
                load[b, 2 * p : 2 * p + 2, :] = got[g % 2, g // 2, 56 * s + 2 * b : 56 * s + 2 * b + 2, :]
    lane = iota((ROWS, 128), 1)
    row = iota((ROWS, 128), 0)
    plane = ids[2] - REACH + row // 2
    inside = (plane >= 0) & (plane < ids[3]) & (row < 2 * WINDOW)
    j, k = (row % 2) * 8 + lane // 16, lane % 16
    weights = [jnp.where(inside, damping / bottom_stiff[a], 0.0) for a in range(3)]
    for a in range(3):
        now[a] = weights[a] * load[a]

    def sweep(_, carry):
        v = [now[b] for b in range(3)]
        views = [v]
        views.append([pltpu.roll(e, 2, 0) for e in v])
        views.append([pltpu.roll(e, ROWS - 2, 0) for e in v])
        low_y, high_y = [], []
        for e in v:
            t = pltpu.roll(e, 16, 1)
            t = jnp.where(lane < 16, pltpu.roll(t, 1, 0), t)
            low_y.append(jnp.where(j == 0, 0.0, t))
            t = pltpu.roll(e, 112, 1)
            t = jnp.where(lane >= 112, pltpu.roll(t, ROWS - 1, 0), t)
            high_y.append(jnp.where(j == 15, 0.0, t))
        views += [low_y, high_y]
        views.append([jnp.where(k == 0, 0.0, pltpu.roll(e, 1, 1)) for e in v])
        views.append([jnp.where(k == 15, 0.0, pltpu.roll(e, 127, 1)) for e in v])
        out = combine([bottom_stiff[a] for a in range(3)], lambda i: bottom_coefs[i], views)
        for a in range(3):
            now[a] = v[a] + weights[a] * (load[a] - out[a])
        return carry

    lax.fori_loop(0, SWEEPS - 1, sweep, 0)

    level = Coarse(ids, packed)
    row, lane = rows8(), lanes8()

    def spread(b, q, y):
        r = 2 * (REACH + q)
        return jnp.broadcast_to(jnp.where(y < 2, now[b, r : r + 1, :], now[b, r + 1 : r + 2, :]), (8, 128))

    for n in range(24):
        m, u = n // 4, n % 4
        rows = slice(8 + 8 * m, 16 + 8 * m)
        under = got[SHIFTS[0].index(1) % 2, SHIFTS[0].index(1) // 2, rows, :]
        over = got[SHIFTS[0].index(-1) % 2, SHIFTS[0].index(-1) // 2, rows, :]
        if u % 2 == 1:
            under = pltpu.roll(under, 4, 0)
        else:
            over = pltpu.roll(over, 4, 0)
        sides = jnp.where(row < 4, under, over)
        ordered[n] = pltpu.roll(sides, 64, 1) if u < 2 else sides
    outer, inner = [], []
    for g in range(8):
        y = level.y[g // 2]
        here = own_lanes(y, level.spot[g % 2])
        for b in range(3):
            e = jnp.where(row < 4, spread(b, -1, y), spread(b, 1, y))
            outer.append(jnp.where(here, e, 0.0))
            inner.append(jnp.where(here, spread(b, 0, y), 0.0))
    source, to = iota((128, 128), 0), iota((128, 128), 1)
    pick = (source % 8 == (to % 32) // 4).astype(F32)
    ups = dot(jnp.concatenate(outer + inner, axis=0), pick)
    for g in range(8):
        up = []
        for b in range(3):
            n = 8 * (3 * g + b)
            up.append(jnp.where((row < 4) & (lane >= 64), ups[192 + n : 200 + n], ups[n : n + 8]))
        for a in range(3):
            n = 3 * g + a
            sides = ordered[3 * level.place[g] + a]
            total = jnp.where(lane < 64, sides, jnp.where(row < 4, mid[n], 0.0))
            for b in range(3):
                total = total + level.prolong(g, 3 * a + b) * up[b]
            guess[n] = total

    def use(g, out):
        for a in range(3):
            n = 3 * g + a
            r = load2[n] - out[a]
            rest[n] = r
            first[n] = r / level.stiff(g, a)

    level.apply(guess, use)
    final = []

    def use_last(g, out):
        for a in range(3):
            n = 3 * g + a
            f = first[n]
            e = guess[n] + f + (carry_coef * f + fresh_coef * ((rest[n] - out[a]) / level.stiff(g, a)))
            under = jnp.where((lane >= 64) & (lane < 96), e, 0.0)
            over = jnp.where(lane >= 96, pltpu.roll(e, 4, 0), 0.0)
            final.append(jnp.where(row < 4, under, over))

    level.apply(first, use_last)

    pick = (source >= 64) & (source % 32 == (to % 64) // 2)
    ups = dot(jnp.concatenate(final, axis=0), pick.astype(F32))
    middle = Middle(ids, packed1)
    for g in range(8):
        for a in range(3):
            total = pre1[3 * g + a]
            for b in range(3):
                n = 8 * (3 * g + b)
                total = total + middle.prolong(g, 3 * a + b) * ups[n : n + 8]
            guess1[3 * g + a] = total
    for m in range(12):
        s, t = guess1[2 * m], guess1[2 * m + 1]
        upper[m] = jnp.where(row < 4, pltpu.roll(s, 4, 0), t)
        lower[m] = jnp.where(row < 4, s, pltpu.roll(t, 4, 0))


def middle_up(
    ids, low, mid, high, load, load_edge, packed, pre, own, other, result, xs, ys, guess_edge, first, first_edge, rest, final
):
    fine = Fine(ids)
    level = Middle(ids, packed)
    row = rows8()
    for n in range(24):
        under, over = low[n // 2], high[n // 2]
        if n % 2 == 1:
            under = pltpu.roll(under, 4, 0)
        else:
            over = pltpu.roll(over, 4, 0)
        guess_edge[n] = jnp.where(row < 4, under, over)

    def use(g, out):
        for a in range(3):
            n = 3 * g + a
            r = load[n] - out[a]
            rest[n] = r
            first[n] = r / level.stiff(g, a)

    def use_edge(g, out):
        for a in range(3):
            n = 3 * g + a
            first_edge[n] = (load_edge[n] - out[a]) / level.stiff_edge(g, a)

    level.apply(mid, guess_edge, use, use_edge)

    def use_last(g, out):
        for a in range(3):
            n = 3 * g + a
            f = first[n]
            e = mid[n] + f + (carry_coef * f + fresh_coef * ((rest[n] - out[a]) / level.stiff(g, a)))
            final[g, 8 * a : 8 * a + 8, :] = e

    level.apply(first, first_edge, use_last)
    rows = (iota((48, 24), 0) // 2 == iota((48, 24), 1)).astype(F32)
    source, to = iota((128, 128), 0), iota((128, 128), 1)
    for h in range(2):
        tall = dot(rows, final[h])
        ups = [dot(tall, (source == 64 * p + to // 2).astype(F32)) for p in range(2)]
        coefs0 = (own, other)[h]
        for a in range(3):
            for x in range(8):
                total = pre[h, 8 * a + x]
                for b in range(3):
                    n = 16 * b + 8 * (x // 4)
                    total = total + coefs0[(63 + 3 * a + b) * 8 + x] * ups[(x // 2) % 2][n : n + 8]
                result[h, 8 * a + x] = total
    fine.send(at(result), xs, ys)


def side_by_side(left, right):
    return jnp.concatenate([left, right], axis=1)


def pack_edges(ids, mc, ms, mp, cc, cs, cp, up, down, coarse, body):
    def mid(i, x):
        if i < 63:
            return mc[i // 9, i // 3 % 3, i % 3, x].astype(F32)
        return jnp.zeros((4, 64), F32)

    for t in range(32):
        up[t] = side_by_side(mid(2 * t + 1, 3), mid(2 * t, 3))
        down[t] = side_by_side(mid(2 * t, 0), mid(2 * t + 1, 0))
    for a in range(3):
        up[32 + a] = side_by_side(ms[a, 2], ms[a, 3])
        down[32 + a] = side_by_side(ms[a, 0], ms[a, 1])

    def low(i):
        if i < 63:
            got = cc[i // 9, i // 3 % 3, i % 3]
        elif i < 66:
            got = cs[i - 63]
        elif i < 75:
            got = cp[(i - 66) // 3, (i - 66) % 3]
        else:
            return [jnp.zeros((4, 32), F32)] * 2
        return [got[0].astype(F32), got[1].astype(F32)]

    for t in range(38):
        both = jnp.concatenate(low(2 * t) + low(2 * t + 1), axis=1)
        coarse[t] = both
    for t in range(16):
        four = [low(i) if i < 63 else low(75) for i in range(4 * t, 4 * t + 4)]
        up[35 + t] = jnp.concatenate([v[1] for v in four], axis=1)
        down[35 + t] = jnp.concatenate([v[0] for v in four], axis=1)
    for t in range(6):
        both = jnp.concatenate(low(63 + 2 * t) + low(64 + 2 * t), axis=1)
        up[51 + t] = both
        down[51 + t] = both


    for i in range(75):
        if i < 63:
            v = [mc[i // 9, i // 3 % 3, i % 3, x].astype(F32) for x in range(4)]
        elif i < 66:
            v = [ms[i - 63, x] for x in range(4)]
        else:
            v = [mp[(i - 66) // 3, (i - 66) % 3, x] for x in range(4)]
        body[i, 0:4, :] = side_by_side(v[0], v[1])
        body[i, 4:8, :] = side_by_side(v[2], v[3])


def pack_levels(ids, body, low, high, coarse, one, two):
    for i in range(75):
        one[i] = body[i]
    for t in range(35):
        one[75 + t, 0:4, :] = low[t]
        one[75 + t, 4:8, :] = high[t]
    for t in range(19):
        two[t, 0:4, :] = coarse[2 * t]
        two[t, 4:8, :] = coarse[2 * t + 1]
    for t in range(22):
        two[19 + t, 0:4, :] = low[35 + t]
        two[19 + t, 4:8, :] = high[35 + t]


def unpack_coarse(ids, packed, fields):
    row, lane = rows8(), lanes8()
    own = (row < 4) & (lane >= 64)
    free = (row >= 4) & (lane >= 64)

    def turned(v, shift):
        return pltpu.roll(v, shift % 128, 1) if shift % 128 else v

    def block(g, carry):
        for f in range(75):
            i = f % 4
            mine = packed[g, f // 4]
            if i // 2:
                mine = pltpu.roll(mine, 4, 0)
            if i % 2 == 0:
                mine = turned(mine, 64)
            if f < 63:
                v = packed[g, 19 + f // 4]
                edges = jnp.where(row < 4, turned(v, 32 - 32 * i), turned(v, -32 * i))
            else:
                edges = turned(packed[g, 35 + (f - 63) // 2], 64 * ((f - 63) % 2))
            v = jnp.where(own, mine, edges)
            if 63 <= f < 66:
                v = jnp.where(free, 1.0, v)
            fields[g, f] = v
        return carry

    lax.fori_loop(0, 8, block, 0)


VMEM = pl.BlockSpec(memory_space=pltpu.VMEM)
SMEM = pl.BlockSpec(memory_space=pltpu.SMEM)


def run(kernel, ids, ins, outs, scratch=()):
    return pl.pallas_call(
        kernel,
        out_shape=[jax.ShapeDtypeStruct(s, F32) for s in outs],
        in_specs=[SMEM] + [VMEM] * len(ins),
        out_specs=[VMEM] * len(outs),
        scratch_shapes=[pltpu.VMEM(s, F32) for s in scratch],
        compiler_params=pltpu.CompilerParams(vmem_limit_bytes=8 * 1024 * 1024),
    )(ids, *ins)


def shifted(value, axis, count, shift):
    return lax.ppermute(value, axis, [(i, i + shift) for i in range(count) if 0 <= i + shift < count])


def split_shift(value, axis, count):
    pairs = [(2 * i, 2 * i + 2) for i in range(count - 1)] + [(2 * i + 3, 2 * i + 1) for i in range(count - 1)]
    return lax.ppermute(value, (axis, "ga"), pairs)


def skewed(value, count, shifts):
    pairs = [
        (8 * i + g, 8 * (i + s) + g) for g, s in enumerate(shifts) for i in range(count) if 0 <= i + s < count
    ]
    return lax.ppermute(value, ("gx", "gy", "ga"), pairs)


def group_gather(value):
    pair = lax.all_gather(value, "gy", axis_index_groups=[[0, 1], [2, 3]])
    four = lax.all_gather(pair, "gy", axis_index_groups=[[0, 2], [1, 3]])
    return lax.all_gather(four.reshape((4,) + value.shape), "ga")


def local(
    right_side,
    fine_stiff,
    fine_couple,
    fine_prolong,
    middle_stiff,
    middle_couple,
    middle_prolong,
    coarse_stiff,
    coarse_couple,
    coarse_prolong,
    bottom_stiff,
    bottom_couple,
):
    count = lax.axis_size("gx")
    gx, gy, ga = lax.axis_index("gx"), lax.axis_index("gy"), lax.axis_index("ga")
    span = min(WINDOW, count)
    start = 2 * jnp.clip(gx - REACH, 0, count - span)
    ids = jnp.stack([ga, gy, gx, jnp.int32(count), start]).astype(jnp.int32)

    def exchange(xs, ys):
        both = jnp.stack([split_shift(xs, "gx", count), split_shift(ys, "gy", 4)])
        return lax.all_gather(both, "ga")

    half = (2, 24, 8, 128)
    edge = (2, 24, 128)
    block = (24, 8, 128)

    cut = lax.dynamic_slice_in_dim(bottom_stiff, start * 128, span * 256, 1)
    cut_couple = lax.dynamic_slice_in_dim(bottom_couple, start * 128, span * 256, 3)
    right_side, middle_stiff, cut = lax.optimization_barrier((right_side, middle_stiff, cut))

    up, down, coarse, body = run(
        pack_edges,
        ids,
        [middle_couple, middle_stiff, middle_prolong, coarse_couple, coarse_stiff, coarse_prolong],
        [(57, 4, 128), (57, 4, 128), (38, 4, 128), (75, 8, 128)],
    )
    below, above = shifted(up, "gx", count, 1), shifted(down, "gx", count, -1)

    ls = lax.all_gather(jnp.stack([right_side.reshape(block), fine_stiff.reshape(block)]), "ga")
    first, xs, ys, own = run(
        fine_first, ids, [ls, fine_couple, fine_prolong], [half, edge, edge, (576, 8, 128)]
    )
    swap = [(0, 1), (1, 0)]
    other = lax.ppermute(own, "ga", swap)
    below, above, _ = lax.optimization_barrier((below, above, xs))
    one, two = run(pack_levels, ids, [body, below, above, coarse], [(110, 8, 128), (41, 8, 128)])
    packed1 = lax.all_gather(one, ("gy", "ga"))
    packed2 = lax.all_gather(two, ("gy", "ga"))
    halo = exchange(xs, ys)
    rest, second, xs, ys, other = run(
        fine_second, ids, [ls, first, halo, own, other], [half, half, edge, edge, (576, 8, 128)]
    )
    halo = exchange(xs, ys)
    pre0, keep, send = run(
        fine_down, ids, [ls, first, second, rest, halo, own, other], [half, (24, 128), (24, 128)]
    )
    got = group_gather(jnp.concatenate([keep, split_shift(send, "gx", count)]))

    tiles = (24, 8, 128)
    load1, edge1, pre1, load2 = run(
        middle_down, ids, [got, packed1], [tiles, tiles, tiles, (8, 8, 128)], [tiles] * 5
    )
    low, high = shifted(load2, "gx", count, 1), shifted(load2, "gx", count, -1)

    cut, cut_couple, packed2, _ = lax.optimization_barrier((cut, cut_couple, packed2, load2))
    bottom_s, bottom_c = run(bottom_window, ids, [cut, cut_couple], [(3, ROWS, 128), (63, ROWS, 128)])
    (fields2,) = run(unpack_coarse, ids, [packed2], [(8, 75, 8, 128)])

    load2, pre2, mine = run(
        coarse_down, ids, [low, load2, high, fields2], [tiles, tiles, (56, 128)], [tiles] * 4
    )
    got = group_gather(jnp.concatenate([skewed(mine, count, SHIFTS[0]), skewed(mine[:8], count, SHIFTS[1])]))

    guess1, lower, upper = run(
        bottom_and_up,
        ids,
        [got, mine, bottom_s, bottom_c, load2, pre2, fields2, pre1, packed1],
        [tiles, (12, 8, 128), (12, 8, 128)],
        [(3, ROWS, 128), (3, ROWS, 128), tiles, tiles, tiles, tiles],
    )
    low, high = shifted(upper, "gx", count, 1), shifted(lower, "gx", count, -1)

    guess, xs, ys = run(
        middle_up,
        ids,
        [low, guess1, high, load1, edge1, packed1, pre0, own, other],
        [half, edge, edge],
        [tiles] * 4 + [(8, 24, 128)],
    )

    halo = exchange(xs, ys)
    rest, first, xs, ys = run(fine_up_first, ids, [ls, guess, halo, own, other], [half, half, edge, edge])
    halo = exchange(xs, ys)
    result, remain, second, xs, ys = run(
        fine_up_second,
        ids,
        [ls, guess, first, rest, halo, own, other],
        [block, block, half, edge, edge],
    )
    halo = exchange(xs, ys)
    (residual,) = run(fine_last, ids, [ls, second, remain, halo, own], [block])
    whole = (3, 8, 8, 128)
    return result.reshape(whole), residual.reshape(whole)


def solution(mesh):
    placed = (
        P(None, "gx", "gy", "ga"),
        P(None, "gx", "gy", "ga"),
        P(None, None, None, "gx", "gy", "ga"),
        P(None, None, "gx", "gy", "ga"),
        P(None, "gx", "gy", "ga"),
        P(None, None, None, "gx", "gy", "ga"),
        P(None, None, "gx", "gy", "ga"),
        P(None, "gx", "gy", "ga"),
        P(None, None, None, "gx", "gy", "ga"),
        P(None, None, "gx", "gy", "ga"),
        P(),
        P(),
    )
    return jax.shard_map(
        local,
        mesh=mesh,
        in_specs=placed,
        out_specs=(P(None, "gx", "gy", "ga"), P(None, "gx", "gy", "ga")),
        check_vma=False,
    )
```
